32 devices in a mesh: grid: 4 (over z), lev: 4 (over y, x), side: 2 (over core).
Axes of the slice: x: 2, y: 2, z: 4, core: 2. Of those that a mesh axis runs over, the one named last changes fastest.
Arguments:
- model_state: float32 [2, 8, 6, 32768], P('side', 'lev', None, 'grid'), may hold values from -6 to 6
- terrain_level: int32 [2, 8, 32768], P('side', None, 'grid'), may hold values from 0 to 7
- panel_owner: int32 [4096, 1], P('grid'), may hold values from 0 to 3, as said below
- panel_cell: int32 [4096], P('grid'), may hold values from 0 to 8191
- block_weight: float32 [256, 16, 128], P('grid'), may hold values from 0 to 0.015625
- block_owner: int32 [256, 1], P('grid'), may hold values from 0 to 3, as said below
- block_row: int32 [256], P('grid'), may hold values from 0 to 511
Outputs:
- new_state: float32 [2, 8, 6, 32768], P('side', 'lev', None, 'grid')
The draws below stay inside these ranges and needn't reach their ends.
Inputs may be any that keep to these rules, and one draw needn't show every extreme that they name: `panel_owner`: the panel slots of nest tile t name only the global tiles (t - 1), (t + 1) and (t + 2), taken modulo 4; within the 1024 slots of one nest tile no global tile is named more than 512 times, and some global tile is named exactly that often. `block_owner`: the blocks of nest tile t name only the global tiles (t - 1), (t + 1) and (t + 2), taken modulo 4; within the 64 blocks of one nest tile no global tile is named more than 32 times, and some global tile is named exactly that often.
All inputs are finite; a program needn't handle non-finite values.
Results may differ from the reference program's by a relative error of at most 0.00005.
Values sent between devices are 32-bit elements; how exact they have to be, the bound alone decides.
No kernel may reach another device: no remote copies, remote signals or barrier semaphores. Data moves between devices by JAX's collectives and lax.ppermute only.
A program may use at most 192 MiB of HBM per device.

```python
import jax
import jax.numpy as jnp
from jax import lax

FIELDS = 6
CELL_DEV = 8192
BLOCK_FINE = 128
BLOCK_COARSE = 16
LEVELS = 8
CELLS = 32768
BLOCKS = 256
BLOCK_CAP = 32
SLOT_CAP = 512
PANEL_DEV = 1024
PANELS = 4096
ROW_BLOCKS = 512
N_GRID = 4


def owner_lists(key, capacity):
    count = 2 * capacity
    offsets = jnp.array([N_GRID - 1, 1, N_GRID // 2], jnp.int32)
    key_first, key_second, key_order = jax.random.split(key, 3)
    first_pick = jax.random.randint(key_first, (N_GRID,), 0, 3, dtype=jnp.int32)
    second_count = jax.random.randint(key_second, (N_GRID,), 0, capacity + 1, dtype=jnp.int32)
    position = jnp.arange(count, dtype=jnp.int32)[None, :]
    ranked = jnp.where(position < capacity, 0, jnp.where(position < capacity + second_count[:, None], 1, 2))
    picked = jnp.mod(first_pick[:, None] + ranked, 3).astype(jnp.int32)
    tile_keys = jax.random.split(key_order, N_GRID)
    orders = jax.vmap(lambda single: jax.random.permutation(single, count))(tile_keys)
    shuffled = jnp.take_along_axis(picked, orders.astype(jnp.int32), axis=1)
    tiles = jnp.arange(N_GRID, dtype=jnp.int32)[:, None]
    owners = jnp.mod(tiles + jnp.take(offsets, shuffled), N_GRID)
    return owners.reshape(-1, 1).astype(jnp.int32)


def draw_panel_owner(key, part):
    return owner_lists(jax.random.fold_in(key, 11), SLOT_CAP)


def draw_block_owner(key, part):
    return owner_lists(jax.random.fold_in(key, 23), BLOCK_CAP)


def with_ends(entries, stream_key, low, top_value):
    place = [jax.random.randint(jax.random.fold_in(stream_key, axis), (), 0, length) for axis, length in enumerate(entries.shape)]
    widest = entries.shape.index(max(entries.shape))
    beside = place[:widest] + [(place[widest] + 1) % entries.shape[widest]] + place[widest + 1:]
    return entries.at[tuple(place)].set(low).at[tuple(beside)].set(top_value)


def level_of(stream_key, shape, cuts, least, high):
    def one(dim, parts):
        steps = jax.random.uniform(jax.random.fold_in(jax.random.fold_in(stream_key, 6), dim), (parts,), jnp.float32, least / len(cuts), high / len(cuts))
        return jnp.repeat(jnp.exp(steps), shape[dim] // parts).reshape((-1,) + (1,) * (len(shape) - dim - 1))

    loudness = one(*cuts[0])
    for cut in cuts[1:]:
        loudness = loudness * one(*cut)
    return loudness


def gaussian(own_key, extent, width, reach, cuts=(), kind=jnp.bfloat16):
    values = width * jax.random.normal(own_key, extent, jnp.float32)
    if cuts:
        values = values * level_of(own_key, extent, cuts, -0.22, 0.18)
    return jnp.clip(values, -reach, reach).astype(kind)


def setup_inputs(seed: int = 0) -> dict:
    splits = jax.random.split(jax.random.key(seed), 8)
    model_state = gaussian(splits[0], (2, LEVELS, FIELDS, CELLS), 1.0, 6.0, ((0, 2), (1, 4), (3, 4)), jnp.float32)
    terrain_level = with_ends(jax.random.randint(splits[1], (2, LEVELS, CELLS), 0, LEVELS), jax.random.fold_in(splits[1], 1), 0, LEVELS - 1).astype(jnp.int32)
    panel_owner = draw_panel_owner(jax.random.fold_in(splits[7], 71), 0)
    panel_cell = with_ends(jax.random.randint(splits[3], (PANELS,), 0, CELL_DEV), jax.random.fold_in(splits[3], 1), 0, CELL_DEV - 1).astype(jnp.int32)
    block_weight = jnp.clip(0.015625 * jax.random.uniform(splits[4], (BLOCKS, BLOCK_COARSE, BLOCK_FINE), jnp.float32) ** level_of(splits[4], (BLOCKS, BLOCK_COARSE, BLOCK_FINE), ((0, 4),), -0.2, 0.2), 0.0, 0.015625)
    block_owner = draw_block_owner(jax.random.fold_in(splits[7], 71), 0)
    block_row = with_ends(jax.random.randint(splits[6], (BLOCKS,), 0, ROW_BLOCKS), jax.random.fold_in(splits[6], 1), 0, ROW_BLOCKS - 1).astype(jnp.int32)
    return dict(model_state=model_state, terrain_level=terrain_level, panel_owner=panel_owner, panel_cell=panel_cell, block_weight=block_weight, block_owner=block_owner, block_row=block_row)


def remap_levels(fields, terrain):
    indices = jnp.broadcast_to(terrain[:, None, :].astype(jnp.int32), fields.shape)
    return jnp.take_along_axis(fields, indices, axis=0)


def reference(model_state, terrain_level, panel_owner, panel_cell, block_weight, block_owner, block_row):
    coarse = model_state[0]
    nested = model_state[1]
    coarse_moved = remap_levels(coarse, terrain_level[0])
    nested_moved = remap_levels(nested, terrain_level[1])
    panel_index = (panel_owner[:, 0] * CELL_DEV + panel_cell).astype(jnp.int32)
    panel_values = coarse_moved[:, :, panel_index]
    blocks = nested_moved.reshape(LEVELS, FIELDS, BLOCKS, BLOCK_FINE)
    partial_sums = jnp.einsum("brj,kfbj->kfbr", block_weight, blocks, precision=lax.Precision.HIGHEST)
    block_mass = jnp.sum(block_weight, axis=2)
    target = (block_owner[:, 0] * CELL_DEV + block_row * BLOCK_COARSE)[:, None] + jnp.arange(BLOCK_COARSE, dtype=jnp.int32)[None, :]
    target = target.reshape(-1).astype(jnp.int32)
    feedback = jnp.zeros_like(coarse).at[:, :, target].add(partial_sums.reshape(LEVELS, FIELDS, BLOCKS * BLOCK_COARSE))
    weight_sum = jnp.zeros((CELLS,), jnp.float32).at[target].add(block_mass.reshape(-1))
    new_coarse = (coarse + feedback) / (1.0 + weight_sum)
    nest_tiles = nested.reshape(LEVELS, FIELDS, N_GRID, CELL_DEV)
    rim_values = panel_values.reshape(LEVELS, FIELDS, N_GRID, PANEL_DEV)
    blended = 0.5 * (nest_tiles[..., :PANEL_DEV] + rim_values)
    new_nested = jnp.concatenate([blended, nest_tiles[..., PANEL_DEV:]], axis=3).reshape(LEVELS, FIELDS, CELLS)
    return jnp.stack([new_coarse, new_nested])
```

```python
import functools

import jax
import jax.numpy as jnp
from jax import lax
from jax.experimental import pallas as pl
from jax.experimental.pallas import tpu as pltpu
from jax.sharding import PartitionSpec as P

LANES = 128
SUBLANES = 8
VALUE_BITS = 16
ID_BITS = 8
MESSAGE_ROWS = 8
FLIPPED = (1, 0, 2)
VMEM = pltpu.VMEM
SMEM = pltpu.SMEM


def grid_steps(groups):
    return (groups - 1, 1, groups // 2)


def iota(shape, dimension):
    return lax.broadcasted_iota(jnp.int32, shape, dimension)


def rank_of(hit):
    rows, lanes = hit.shape
    lane, row = iota(hit.shape, 1), iota(hit.shape, 0)
    ones = hit.astype(jnp.int32)
    running = ones
    step = 1
    while step < lanes:
        running = running + jnp.where(lane >= step, pltpu.roll(running, step, 1), 0)
        step *= 2
    total = jnp.broadcast_to(jnp.sum(ones, axis=1, keepdims=True), hit.shape)
    above = jnp.where(row >= 1, pltpu.roll(total, 1, 0), 0)
    step = 1
    while step < rows:
        above = above + jnp.where(row >= step, pltpu.roll(above, step, 0), 0)
        step *= 2
    return running - ones + above


def squeeze(hit, rank, value, value_bits):
    rows, lanes = hit.shape
    lane, row = iota(hit.shape, 1), iota(hit.shape, 0)
    held = jnp.where(hit, ((row * lanes + lane - rank) << value_bits) | value, -1)
    bit = 0
    while 1 << bit < rows * lanes:
        step = 1 << bit
        if step < lanes:
            turned = pltpu.roll(held, lanes - step, 1)
            coming = jnp.where(lane < lanes - step, turned, pltpu.roll(turned, rows - 1, 0))
        else:
            coming = pltpu.roll(held, rows - step // lanes, 0)
        comes = (coming >= 0) & ((coming >> (value_bits + bit)) & 1 == 1)
        stays = (held >= 0) & ((held >> (value_bits + bit)) & 1 == 0)
        held = jnp.where(comes, coming, jnp.where(stays, held, -1))
        bit += 1
    return jnp.where(held >= 0, held & ((1 << value_bits) - 1), -1)


def list_kernel(groups, panel_owner, panel_cell, block_owner, block_row, *refs):
    requests, own_ref, slot_ref, owner_pad, row_pad = refs[:3], refs[3], refs[4], refs[5], refs[6]
    tile = lax.axis_index("grid")
    blocks = block_owner.shape[1]
    owner_pad[...] = jnp.full(owner_pad.shape, -1, jnp.int32)
    row_pad[...] = jnp.zeros(row_pad.shape, jnp.int32)
    owner_pad[0:1, 0:blocks] = block_owner[...]
    row_pad[0:1, 0:blocks] = block_row[...]
    owners, cells = panel_owner[...], panel_cell[...]
    landing = owner_pad[...]
    lane = iota(landing.shape, 1)
    marked = row_pad[...] | (lane << VALUE_BITS)
    half = owners.shape[0] // 2
    slots = jnp.zeros_like(owners)
    own_ref[...] = jnp.full(own_ref.shape, -1, jnp.int32)
    for number, step in enumerate(grid_steps(groups)):
        partner = lax.rem(tile + step, groups)
        hit = owners == partner
        rank = rank_of(hit)
        slots = jnp.where(hit, number * half * LANES + rank, slots)
        wanted = squeeze(hit, rank, cells, VALUE_BITS)
        lands = landing == partner
        block = squeeze(lands, rank_of(lands), marked, VALUE_BITS + ID_BITS)
        requests[number][...] = jnp.full(requests[number].shape, -1, jnp.int32)
        requests[number][0:half, :] = jnp.maximum(wanted[0:half], 0)
        requests[number][half : half + 1, :] = jnp.where(
            block >= 0, block & ((1 << VALUE_BITS) - 1), -1
        )[0:1]
        own_ref[number : number + 1, :] = jnp.where(block >= 0, block >> VALUE_BITS, -1)[0:1]
    slot_ref[...] = slots


def gather_lanes(values, index):
    return jnp.take_along_axis(values, index, axis=1)


def fold(values, least):
    step = values.shape[0] // 2
    while step >= least:
        values = values + pltpu.roll(values, step, 0)
        step //= 2
    return values


def panel_rows(lev_dev, fields, tiles, lists, group, state, terrain, packed, scratch):
    levels = SUBLANES
    bits = (levels - 1).bit_length()
    total = jnp.zeros((tiles, LANES), jnp.int32)
    for level in range(levels):
        total = total | (terrain[pl.ds(level, tiles, stride=levels), :] << (bits * level))
    packed[...] = total
    shape = (SUBLANES, LANES)
    sub = iota(shape, 0)
    per = SUBLANES // lev_dev
    quarters = lists[0].shape[0] // 2
    for number in range(3):
        for quarter in range(quarters):
            cells = jnp.broadcast_to(lists[number][quarter : quarter + 1, :], shape)
            high, low = cells // LANES, cells % LANES
            sums = [jnp.zeros(shape, jnp.float32) for _ in range(fields)]
            for chunk in range(tiles // per):
                here = high == chunk * per + sub // lev_dev
                for field in range(fields):
                    start = field * tiles * lev_dev + chunk * SUBLANES
                    got = gather_lanes(state[start : start + SUBLANES, :], low)
                    sums[field] = jnp.where(here, got, sums[field])
            code = jnp.zeros(shape, jnp.int32)
            for chunk in range(tiles // SUBLANES):
                got = gather_lanes(packed[chunk * SUBLANES : (chunk + 1) * SUBLANES, :], low)
                code = jnp.where(high == chunk * SUBLANES + sub, got, code)
            code = fold(code, 1)
            source = (code >> (bits * sub)) & (levels - 1)
            section = FLIPPED[number]
            for field in range(fields):
                both = fold(sums[field], lev_dev)
                placed = jnp.zeros(shape, jnp.float32)
                for level in range(lev_dev):
                    one = both
                    for turn in range(1, lev_dev):
                        one = jnp.where((sub - level) % lev_dev == turn, pltpu.roll(both, turn, 0), one)
                    placed = jnp.where(source == group * lev_dev + level, one, placed)
                row = ((section * fields + field) * quarters + quarter) * levels
                scratch[row : row + levels, :] = placed


def block_rows(lev_dev, fields, tiles, own, group, state, terrain, weight, scratch, mass):
    levels = SUBLANES
    coarse = weight.shape[1]
    per = LANES // coarse
    quarters = tiles // 2 // per

    def one_tile(index, carry):
        number, quarter = index // quarters, index % quarters
        lefts, rights = [], []
        for place in range(per):
            name = own[number, quarter * per + place]
            block = jnp.maximum(name, 0)
            source = terrain[pl.ds(pl.multiple_of(block * levels, levels), levels), :]
            parts = []
            for field in range(fields):
                placed = jnp.zeros((levels, LANES), jnp.float32)
                for level in range(lev_dev):
                    line = state[pl.ds((field * tiles + block) * lev_dev + level, 1), :]
                    placed = jnp.where(source == group * lev_dev + level, line, placed)
                parts.append(placed)
            moved = jnp.concatenate(parts, axis=0)
            moved_high = moved.astype(jnp.bfloat16)
            moved_low = (moved - moved_high.astype(jnp.float32)).astype(jnp.bfloat16)
            lefts.append(
                jnp.concatenate(
                    [moved_high, moved_low, jnp.ones((2 * SUBLANES, LANES), jnp.bfloat16)], axis=0
                )
            )
            dense = jnp.where(name >= 0, weight[block], 0.0)
            dense_high = dense.astype(jnp.bfloat16)
            dense_low = (dense - dense_high.astype(jnp.float32)).astype(jnp.bfloat16)
            blank = jnp.zeros((coarse, LANES), jnp.bfloat16)
            rights.append(
                jnp.concatenate(
                    [dense_high if other == place else blank for other in range(per)]
                    + [dense_low if other == place else blank for other in range(per)],
                    axis=0,
                )
            )
        product = lax.dot_general(
            jnp.concatenate(lefts, axis=1),
            jnp.concatenate(rights, axis=1),
            (((1,), (1,)), ((), ())),
            preferred_element_type=jnp.float32,
        )
        product = product[:, :LANES] + product[:, LANES:]
        rows = fields * levels
        result = product[:rows] + product[rows : 2 * rows]
        for field in range(fields):
            row = ((number * fields + field) * quarters + quarter) * levels
            scratch[pl.ds(pl.multiple_of(row, levels), levels), :] = result[
                field * levels : (field + 1) * levels
            ]
        mass[pl.ds(index, 1), :] = product[2 * rows : 2 * rows + 1]
        return carry

    lax.fori_loop(0, 3 * quarters, one_tile, 0)


def produce_kernel(lev_dev, fields, partners, own, *refs):
    lists, state, terrain, weight = refs[:3], refs[3], refs[4], refs[5]
    parts = refs[6 : 6 + partners]
    mass, scratch, packed = refs[6 + partners :]
    tiles = terrain.shape[0] // SUBLANES
    side, group = lax.axis_index("side"), lax.axis_index("lev")

    @pl.when(side == 0)
    def _():
        mass[...] = jnp.zeros_like(mass)
        panel_rows(lev_dev, fields, tiles, lists, group, state, terrain, packed, scratch)

    @pl.when(side == 1)
    def _():
        block_rows(lev_dev, fields, tiles, own, group, state, terrain, weight, scratch, mass)

    rows = scratch.shape[0] // SUBLANES
    for distance in range(partners):
        target = group ^ distance
        for level in range(lev_dev):
            parts[distance][level * rows : (level + 1) * rows, :] = scratch[
                pl.ds(target * lev_dev + level, rows, stride=SUBLANES), :
            ]


def sum_kernel(lev_dev, fields, partners, *refs):
    parts, mass, sections = refs[:partners], refs[partners], refs[partners + 1 :]
    total = parts[0][...]
    for part in parts[1:]:
        total = total + part[...]
    rows = total.shape[0] // lev_dev
    span = rows // 3
    quarters = span // fields
    for number, section in enumerate(sections):
        for level in range(lev_dev):
            start = level * rows + number * span
            section[level * span : (level + 1) * span, :] = total[start : start + span]
        section[lev_dev * span : lev_dev * span + quarters, :] = mass[
            number * quarters : (number + 1) * quarters, :
        ]
        tail = lev_dev * span + quarters
        section[tail:, :] = jnp.zeros((section.shape[0] - tail, LANES), jnp.float32)


def finish_panel(lev_dev, fields, tiles, sections, slots, state, out):
    shape = (SUBLANES, LANES)
    sub = iota(shape, 0)
    out[...] = state[...]
    panel_tiles = slots.shape[0]
    quarters = panel_tiles // 2
    span = fields * quarters
    share = SUBLANES // quarters
    for tile in range(panel_tiles):
        place = jnp.broadcast_to(slots[tile : tile + 1, :], shape)
        high, low = place // LANES, place % LANES
        here = [high == number * quarters + sub % quarters for number in range(3)]
        for level in range(lev_dev):
            for chunk in range(span // SUBLANES):
                start = level * span + chunk * SUBLANES
                found = jnp.zeros(shape, jnp.float32)
                for number in range(3):
                    values = sections[FLIPPED[number]][start : start + SUBLANES, :]
                    found = jnp.where(here[number], gather_lanes(values, low), found)
                for part in range(share):
                    field = chunk * share + part
                    rim = jnp.sum(
                        jnp.where(sub // quarters == part, found, 0.0), axis=0, keepdims=True
                    )
                    row = (field * tiles + tile) * lev_dev + level
                    out[row : row + 1, :] = 0.5 * (state[row : row + 1, :] + rim)


def finish_coarse(lev_dev, fields, tiles, coarse, sections, lists, state, out, landed):
    per = LANES // coarse
    kinds = lev_dev * fields + 1
    stride = landed.shape[0] // (tiles + 1)
    landed[...] = jnp.zeros_like(landed)
    quarters = lists[0].shape[0] // 2
    rows = sections[0].shape[0] // quarters
    lane = iota((rows, LANES), 1)
    for number in range(3):
        for quarter in range(quarters):
            chunk = sections[number][pl.ds(quarter, rows, stride=quarters), :]
            for place in range(per):
                run = lists[number][quarters, quarter * per + place]
                run = jnp.where(run < 0, tiles * per, run)
                tile, offset = run // per, run % per
                piece = jnp.where(lane // coarse == place, chunk, 0.0)
                turn = lax.rem(offset + per - place, per) * coarse
                start = pl.multiple_of(tile * stride, SUBLANES)
                landed[pl.ds(start, rows), :] = landed[pl.ds(start, rows), :] + pltpu.roll(
                    piece, turn, 1
                )
    weight_sum = landed[pl.ds(kinds - 1, tiles, stride=stride), :]
    scale = 1.0 / (1.0 + weight_sum)
    for field in range(fields):
        for level in range(lev_dev):
            here = pl.ds(field * tiles * lev_dev + level, tiles, stride=lev_dev)
            feedback = landed[pl.ds(level * fields + field, tiles, stride=stride), :]
            out[here, :] = (state[here, :] + feedback) * scale


def finish_kernel(lev_dev, fields, coarse, *refs):
    sections, lists, slots, state, out, landed = refs[:3], refs[3:6], *refs[6:]
    tiles = state.shape[0] // (fields * lev_dev)
    side = lax.axis_index("side")

    @pl.when(side == 0)
    def _():
        finish_coarse(lev_dev, fields, tiles, coarse, sections, lists, state, out, landed)

    @pl.when(side == 1)
    def _():
        finish_panel(lev_dev, fields, tiles, sections, slots, state, out)


def specs(*spaces):
    return [pl.BlockSpec(memory_space=space) for space in spaces]


def params():
    return pltpu.CompilerParams(vmem_limit_bytes=16 * 1024 * 1024)


def struct(shape, dtype=jnp.float32):
    return jax.ShapeDtypeStruct(shape, dtype)


def on_device(
    model_state, terrain_level, panel_owner, panel_cell, block_weight, block_owner, block_row
):
    groups, partners = lax.axis_size("grid"), lax.axis_size("lev")
    sides = lax.axis_size("side")
    steps = grid_steps(groups)
    _, lev_dev, fields, cell_dev = model_state.shape
    levels = terrain_level.shape[1]
    tiles = cell_dev // LANES
    blocks, coarse, _ = block_weight.shape
    panel_tiles = panel_cell.shape[0] // LANES
    quarters = panel_tiles // 2
    state = (
        model_state.reshape(lev_dev, fields, tiles, LANES)
        .transpose(1, 2, 0, 3)
        .reshape(fields * tiles * lev_dev, LANES)
    )
    terrain = (
        terrain_level.reshape(levels, tiles, LANES).transpose(1, 0, 2).reshape(tiles * levels, LANES)
    )
    message = struct((MESSAGE_ROWS, LANES), jnp.int32)
    *requests, own, slots = pl.pallas_call(
        functools.partial(list_kernel, groups),
        out_shape=[message] * 4 + [struct((panel_tiles, LANES), jnp.int32)],
        in_specs=specs(*[VMEM] * 4),
        out_specs=specs(*[VMEM] * 5),
        scratch_shapes=[VMEM((SUBLANES, LANES), jnp.int32)] * 2,
        compiler_params=params(),
        name="lists",
    )(
        panel_owner.reshape(panel_tiles, LANES),
        panel_cell.reshape(panel_tiles, LANES),
        block_owner.reshape(1, blocks),
        block_row.reshape(1, blocks),
    )
    lists = [
        lax.ppermute(
            request,
            ("grid", "side"),
            [(tile * sides, (tile + step) % groups * sides) for tile in range(groups)],
        )
        for request, step in zip(requests, steps)
    ]
    scratch_rows = 3 * fields * quarters
    part = struct((lev_dev * scratch_rows, LANES))
    *parts, mass = pl.pallas_call(
        functools.partial(produce_kernel, lev_dev, fields, partners),
        out_shape=[part] * partners + [struct((2 * SUBLANES, LANES))],
        in_specs=specs(SMEM, *[VMEM] * 6),
        out_specs=specs(*[VMEM] * (partners + 1)),
        scratch_shapes=[
            VMEM((scratch_rows * SUBLANES, LANES), jnp.float32),
            VMEM((tiles, LANES), jnp.int32),
        ],
        compiler_params=params(),
        name="produce",
    )(own, *lists, state, terrain, block_weight)
    arrived = [parts[0]] + [
        lax.ppermute(parts[distance], "lev", [(rank, rank ^ distance) for rank in range(partners)])
        for distance in range(1, partners)
    ]
    section_rows = lev_dev * fields * quarters + quarters
    section_rows += -section_rows % SUBLANES
    sections = pl.pallas_call(
        functools.partial(sum_kernel, lev_dev, fields, partners),
        out_shape=[struct((section_rows, LANES))] * 3,
        in_specs=specs(*[VMEM] * (partners + 1)),
        out_specs=specs(*[VMEM] * 3),
        compiler_params=params(),
        name="sections",
    )(*arrived, mass)
    sections = [
        lax.ppermute(
            section,
            ("grid", "side"),
            [
                (tile * sides + side, (tile + step) % groups * sides + (1 - side))
                for tile in range(groups)
                for side in range(sides)
            ],
        )
        for section, step in zip(sections, steps)
    ]
    stride = lev_dev * fields + 1
    stride += -stride % SUBLANES
    result = pl.pallas_call(
        functools.partial(finish_kernel, lev_dev, fields, coarse),
        out_shape=struct(state.shape),
        in_specs=specs(*[VMEM] * 3, *[SMEM] * 3, VMEM, VMEM),
        out_specs=pl.BlockSpec(memory_space=VMEM),
        scratch_shapes=[VMEM(((tiles + 1) * stride, LANES), jnp.float32)],
        compiler_params=params(),
        name="finish",
    )(*sections, *lists, slots, state)
    return (
        result.reshape(fields, tiles, lev_dev, LANES)
        .transpose(2, 0, 1, 3)
        .reshape(1, lev_dev, fields, cell_dev)
    )


def solution(mesh):
    in_specs = (
        P("side", "lev", None, "grid"),
        P("side", None, "grid"),
        P("grid", None),
        P("grid"),
        P("grid", None, None),
        P("grid", None),
        P("grid"),
    )
    out_specs = P("side", "lev", None, "grid")
    return jax.shard_map(
        on_device, mesh=mesh, in_specs=in_specs, out_specs=out_specs, check_vma=False
    )
```

```python
import functools

import jax
import jax.numpy as jnp
from jax import lax
from jax.experimental import pallas as pl
from jax.experimental.pallas import tpu as pltpu
from jax.sharding import PartitionSpec as P

LANES = 128
LANE_BITS = 7
SUBLANES = 8
VALUE_BITS = 16
ID_BITS = 8
MESSAGE_ROWS = 8
ROUNDS = 3
VMEM = pltpu.VMEM
SMEM = pltpu.SMEM


def partner_of(tile, number, groups):
    if groups == ROUNDS + 1:
        return tile ^ (number + 1)
    return (tile + (groups - 1, 1, groups // 2)[number]) % groups


def answer_round(number, groups):
    return number if groups == ROUNDS + 1 else (1, 0, 2)[number]


def iota(shape, dimension):
    return lax.broadcasted_iota(jnp.int32, shape, dimension)


def rank_of(hit):
    rows, lanes = hit.shape
    lane, row = iota(hit.shape, 1), iota(hit.shape, 0)
    ones = hit.astype(jnp.int32)
    running = ones
    step = 1
    while step < lanes:
        running = running + jnp.where(lane >= step, pltpu.roll(running, step, 1), 0)
        step *= 2
    total = jnp.broadcast_to(jnp.sum(ones, axis=1, keepdims=True), hit.shape)
    above = jnp.where(row >= 1, pltpu.roll(total, 1, 0), 0)
    step = 1
    while step < rows:
        above = above + jnp.where(row >= step, pltpu.roll(above, step, 0), 0)
        step *= 2
    return running - ones + above


def squeeze(hit, rank, value, value_bits):
    rows, lanes = hit.shape
    lane, row = iota(hit.shape, 1), iota(hit.shape, 0)
    held = jnp.where(hit, ((row * lanes + lane - rank) << value_bits) | value, -1)
    bit = 0
    while 1 << bit < rows * lanes:
        step = 1 << bit
        if step < lanes:
            turned = pltpu.roll(held, lanes - step, 1)
            coming = jnp.where(lane < lanes - step, turned, pltpu.roll(turned, rows - 1, 0))
        else:
            coming = pltpu.roll(held, rows - step // lanes, 0)
        comes = (coming >= 0) & ((coming >> (value_bits + bit)) & 1 == 1)
        stays = (held >= 0) & ((held >> (value_bits + bit)) & 1 == 0)
        held = jnp.where(comes, coming, jnp.where(stays, held, -1))
        bit += 1
    return jnp.where(held >= 0, held & ((1 << value_bits) - 1), -1)


def list_kernel(groups, owner_ref, block_ref, row_ref, cell_ref, *refs):
    first, second, own_ref, slot_ref, block_pad, row_pad = refs
    blocks = block_ref.shape[1]
    block_pad[...] = jnp.full(block_pad.shape, -1, jnp.int32)
    row_pad[...] = jnp.zeros(row_pad.shape, jnp.int32)
    block_pad[0:1, 0:blocks] = block_ref[...]
    row_pad[0:1, 0:blocks] = row_ref[...]
    tile, side = lax.axis_index("grid"), lax.axis_index("side")
    owners = owner_ref[...]
    landing = block_pad[...]
    marked = row_pad[...] | (iota(landing.shape, 1) << VALUE_BITS)
    half = owners.shape[0] // 2
    hits = [owners == partner_of(tile, number, groups) for number in range(ROUNDS)]
    ranks = [rank_of(hit) for hit in hits]
    cells = cell_ref[...]
    slots = jnp.zeros_like(owners)
    own_ref[...] = jnp.full(own_ref.shape, -1, jnp.int32)
    pages = []
    for number in range(ROUNDS):
        partner = partner_of(tile, number, groups)
        hit, rank = hits[number], ranks[number]
        slots = jnp.where(hit, number * half * LANES + rank, slots)
        wanted = squeeze(hit, rank, cells, VALUE_BITS)
        lands = landing == partner
        block = squeeze(lands, rank_of(lands), marked, VALUE_BITS + ID_BITS)
        rows = jnp.where(block >= 0, block & ((1 << VALUE_BITS) - 1), -1)
        pages.append((jnp.maximum(wanted[0:half], 0), rows[0:1]))
        own_ref[number : number + 1, :] = jnp.where(block >= 0, block >> VALUE_BITS, -1)[0:1]
    slot_ref[...] = slots
    for target, (here, there) in ((first, (pages[0], pages[2])), (second, (pages[1], pages[1]))):
        target[...] = jnp.full(target.shape, -1, jnp.int32)
        target[0:half, :] = jnp.where(side == 0, here[0], there[0])
        target[half : half + 1, :] = jnp.where(side == 0, here[1], there[1])


def gather_lanes(values, index):
    return jnp.take_along_axis(values, index, axis=1)


def fold(values, least):
    step = values.shape[0] // 2
    while step >= least:
        values = values + pltpu.roll(values, step, 0)
        step //= 2
    return values


def panel_rows(lev_dev, fields, tiles, groups, lists, group, state, terrain, packed, scratch):
    levels = SUBLANES
    bits = (levels - 1).bit_length()
    total = jnp.zeros((tiles, LANES), jnp.int32)
    for level in range(levels):
        total = total | (terrain[pl.ds(level, tiles, stride=levels), :] << (bits * level))
    packed[...] = total
    shape = (SUBLANES, LANES)
    sub = iota(shape, 0)
    per = SUBLANES // lev_dev
    quarters = lists[0].shape[0] // 2
    for number in range(ROUNDS):
        for quarter in range(quarters):
            cells = jnp.broadcast_to(lists[number][quarter : quarter + 1, :], shape)
            high, low = cells >> LANE_BITS, cells & (LANES - 1)
            sums = [jnp.zeros(shape, jnp.float32) for _ in range(fields)]
            for chunk in range(tiles // per):
                here = high == chunk * per + sub // lev_dev
                for field in range(fields):
                    start = field * tiles * lev_dev + chunk * SUBLANES
                    got = gather_lanes(state[start : start + SUBLANES, :], low)
                    sums[field] = jnp.where(here, got, sums[field])
            code = jnp.zeros(shape, jnp.int32)
            for chunk in range(tiles // SUBLANES):
                got = gather_lanes(packed[chunk * SUBLANES : (chunk + 1) * SUBLANES, :], low)
                code = jnp.where(high == chunk * SUBLANES + sub, got, code)
            code = fold(code, 1)
            source = (code >> (bits * sub)) & (levels - 1)
            section = answer_round(number, groups)
            for field in range(fields):
                both = fold(sums[field], lev_dev)
                placed = jnp.zeros(shape, jnp.float32)
                for level in range(lev_dev):
                    one = both
                    for turn in range(1, lev_dev):
                        one = jnp.where((sub - level) % lev_dev == turn, pltpu.roll(both, turn, 0), one)
                    placed = jnp.where(source == group * lev_dev + level, one, placed)
                row = ((section * fields + field) * quarters + quarter) * levels
                scratch[row : row + levels, :] = placed


def block_rows(lev_dev, fields, tiles, own, group, state, terrain, weight, scratch, mass):
    levels = SUBLANES
    coarse = weight.shape[1]
    per = LANES // coarse
    quarters = tiles // 2 // per

    def one_tile(index, carry):
        number, quarter = index // quarters, index % quarters
        pl.when(own[number, quarter * per] >= 0)(lambda: fill_tile(index, number, quarter))
        return carry

    def fill_tile(index, number, quarter):
        lefts, rights = [], []
        for place in range(per):
            name = own[number, quarter * per + place]
            block = jnp.maximum(name, 0)
            source = terrain[pl.ds(pl.multiple_of(block * levels, levels), levels), :]
            parts = []
            for field in range(fields):
                placed = jnp.zeros((levels, LANES), jnp.float32)
                for level in range(lev_dev):
                    line = state[pl.ds((field * tiles + block) * lev_dev + level, 1), :]
                    placed = jnp.where(source == group * lev_dev + level, line, placed)
                parts.append(placed)
            moved = jnp.concatenate(parts, axis=0)
            moved_high = moved.astype(jnp.bfloat16)
            moved_low = (moved - moved_high.astype(jnp.float32)).astype(jnp.bfloat16)
            lefts.append(
                jnp.concatenate(
                    [moved_high, moved_low, jnp.ones((2 * SUBLANES, LANES), jnp.bfloat16)], axis=0
                )
            )
            dense = jnp.where(name >= 0, weight[block], 0.0)
            dense_high = dense.astype(jnp.bfloat16)
            dense_low = (dense - dense_high.astype(jnp.float32)).astype(jnp.bfloat16)
            blank = jnp.zeros((coarse, LANES), jnp.bfloat16)
            rights.append(
                jnp.concatenate(
                    [dense_high if other == place else blank for other in range(per)]
                    + [dense_low if other == place else blank for other in range(per)],
                    axis=0,
                )
            )
        product = lax.dot_general(
            jnp.concatenate(lefts, axis=1),
            jnp.concatenate(rights, axis=1),
            (((1,), (1,)), ((), ())),
            preferred_element_type=jnp.float32,
        )
        product = product[:, :LANES] + product[:, LANES:]
        rows = fields * levels
        result = product[:rows] + product[rows : 2 * rows]
        for field in range(fields):
            row = ((number * fields + field) * quarters + quarter) * levels
            scratch[pl.ds(pl.multiple_of(row, levels), levels), :] = result[
                field * levels : (field + 1) * levels
            ]
        mass[pl.ds(index, 1), :] = product[2 * rows : 2 * rows + 1]

    lax.fori_loop(0, ROUNDS * quarters, one_tile, 0)


def produce_kernel(lev_dev, fields, partners, groups, own, *refs):
    lists, state, terrain, weight = refs[:3], refs[3], refs[4], refs[5]
    parts = refs[6 : 6 + partners]
    mass, scratch, packed = refs[6 + partners :]
    tiles = terrain.shape[0] // SUBLANES
    side, group = lax.axis_index("side"), lax.axis_index("lev")

    @pl.when(side == 0)
    def _():
        mass[...] = jnp.zeros_like(mass)
        panel_rows(lev_dev, fields, tiles, groups, lists, group, state, terrain, packed, scratch)

    @pl.when(side == 1)
    def _():
        block_rows(lev_dev, fields, tiles, own, group, state, terrain, weight, scratch, mass)

    rows = scratch.shape[0] // SUBLANES
    for distance in range(partners):
        target = group ^ distance
        for level in range(lev_dev):
            parts[distance][level * rows : (level + 1) * rows, :] = scratch[
                pl.ds(target * lev_dev + level, rows, stride=SUBLANES), :
            ]


def sum_kernel(lev_dev, fields, partners, *refs):
    parts, mass, sections = refs[:partners], refs[partners], refs[partners + 1 :]
    total = parts[0][...]
    for part in parts[1:]:
        total = total + part[...]
    rows = total.shape[0] // lev_dev
    span = rows // 3
    quarters = span // fields
    for number, section in enumerate(sections):
        for level in range(lev_dev):
            start = level * rows + number * span
            section[level * span : (level + 1) * span, :] = total[start : start + span]
        section[lev_dev * span : lev_dev * span + quarters, :] = mass[
            number * quarters : (number + 1) * quarters, :
        ]
        tail = lev_dev * span + quarters
        section[tail:, :] = jnp.zeros((section.shape[0] - tail, LANES), jnp.float32)


def finish_panel(lev_dev, fields, tiles, groups, sections, slots, state, out):
    shape = (SUBLANES, LANES)
    sub = iota(shape, 0)
    out[...] = state[...]
    panel_tiles = slots.shape[0]
    quarters = panel_tiles // 2
    span = fields * quarters
    share = SUBLANES // quarters
    for tile in range(panel_tiles):
        place = jnp.broadcast_to(slots[tile : tile + 1, :], shape)
        high, low = place >> LANE_BITS, place & (LANES - 1)
        here = [high == number * quarters + sub % quarters for number in range(ROUNDS)]
        for level in range(lev_dev):
            for chunk in range(span // SUBLANES):
                start = level * span + chunk * SUBLANES
                found = jnp.zeros(shape, jnp.float32)
                for number in range(ROUNDS):
                    values = sections[answer_round(number, groups)][start : start + SUBLANES, :]
                    found = jnp.where(here[number], gather_lanes(values, low), found)
                for part in range(share):
                    field = chunk * share + part
                    rim = jnp.sum(
                        jnp.where(sub // quarters == part, found, 0.0), axis=0, keepdims=True
                    )
                    row = (field * tiles + tile) * lev_dev + level
                    out[row : row + 1, :] = 0.5 * (state[row : row + 1, :] + rim)


def finish_coarse(lev_dev, fields, tiles, coarse, sections, lists, state, out, landed):
    per = LANES // coarse
    kinds = lev_dev * fields + 1
    stride = landed.shape[0] // (tiles + 1)
    landed[...] = jnp.zeros_like(landed)
    quarters = lists[0].shape[0] // 2
    rows = sections[0].shape[0] // quarters
    lane = iota((rows, LANES), 1)
    for number in range(ROUNDS):
        for quarter in range(quarters):
            chunk = sections[number][pl.ds(quarter, rows, stride=quarters), :]
            for place in range(per):
                run = lists[number][quarters, quarter * per + place]
                run = jnp.where(run < 0, tiles * per, run)
                tile, offset = run // per, run % per
                piece = jnp.where(lane // coarse == place, chunk, 0.0)
                turn = lax.rem(offset + per - place, per) * coarse
                start = pl.multiple_of(tile * stride, SUBLANES)
                landed[pl.ds(start, rows), :] = landed[pl.ds(start, rows), :] + pltpu.roll(
                    piece, turn, 1
                )
    weight_sum = landed[pl.ds(kinds - 1, tiles, stride=stride), :]
    scale = 1.0 / (1.0 + weight_sum)
    for field in range(fields):
        for level in range(lev_dev):
            here = pl.ds(field * tiles * lev_dev + level, tiles, stride=lev_dev)
            feedback = landed[pl.ds(level * fields + field, tiles, stride=stride), :]
            out[here, :] = (state[here, :] + feedback) * scale


def finish_kernel(lev_dev, fields, coarse, groups, *refs):
    sections, lists, slots, state, out, landed = refs[:3], refs[3:6], *refs[6:]
    tiles = state.shape[0] // (fields * lev_dev)
    side = lax.axis_index("side")

    @pl.when(side == 0)
    def _():
        finish_coarse(lev_dev, fields, tiles, coarse, sections, lists, state, out, landed)

    @pl.when(side == 1)
    def _():
        finish_panel(lev_dev, fields, tiles, groups, sections, slots, state, out)


def specs(*spaces):
    return [pl.BlockSpec(memory_space=space) for space in spaces]


def params():
    return pltpu.CompilerParams(vmem_limit_bytes=16 * 1024 * 1024)


def struct(shape, dtype=jnp.float32):
    return jax.ShapeDtypeStruct(shape, dtype)


def on_device(
    model_state, terrain_level, panel_owner, panel_cell, block_weight, block_owner, block_row
):
    groups, partners = lax.axis_size("grid"), lax.axis_size("lev")
    sides = lax.axis_size("side")
    _, lev_dev, fields, cell_dev = model_state.shape
    levels = terrain_level.shape[1]
    tiles = cell_dev // LANES
    blocks, coarse, _ = block_weight.shape
    panel_tiles = panel_cell.shape[0] // LANES
    quarters = panel_tiles // 2
    state = (
        model_state.reshape(lev_dev, fields, tiles, LANES)
        .transpose(1, 2, 0, 3)
        .reshape(fields * tiles * lev_dev, LANES)
    )
    terrain = (
        terrain_level.reshape(levels, tiles, LANES).transpose(1, 0, 2).reshape(tiles * levels, LANES)
    )
    message = struct((MESSAGE_ROWS, LANES), jnp.int32)
    page = struct((panel_tiles, LANES), jnp.int32)
    first, second, own, slots = pl.pallas_call(
        functools.partial(list_kernel, groups),
        out_shape=[message] * 3 + [page],
        in_specs=specs(*[VMEM] * 4),
        out_specs=specs(*[VMEM] * 4),
        scratch_shapes=[VMEM((SUBLANES, LANES), jnp.int32)] * 2,
        cost_estimate=pl.CostEstimate(flops=0, bytes_accessed=40_000_000, transcendentals=0),
        compiler_params=params(),
        name="lists",
    )(
        panel_owner.reshape(page.shape),
        block_owner.reshape(1, blocks),
        block_row.reshape(1, blocks),
        panel_cell.reshape(page.shape),
    )

    def towards(number_of, cross):
        return [
            (tile * sides + side, partner_of(tile, number_of(side), groups) * sides + (side ^ cross))
            for tile in range(groups)
            for side in range(sides)
        ]

    first = lax.ppermute(first, ("grid", "side"), towards(lambda side: 2 * side, 0))
    second = lax.ppermute(second, ("grid", "side"), towards(lambda side: 1, 0))
    third = lax.ppermute(first, "side", [(0, 1), (1, 0)])
    lists = [first, second, third]
    scratch_rows = ROUNDS * fields * quarters
    part = struct((lev_dev * scratch_rows, LANES))
    *parts, mass = pl.pallas_call(
        functools.partial(produce_kernel, lev_dev, fields, partners, groups),
        out_shape=[part] * partners + [struct((2 * SUBLANES, LANES))],
        in_specs=specs(SMEM, *[VMEM] * 6),
        out_specs=specs(*[VMEM] * (partners + 1)),
        scratch_shapes=[
            VMEM((scratch_rows * SUBLANES, LANES), jnp.float32),
            VMEM((tiles, LANES), jnp.int32),
        ],
        compiler_params=params(),
        name="produce",
    )(own, *lists, state, terrain, block_weight)
    arrived = [parts[0]] + [
        lax.ppermute(parts[distance], "lev", [(rank, rank ^ distance) for rank in range(partners)])
        for distance in range(partners - 1, 0, -1)
    ]
    section_rows = lev_dev * fields * quarters + quarters
    section_rows += -section_rows % SUBLANES
    sections = pl.pallas_call(
        functools.partial(sum_kernel, lev_dev, fields, partners),
        out_shape=[struct((section_rows, LANES))] * 3,
        in_specs=specs(*[VMEM] * (partners + 1)),
        out_specs=specs(*[VMEM] * 3),
        compiler_params=params(),
        name="sections",
    )(*arrived, mass)
    sections = [
        lax.ppermute(sections[number], ("grid", "side"), towards(lambda side: number, 1))
        for number in range(ROUNDS - 1, -1, -1)
    ][::-1]
    stride = lev_dev * fields + 1
    stride += -stride % SUBLANES
    result = pl.pallas_call(
        functools.partial(finish_kernel, lev_dev, fields, coarse, groups),
        out_shape=struct(state.shape),
        in_specs=specs(*[VMEM] * 3, *[SMEM] * 3, VMEM, VMEM),
        out_specs=pl.BlockSpec(memory_space=VMEM),
        scratch_shapes=[VMEM(((tiles + 1) * stride, LANES), jnp.float32)],
        compiler_params=params(),
        name="finish",
    )(*sections, *lists, slots, state)
    return (
        result.reshape(fields, tiles, lev_dev, LANES)
        .transpose(2, 0, 1, 3)
        .reshape(1, lev_dev, fields, cell_dev)
    )


def solution(mesh):
    in_specs = (
        P("side", "lev", None, "grid"),
        P("side", None, "grid"),
        P("grid", None),
        P("grid"),
        P("grid", None, None),
        P("grid", None),
        P("grid"),
    )
    out_specs = P("side", "lev", None, "grid")
    return jax.shard_map(
        on_device, mesh=mesh, in_specs=in_specs, out_specs=out_specs, check_vma=False
    )
```

```python
import functools

import jax
import jax.numpy as jnp
from jax import lax
from jax.experimental import pallas as pl
from jax.experimental.pallas import tpu as pltpu
from jax.sharding import PartitionSpec as P

LANES = 128
LANE_BITS = 7
SUBLANES = 8
VALUE_BITS = 16
ID_BITS = 8
MESSAGE_ROWS = 8
HELD_ROWS = 16
ROUNDS = 3
TOGETHER = 2
VMEM = pltpu.VMEM
SMEM = pltpu.SMEM


def partner_of(tile, number, groups):
    if groups == ROUNDS + 1:
        return tile ^ (number + 1)
    return (tile + (groups - 1, 1, groups // 2)[number]) % groups


def answer_round(number, groups):
    return number if groups == ROUNDS + 1 else (1, 0, 2)[number]


def iota(shape, dimension):
    return lax.broadcasted_iota(jnp.int32, shape, dimension)


def rank_of(hit):
    rows, lanes = hit.shape
    lane, row = iota(hit.shape, 1), iota(hit.shape, 0)
    ones = hit.astype(jnp.int32)
    running = ones
    step = 1
    while step < lanes:
        running = running + jnp.where(lane >= step, pltpu.roll(running, step, 1), 0)
        step *= 2
    total = jnp.broadcast_to(jnp.sum(ones, axis=1, keepdims=True), hit.shape)
    above = jnp.where(row >= 1, pltpu.roll(total, 1, 0), 0)
    step = 1
    while step < rows:
        above = above + jnp.where(row >= step, pltpu.roll(above, step, 0), 0)
        step *= 2
    return running - ones + above


def squeeze(hit, rank, value, value_bits):
    rows, lanes = hit.shape
    lane, row = iota(hit.shape, 1), iota(hit.shape, 0)
    held = jnp.where(hit, ((row * lanes + lane - rank) << value_bits) | value, -1)
    bit = 0
    while 1 << bit < rows * lanes:
        step = 1 << bit
        if step < lanes:
            turned = pltpu.roll(held, lanes - step, 1)
            coming = jnp.where(lane < lanes - step, turned, pltpu.roll(turned, rows - 1, 0))
        else:
            coming = pltpu.roll(held, rows - step // lanes, 0)
        comes = (coming >= 0) & ((coming >> (value_bits + bit)) & 1 == 1)
        stays = (held >= 0) & ((held >> (value_bits + bit)) & 1 == 0)
        held = jnp.where(comes, coming, jnp.where(stays, held, -1))
        bit += 1
    return jnp.where(held >= 0, held & ((1 << value_bits) - 1), -1)


def list_kernel(groups, owner_ref, block_ref, row_ref, *refs):
    sources, (first, second, own_ref, slot_ref, *kept) = refs[:4], refs[4:11]
    cell_ref, block_pad, row_pad, sems = refs[11:]
    copies = [
        pltpu.make_async_copy(source, target, sems.at[index])
        for index, (source, target) in enumerate(zip(sources, (cell_ref, *kept)))
    ]
    for copy in copies:
        copy.start()
    blocks = block_ref.shape[1]
    block_pad[...] = jnp.full(block_pad.shape, -1, jnp.int32)
    row_pad[...] = jnp.zeros(row_pad.shape, jnp.int32)
    block_pad[0:1, 0:blocks] = block_ref[...]
    row_pad[0:1, 0:blocks] = row_ref[...]
    tile, side = lax.axis_index("grid"), lax.axis_index("side")
    owners = owner_ref[...]
    landing = block_pad[...]
    marked = row_pad[...] | (iota(landing.shape, 1) << VALUE_BITS)
    half = owners.shape[0] // 2
    hits = [owners == partner_of(tile, number, groups) for number in range(ROUNDS)]
    ranks = [rank_of(hit) for hit in hits]
    copies[0].wait()
    cells = cell_ref[...]
    slots = jnp.zeros_like(owners)
    own_ref[...] = jnp.full(own_ref.shape, -1, jnp.int32)
    pages = []
    for number in range(ROUNDS):
        partner = partner_of(tile, number, groups)
        hit, rank = hits[number], ranks[number]
        slots = jnp.where(hit, number * half * LANES + rank, slots)
        wanted = squeeze(hit, rank, cells, VALUE_BITS)
        lands = landing == partner
        block = squeeze(lands, rank_of(lands), marked, VALUE_BITS + ID_BITS)
        rows = jnp.where(block >= 0, block & ((1 << VALUE_BITS) - 1), -1)
        pages.append((jnp.maximum(wanted[0:half], 0), rows[0:1]))
        own_ref[number : number + 1, :] = jnp.where(block >= 0, block >> VALUE_BITS, -1)[0:1]
    slot_ref[...] = slots
    for target, (here, there) in ((first, (pages[0], pages[2])), (second, (pages[1], pages[1]))):
        target[...] = jnp.full(target.shape, -1, jnp.int32)
        target[0:half, :] = jnp.where(side == 0, here[0], there[0])
        target[half : half + 1, :] = jnp.where(side == 0, here[1], there[1])
    for copy in copies[1:]:
        copy.wait()


def gather_lanes(values, index):
    return jnp.take_along_axis(values, index, axis=1, mode="promise_in_bounds")


def fold(values, least):
    step = values.shape[0] // 2
    while step >= least:
        values = values + pltpu.roll(values, step, 0)
        step //= 2
    return values


def panel_rows(lev_dev, fields, tiles, groups, lists, group, state, terrain, packed, scratch):
    levels = SUBLANES
    bits = (levels - 1).bit_length()
    total = jnp.zeros((tiles, LANES), jnp.int32)
    for level in range(levels):
        total = total | (terrain[pl.ds(level, tiles, stride=levels), :] << (bits * level))
    packed[...] = total
    shape = (SUBLANES, LANES)
    sub = iota(shape, 0)
    per = SUBLANES // lev_dev
    quarters = lists[0].shape[0] // 2
    for number in range(ROUNDS):
        for quarter in range(quarters):
            cells = jnp.broadcast_to(lists[number][quarter : quarter + 1, :], shape)
            high, low = cells >> LANE_BITS, cells & (LANES - 1)
            sums = [jnp.zeros(shape, jnp.float32) for _ in range(fields)]
            code = jnp.zeros(shape, jnp.int32)
            for chunk in range(tiles // per):
                here = high == chunk * per + sub // lev_dev
                for field in range(fields):
                    start = field * tiles * lev_dev + chunk * SUBLANES
                    got = gather_lanes(state[start : start + SUBLANES, :], low)
                    sums[field] = jnp.where(here, got, sums[field])
            for chunk in range(tiles // SUBLANES):
                got = gather_lanes(packed[chunk * SUBLANES : (chunk + 1) * SUBLANES, :], low)
                code = jnp.where(high == chunk * SUBLANES + sub, got, code)
            source = (fold(code, 1) >> (bits * sub)) & (levels - 1)
            section = answer_round(number, groups)
            for field in range(fields):
                both = fold(sums[field], lev_dev)
                placed = jnp.zeros(shape, jnp.float32)
                for level in range(lev_dev):
                    one = both
                    for turn in range(1, lev_dev):
                        one = jnp.where((sub - level) % lev_dev == turn, pltpu.roll(both, turn, 0), one)
                    placed = jnp.where(source == group * lev_dev + level, one, placed)
                row = ((section * fields + field) * quarters + quarter) * levels
                scratch[row : row + levels, :] = placed


def block_rows(lev_dev, fields, tiles, own, group, state, terrain, weight, scratch, mass):
    levels = SUBLANES
    coarse = weight.shape[1]
    per = LANES // coarse
    quarters = tiles // 2 // per

    def some_tiles(index, carry):
        number, quarter = index // (quarters // TOGETHER), index % (quarters // TOGETHER) * TOGETHER

        @pl.when(own[number, quarter * per] >= 0)
        def _():
            for more in range(TOGETHER):
                fill_tile(number * quarters + quarter + more, number, quarter + more)

        return carry

    def fill_tile(index, number, quarter):
        lefts, rights = [], []
        for place in range(per):
            name = own[number, quarter * per + place]
            block = jnp.maximum(name, 0)
            source = terrain[pl.ds(pl.multiple_of(block * levels, levels), levels), :]
            parts = []
            for field in range(fields):
                placed = jnp.zeros((levels, LANES), jnp.float32)
                for level in range(lev_dev):
                    line = state[pl.ds((field * tiles + block) * lev_dev + level, 1), :]
                    placed = jnp.where(source == group * lev_dev + level, line, placed)
                parts.append(placed)
            moved = jnp.concatenate(parts, axis=0)
            moved_high = moved.astype(jnp.bfloat16)
            moved_low = (moved - moved_high.astype(jnp.float32)).astype(jnp.bfloat16)
            lefts.append(
                jnp.concatenate(
                    [moved_high, moved_low, jnp.ones((2 * SUBLANES, LANES), jnp.bfloat16)], axis=0
                )
            )
            dense = jnp.where(name >= 0, weight[block], 0.0)
            dense_high = dense.astype(jnp.bfloat16)
            dense_low = (dense - dense_high.astype(jnp.float32)).astype(jnp.bfloat16)
            blank = jnp.zeros((coarse, LANES), jnp.bfloat16)
            rights.append(
                jnp.concatenate(
                    [dense_high if other == place else blank for other in range(per)]
                    + [dense_low if other == place else blank for other in range(per)],
                    axis=0,
                )
            )
        product = lax.dot_general(
            jnp.concatenate(lefts, axis=1),
            jnp.concatenate(rights, axis=1),
            (((1,), (1,)), ((), ())),
            preferred_element_type=jnp.float32,
        )
        product = product[:, :LANES] + product[:, LANES:]
        rows = fields * levels
        result = product[:rows] + product[rows : 2 * rows]
        for field in range(fields):
            row = ((number * fields + field) * quarters + quarter) * levels
            scratch[pl.ds(pl.multiple_of(row, levels), levels), :] = result[
                field * levels : (field + 1) * levels
            ]
        mass[pl.ds(index, 1), :] = product[2 * rows : 2 * rows + 1]

    lax.fori_loop(0, ROUNDS * quarters // TOGETHER, some_tiles, 0)


def produce_kernel(lev_dev, fields, partners, groups, own, *refs):
    lists, state, terrain, weight = refs[:3], refs[3], refs[4], refs[5]
    parts = refs[6 : 6 + partners]
    mass, scratch, packed = refs[6 + partners :]
    tiles = terrain.shape[0] // SUBLANES
    side, group = lax.axis_index("side"), lax.axis_index("lev")

    @pl.when(side == 0)
    def _():
        mass[...] = jnp.zeros_like(mass)
        panel_rows(lev_dev, fields, tiles, groups, lists, group, state, terrain, packed, scratch)

    @pl.when(side == 1)
    def _():
        block_rows(lev_dev, fields, tiles, own, group, state, terrain, weight, scratch, mass)

    rows = scratch.shape[0] // SUBLANES
    for distance in range(partners):
        target = group ^ distance
        for level in range(lev_dev):
            parts[distance][level * rows : (level + 1) * rows, :] = scratch[
                pl.ds(target * lev_dev + level, rows, stride=SUBLANES), :
            ]


def sum_kernel(lev_dev, fields, partners, *refs):
    parts, mass, sections = refs[:partners], refs[partners], refs[partners + 1 :]
    total = parts[0][...]
    for part in parts[1:]:
        total = total + part[...]
    rows = total.shape[0] // lev_dev
    span = rows // 3
    quarters = span // fields
    for number, section in enumerate(sections):
        for level in range(lev_dev):
            start = level * rows + number * span
            section[level * span : (level + 1) * span, :] = total[start : start + span]
        section[lev_dev * span : lev_dev * span + quarters, :] = mass[
            number * quarters : (number + 1) * quarters, :
        ]
        tail = lev_dev * span + quarters
        section[tail:, :] = jnp.zeros((section.shape[0] - tail, LANES), jnp.float32)


def place_panel(lev_dev, fields, number, section, slots, held):
    shape = (SUBLANES, LANES)
    sub = iota(shape, 0)
    panel_tiles = slots.shape[0]
    quarters = panel_tiles // 2
    chunks = lev_dev * fields * quarters // SUBLANES
    for tile in range(panel_tiles):
        place = jnp.broadcast_to(slots[tile : tile + 1, :], shape)
        here = place >> LANE_BITS == number * quarters + sub % quarters
        for chunk in range(chunks):
            got = gather_lanes(
                section[chunk * SUBLANES : (chunk + 1) * SUBLANES, :], place & (LANES - 1)
            )
            row = (tile * chunks + chunk) * SUBLANES
            held[row : row + SUBLANES, :] = jnp.where(here, got, held[row : row + SUBLANES, :])


def place_blocks(coarse, spare, section, runs, held):
    per = LANES // coarse
    quarters = section.shape[0] // HELD_ROWS
    lane = iota((HELD_ROWS, LANES), 1)
    for quarter in range(quarters):
        chunk = section[pl.ds(quarter, HELD_ROWS, stride=quarters), :]
        for place in range(per):
            run = runs[quarters, quarter * per + place]
            run = jnp.where(run < 0, spare * per, run)
            turn = (run + (per - place)) % per * coarse
            start = pl.multiple_of(run // per * HELD_ROWS, SUBLANES)
            piece = pltpu.roll(jnp.where(lane // coarse == place, chunk, 0.0), turn, 1)
            held[pl.ds(start, HELD_ROWS), :] = held[pl.ds(start, HELD_ROWS), :] + piece


def place_kernel(lev_dev, fields, coarse, groups, spare, numbers, *refs):
    count = len(numbers)
    sections, runs = refs[:count], refs[count : 2 * count]
    slots, held_in, held = refs[2 * count], refs[2 * count + 1], refs[-1]
    del held_in
    side = lax.axis_index("side")

    @pl.when(side == 0)
    def _():
        for section, run in zip(sections, runs):
            place_blocks(coarse, spare, section, run, held)

    @pl.when(side == 1)
    def _():
        for section, number in zip(sections, numbers):
            place_panel(lev_dev, fields, answer_round(number, groups), section, slots, held)


def finish_panel(lev_dev, fields, tiles, panel_tiles, held, state, staged, send):
    shape = (SUBLANES, LANES)
    sub = iota(shape, 0)
    quarters = panel_tiles // 2
    chunks = lev_dev * fields * quarters // SUBLANES
    share = SUBLANES // quarters
    rows = tiles * lev_dev
    for field in range(fields):
        start = field * rows
        part = field % share
        for tile in range(panel_tiles):
            for level in range(lev_dev):
                chunk = (level * fields + field) // share
                row = (tile * chunks + chunk) * SUBLANES
                rim = jnp.sum(
                    jnp.where(sub // quarters == part, held[row : row + SUBLANES, :], 0.0),
                    axis=0,
                    keepdims=True,
                )
                row = start + tile * lev_dev + level
                staged[row : row + 1, :] = 0.5 * (state[row : row + 1, :] + rim)
        rest = start + panel_tiles * lev_dev
        staged[rest : start + rows, :] = state[rest : start + rows, :]
        send(field)


def finish_coarse(lev_dev, fields, tiles, held, state, staged, send):
    weight_sum = held[pl.ds(lev_dev * fields, tiles, stride=HELD_ROWS), :]
    scale = 1.0 / (1.0 + weight_sum)
    for field in range(fields):
        for level in range(lev_dev):
            here = pl.ds(field * tiles * lev_dev + level, tiles, stride=lev_dev)
            feedback = held[pl.ds(level * fields + field, tiles, stride=HELD_ROWS), :]
            staged[here, :] = (state[here, :] + feedback) * scale
        send(field)


def finish_kernel(lev_dev, fields, coarse, groups, spare, numbers, *refs):
    count = len(numbers)
    slots, state = refs[2 * count], refs[2 * count + 2]
    out, held, staged, sems = refs[2 * count + 3 :]
    held[...] = refs[2 * count + 1][...]
    place_kernel(lev_dev, fields, coarse, groups, spare, numbers, *refs[: 2 * count + 2], held)
    tiles = spare
    rows = tiles * lev_dev
    copies = [
        pltpu.make_async_copy(
            staged.at[field * rows : (field + 1) * rows],
            out.at[field * rows : (field + 1) * rows],
            sems.at[field],
        )
        for field in range(fields)
    ]
    side = lax.axis_index("side")

    @pl.when(side == 0)
    def _():
        finish_coarse(
            lev_dev, fields, tiles, held, state, staged, lambda field: copies[field].start()
        )

    @pl.when(side == 1)
    def _():
        finish_panel(
            lev_dev, fields, tiles, slots.shape[0], held, state, staged, lambda field: copies[field].start()
        )

    for copy in copies:
        copy.wait()


def specs(*spaces):
    return [pl.BlockSpec(memory_space=space) for space in spaces]


def params():
    return pltpu.CompilerParams(vmem_limit_bytes=16 * 1024 * 1024)


def in_hbm(value):
    return pltpu.with_memory_space_constraint(value, pltpu.HBM)


def struct(shape, dtype=jnp.float32):
    return jax.ShapeDtypeStruct(shape, dtype)


def on_device(
    model_state, terrain_level, panel_owner, panel_cell, block_weight, block_owner, block_row
):
    groups, partners = lax.axis_size("grid"), lax.axis_size("lev")
    sides = lax.axis_size("side")
    _, lev_dev, fields, cell_dev = model_state.shape
    levels = terrain_level.shape[1]
    tiles = cell_dev // LANES
    blocks, coarse, _ = block_weight.shape
    panel_tiles = panel_cell.shape[0] // LANES
    quarters = panel_tiles // 2
    state = (
        model_state.reshape(lev_dev, fields, tiles, LANES)
        .transpose(1, 2, 0, 3)
        .reshape(fields * tiles * lev_dev, LANES)
    )
    terrain = (
        terrain_level.reshape(levels, tiles, LANES).transpose(1, 0, 2).reshape(tiles * levels, LANES)
    )
    message = struct((MESSAGE_ROWS, LANES), jnp.int32)
    page = struct((panel_tiles, LANES), jnp.int32)
    first, second, own, slots, state, terrain, weight = pl.pallas_call(
        functools.partial(list_kernel, groups),
        out_shape=[message] * 3
        + [page]
        + [struct(state.shape), struct(terrain.shape, jnp.int32), struct(block_weight.shape)],
        in_specs=specs(*[VMEM] * 3, *[pl.ANY] * 4),
        out_specs=specs(*[VMEM] * 7),
        scratch_shapes=[
            VMEM(page.shape, jnp.int32),
            VMEM((SUBLANES, LANES), jnp.int32),
            VMEM((SUBLANES, LANES), jnp.int32),
            pltpu.SemaphoreType.DMA((4,)),
        ],
        compiler_params=params(),
        name="lists",
    )(
        panel_owner.reshape(page.shape),
        block_owner.reshape(1, blocks),
        block_row.reshape(1, blocks),
        panel_cell.reshape(page.shape),
        in_hbm(state),
        in_hbm(terrain),
        in_hbm(block_weight),
    )

    def towards(number_of, cross):
        return [
            (tile * sides + side, partner_of(tile, number_of(side), groups) * sides + (side ^ cross))
            for tile in range(groups)
            for side in range(sides)
        ]

    first = lax.ppermute(first, ("grid", "side"), towards(lambda side: 2 * side, 0))
    second = lax.ppermute(second, ("grid", "side"), towards(lambda side: 1, 0))
    third = lax.ppermute(first, "side", [(0, 1), (1, 0)])
    lists = [first, second, third]
    scratch_rows = ROUNDS * fields * quarters
    part = struct((lev_dev * scratch_rows, LANES))
    *parts, mass = pl.pallas_call(
        functools.partial(produce_kernel, lev_dev, fields, partners, groups),
        out_shape=[part] * partners + [struct((2 * SUBLANES, LANES))],
        in_specs=specs(SMEM, *[VMEM] * 6),
        out_specs=specs(*[VMEM] * (partners + 1)),
        scratch_shapes=[
            VMEM((scratch_rows * SUBLANES, LANES), jnp.float32),
            VMEM((tiles, LANES), jnp.int32),
        ],
        compiler_params=params(),
        name="produce",
    )(own, *lists, state, terrain, weight)
    arrived = [parts[0]] + [
        lax.ppermute(parts[distance], "lev", [(rank, rank ^ distance) for rank in range(partners)])
        for distance in range(partners - 1, 0, -1)
    ]
    section_rows = HELD_ROWS * quarters
    sections = pl.pallas_call(
        functools.partial(sum_kernel, lev_dev, fields, partners),
        out_shape=[struct((section_rows, LANES))] * 3,
        in_specs=specs(*[VMEM] * (partners + 1)),
        out_specs=specs(*[VMEM] * 3),
        compiler_params=params(),
        name="sections",
    )(*arrived, mass)
    sections = [
        lax.ppermute(sections[number], ("grid", "side"), towards(lambda side: number, 1))
        for number in range(ROUNDS - 1, -1, -1)
    ][::-1]
    held_shape = ((tiles + 1) * HELD_ROWS, LANES)
    held = jnp.zeros(held_shape, jnp.float32)
    sizes = (lev_dev, fields, coarse, groups, tiles)
    for number in range(ROUNDS - 1, 0, -1):
        held = pl.pallas_call(
            functools.partial(place_kernel, *sizes, [number]),
            out_shape=struct(held_shape),
            in_specs=specs(VMEM, SMEM, VMEM, VMEM),
            out_specs=pl.BlockSpec(memory_space=VMEM),
            input_output_aliases={3: 0},
            compiler_params=params(),
            name="place",
        )(sections[number], lists[number], slots, held)
    result = pl.pallas_call(
        functools.partial(finish_kernel, *sizes, [0]),
        out_shape=pltpu.HBM(state.shape, jnp.float32),
        in_specs=specs(VMEM, SMEM, VMEM, VMEM, VMEM),
        out_specs=pl.BlockSpec(memory_space=pltpu.HBM),
        scratch_shapes=[
            VMEM(held_shape, jnp.float32),
            VMEM(state.shape, jnp.float32),
            pltpu.SemaphoreType.DMA((fields,)),
        ],
        compiler_params=params(),
        name="finish",
    )(sections[0], lists[0], slots, held, state)
    return (
        result.reshape(fields, tiles, lev_dev, LANES)
        .transpose(2, 0, 1, 3)
        .reshape(1, lev_dev, fields, cell_dev)
    )


def solution(mesh):
    in_specs = (
        P("side", "lev", None, "grid"),
        P("side", None, "grid"),
        P("grid", None),
        P("grid"),
        P("grid", None, None),
        P("grid", None),
        P("grid"),
    )
    out_specs = P("side", "lev", None, "grid")
    return jax.shard_map(
        on_device, mesh=mesh, in_specs=in_specs, out_specs=out_specs, check_vma=False
    )
```

```python
import functools

import jax
import jax.numpy as jnp
from jax import lax
from jax.experimental import pallas as pl
from jax.experimental.pallas import tpu as pltpu
from jax.sharding import PartitionSpec as P

LANES = 128
LANE_BITS = 7
SUBLANES = 8
VALUE_BITS = 16
ID_BITS = 8
MESSAGE_ROWS = 8
HELD_ROWS = 16
ROUNDS = 3
TOGETHER = 2
VMEM = pltpu.VMEM
SMEM = pltpu.SMEM


def partner_of(tile, number, groups):
    if groups == ROUNDS + 1:
        return tile ^ (number + 1)
    return (tile + (groups - 1, 1, groups // 2)[number]) % groups


def answer_round(number, groups):
    return number if groups == ROUNDS + 1 else (1, 0, 2)[number]


def iota(shape, dimension):
    return lax.broadcasted_iota(jnp.int32, shape, dimension)


def rank_of(hit):
    rows, lanes = hit.shape
    lane, row = iota(hit.shape, 1), iota(hit.shape, 0)
    ones = hit.astype(jnp.int32)
    running = ones
    step = 1
    while step < lanes:
        running = running + jnp.where(lane >= step, pltpu.roll(running, step, 1), 0)
        step *= 2
    total = jnp.broadcast_to(jnp.sum(ones, axis=1, keepdims=True), hit.shape)
    above = jnp.where(row >= 1, pltpu.roll(total, 1, 0), 0)
    step = 1
    while step < rows:
        above = above + jnp.where(row >= step, pltpu.roll(above, step, 0), 0)
        step *= 2
    return running - ones + above


def squeeze(hit, rank, value, value_bits):
    rows, lanes = hit.shape
    lane, row = iota(hit.shape, 1), iota(hit.shape, 0)
    held = jnp.where(hit, ((row * lanes + lane - rank) << value_bits) | value, -1)
    bit = 0
    while 1 << bit < rows * lanes:
        step = 1 << bit
        if step < lanes:
            turned = pltpu.roll(held, lanes - step, 1)
            coming = jnp.where(lane < lanes - step, turned, pltpu.roll(turned, rows - 1, 0))
        else:
            coming = pltpu.roll(held, rows - step // lanes, 0)
        comes = (coming >= 0) & ((coming >> (value_bits + bit)) & 1 == 1)
        stays = (held >= 0) & ((held >> (value_bits + bit)) & 1 == 0)
        held = jnp.where(comes, coming, jnp.where(stays, held, -1))
        bit += 1
    return jnp.where(held >= 0, held & ((1 << value_bits) - 1), -1)


def list_kernel(groups, owner_ref, block_ref, row_ref, *refs):
    sources, (first, second, own_ref, slot_ref, *kept) = refs[:4], refs[4:11]
    cell_ref, block_pad, row_pad, sems = refs[11:]
    copies = [
        pltpu.make_async_copy(source, target, sems.at[index])
        for index, (source, target) in enumerate(zip(sources, (cell_ref, *kept)))
    ]
    for copy in copies:
        copy.start()
    blocks = block_ref.shape[1]
    block_pad[...] = jnp.full(block_pad.shape, -1, jnp.int32)
    row_pad[...] = jnp.zeros(row_pad.shape, jnp.int32)
    block_pad[0:1, 0:blocks] = block_ref[...]
    row_pad[0:1, 0:blocks] = row_ref[...]
    tile, side = lax.axis_index("grid"), lax.axis_index("side")
    owners = owner_ref[...]
    landing = block_pad[...]
    marked = row_pad[...] | (iota(landing.shape, 1) << VALUE_BITS)
    half = owners.shape[0] // 2
    hits = [owners == partner_of(tile, number, groups) for number in range(ROUNDS)]
    ranks = [rank_of(hit) for hit in hits]
    copies[0].wait()
    cells = cell_ref[...]
    slots = jnp.zeros_like(owners)
    own_ref[...] = jnp.full(own_ref.shape, -1, jnp.int32)
    pages = []
    for number in range(ROUNDS):
        partner = partner_of(tile, number, groups)
        hit, rank = hits[number], ranks[number]
        slots = jnp.where(hit, number * half * LANES + rank, slots)
        wanted = squeeze(hit, rank, cells, VALUE_BITS)
        lands = landing == partner
        block = squeeze(lands, rank_of(lands), marked, VALUE_BITS + ID_BITS)
        rows = jnp.where(block >= 0, block & ((1 << VALUE_BITS) - 1), -1)
        pages.append((jnp.maximum(wanted[0:half], 0), rows[0:1]))
        own_ref[number : number + 1, :] = jnp.where(block >= 0, block >> VALUE_BITS, -1)[0:1]
    slot_ref[...] = slots
    for target, (here, there) in ((first, (pages[0], pages[2])), (second, (pages[1], pages[1]))):
        target[...] = jnp.full(target.shape, -1, jnp.int32)
        target[0:half, :] = jnp.where(side == 0, here[0], there[0])
        target[half : half + 1, :] = jnp.where(side == 0, here[1], there[1])
    for copy in copies[1:]:
        copy.wait()


def gather_lanes(values, index):
    return jnp.take_along_axis(values, index, axis=1, mode="promise_in_bounds")


def fold(values, least):
    step = values.shape[0] // 2
    while step >= least:
        values = values + pltpu.roll(values, step, 0)
        step //= 2
    return values


def panel_rows(lev_dev, fields, tiles, groups, lists, group, state, terrain, packed, scratch):
    levels = SUBLANES
    bits = (levels - 1).bit_length()
    total = jnp.zeros((tiles, LANES), jnp.int32)
    for level in range(levels):
        total = total | (terrain[pl.ds(level, tiles, stride=levels), :] << (bits * level))
    packed[...] = total
    shape = (SUBLANES, LANES)
    sub = iota(shape, 0)
    per = SUBLANES // lev_dev
    quarters = lists[0].shape[0] // 2
    for number in range(ROUNDS):
        for quarter in range(quarters):
            cells = jnp.broadcast_to(lists[number][quarter : quarter + 1, :], shape)
            high, low = cells >> LANE_BITS, cells & (LANES - 1)
            sums = [jnp.zeros(shape, jnp.float32) for _ in range(fields)]
            code = jnp.zeros(shape, jnp.int32)
            for chunk in range(tiles // per):
                here = high == chunk * per + sub // lev_dev
                for field in range(fields):
                    start = field * tiles * lev_dev + chunk * SUBLANES
                    got = gather_lanes(state[start : start + SUBLANES, :], low)
                    sums[field] = jnp.where(here, got, sums[field])
            for chunk in range(tiles // SUBLANES):
                got = gather_lanes(packed[chunk * SUBLANES : (chunk + 1) * SUBLANES, :], low)
                code = jnp.where(high == chunk * SUBLANES + sub, got, code)
            source = (fold(code, 1) >> (bits * sub)) & (levels - 1)
            section = answer_round(number, groups)
            for field in range(fields):
                both = fold(sums[field], lev_dev)
                placed = jnp.zeros(shape, jnp.float32)
                for level in range(lev_dev):
                    one = both
                    for turn in range(1, lev_dev):
                        one = jnp.where((sub - level) % lev_dev == turn, pltpu.roll(both, turn, 0), one)
                    placed = jnp.where(source == group * lev_dev + level, one, placed)
                row = ((section * fields + field) * quarters + quarter) * levels
                scratch[row : row + levels, :] = placed


def block_rows(lev_dev, fields, tiles, own, group, state, terrain, weight, scratch, mass):
    levels = SUBLANES
    coarse = weight.shape[1]
    per = LANES // coarse
    quarters = tiles // 2 // per

    def some_tiles(index, carry):
        number, quarter = index // (quarters // TOGETHER), index % (quarters // TOGETHER) * TOGETHER

        @pl.when(own[number, quarter * per] >= 0)
        def _():
            for more in range(TOGETHER):
                fill_tile(number * quarters + quarter + more, number, quarter + more)

        return carry

    def fill_tile(index, number, quarter):
        lefts, rights = [], []
        for place in range(per):
            name = own[number, quarter * per + place]
            block = jnp.maximum(name, 0)
            source = terrain[pl.ds(pl.multiple_of(block * levels, levels), levels), :]
            parts = []
            for field in range(fields):
                placed = jnp.zeros((levels, LANES), jnp.float32)
                for level in range(lev_dev):
                    line = state[pl.ds((field * tiles + block) * lev_dev + level, 1), :]
                    placed = jnp.where(source == group * lev_dev + level, line, placed)
                parts.append(placed)
            moved = jnp.concatenate(parts, axis=0)
            moved_high = moved.astype(jnp.bfloat16)
            moved_low = (moved - moved_high.astype(jnp.float32)).astype(jnp.bfloat16)
            lefts.append(
                jnp.concatenate(
                    [moved_high, moved_low, jnp.ones((2 * SUBLANES, LANES), jnp.bfloat16)], axis=0
                )
            )
            dense = jnp.where(name >= 0, weight[block], 0.0)
            dense_high = dense.astype(jnp.bfloat16)
            dense_low = (dense - dense_high.astype(jnp.float32)).astype(jnp.bfloat16)
            blank = jnp.zeros((coarse, LANES), jnp.bfloat16)
            rights.append(
                jnp.concatenate(
                    [dense_high if other == place else blank for other in range(per)]
                    + [dense_low if other == place else blank for other in range(per)],
                    axis=0,
                )
            )
        product = lax.dot_general(
            jnp.concatenate(lefts, axis=1),
            jnp.concatenate(rights, axis=1),
            (((1,), (1,)), ((), ())),
            preferred_element_type=jnp.float32,
        )
        product = product[:, :LANES] + product[:, LANES:]
        rows = fields * levels
        result = product[:rows] + product[rows : 2 * rows]
        for field in range(fields):
            row = ((number * fields + field) * quarters + quarter) * levels
            scratch[pl.ds(pl.multiple_of(row, levels), levels), :] = result[
                field * levels : (field + 1) * levels
            ]
        mass[pl.ds(index, 1), :] = product[2 * rows : 2 * rows + 1]

    lax.fori_loop(0, ROUNDS * quarters // TOGETHER, some_tiles, 0)


def produce_kernel(lev_dev, fields, partners, groups, own_ref, *refs):
    lists, state, terrain, weight = refs[:3], refs[3], refs[4], refs[5]
    parts = refs[6 : 6 + partners]
    mass, scratch, packed, own, sem = refs[6 + partners :]
    copy = pltpu.make_async_copy(own_ref, own, sem)
    copy.start()
    tiles = terrain.shape[0] // SUBLANES
    side, group = lax.axis_index("side"), lax.axis_index("lev")

    @pl.when(side == 0)
    def _():
        mass[...] = jnp.zeros_like(mass)
        panel_rows(lev_dev, fields, tiles, groups, lists, group, state, terrain, packed, scratch)
        copy.wait()

    @pl.when(side == 1)
    def _():
        copy.wait()
        block_rows(lev_dev, fields, tiles, own, group, state, terrain, weight, scratch, mass)

    rows = scratch.shape[0] // SUBLANES
    for distance in range(partners):
        target = group ^ distance
        for level in range(lev_dev):
            parts[distance][level * rows : (level + 1) * rows, :] = scratch[
                pl.ds(target * lev_dev + level, rows, stride=SUBLANES), :
            ]


def sum_kernel(lev_dev, fields, partners, *refs):
    parts, mass, sections = refs[:partners], refs[partners], refs[partners + 1 :]
    total = parts[0][...]
    for part in parts[1:]:
        total = total + part[...]
    rows = total.shape[0] // lev_dev
    span = rows // 3
    quarters = span // fields
    for number, section in enumerate(sections):
        for level in range(lev_dev):
            start = level * rows + number * span
            section[level * span : (level + 1) * span, :] = total[start : start + span]
        section[lev_dev * span : lev_dev * span + quarters, :] = mass[
            number * quarters : (number + 1) * quarters, :
        ]
        tail = lev_dev * span + quarters
        section[tail:, :] = jnp.zeros((section.shape[0] - tail, LANES), jnp.float32)


def place_panel(lev_dev, fields, number, fresh, section, slots, found):
    shape = (SUBLANES, LANES)
    sub = iota(shape, 0)
    panel_tiles = slots.shape[0]
    quarters = panel_tiles // 2
    chunks = lev_dev * fields * quarters // SUBLANES
    for tile in range(panel_tiles):
        place = jnp.broadcast_to(slots[tile : tile + 1, :], shape)
        here = place >> LANE_BITS == number * quarters + sub % quarters
        low = place & (LANES - 1)
        for chunk in range(chunks):
            got = gather_lanes(section[chunk * SUBLANES : (chunk + 1) * SUBLANES, :], low)
            row = (tile * chunks + chunk) * SUBLANES
            before = 0.0 if fresh else found[row : row + SUBLANES, :]
            found[row : row + SUBLANES, :] = jnp.where(here, got, before)


def place_blocks(coarse, number, section, page, spread_high, spread_low):
    shape = (SUBLANES, LANES)
    lane, sub = iota(shape, 1), iota(shape, 0)
    quarters = page.shape[0] // 2
    kinds = spread_high.shape[1] // LANES
    runs = jnp.broadcast_to(page[quarters : quarters + 1, :], shape)
    indices, heres = [], []
    for quarter in range(quarters):
        run = jnp.where(lane == quarter * SUBLANES + sub, runs, 0)
        run = jnp.broadcast_to(jnp.sum(run, axis=1, keepdims=True), shape)
        shift = lane - (run & (LANES // coarse - 1)) * coarse
        indices.append((shift + sub * coarse) & (LANES - 1))
        heres.append((shift >= 0) & (shift < coarse) & (run >= 0))
    for pair in range(0, quarters, 2):
        for kind in range(kinds):
            both = []
            for quarter in (pair, pair + 1):
                row = kind * quarters + quarter
                line = jnp.broadcast_to(section[row : row + 1, :], shape)
                both.append(jnp.where(heres[quarter], gather_lanes(line, indices[quarter]), 0.0))
            both = jnp.concatenate(both, axis=0)
            high = both.astype(jnp.bfloat16)
            start = (number * quarters + pair) * SUBLANES
            here = (slice(start, start + 2 * SUBLANES), slice(kind * LANES, (kind + 1) * LANES))
            spread_high[here] = high
            spread_low[here] = (both - high.astype(jnp.float32)).astype(jnp.bfloat16)


def place_kernel(lev_dev, fields, coarse, groups, number, fresh, section, page, slots, *refs):
    spread_high, spread_low, found = refs[-3:]
    side = lax.axis_index("side")

    @pl.when(side == 0)
    def _():
        place_blocks(coarse, number, section, page, spread_high, spread_low)

    @pl.when(side == 1)
    def _():
        place_panel(lev_dev, fields, answer_round(number, groups), fresh, section, slots, found)


def finish_panel(lev_dev, fields, tiles, panel_tiles, found, state, staged, send):
    shape = (SUBLANES, LANES)
    sub = iota(shape, 0)
    quarters = panel_tiles // 2
    chunks = lev_dev * fields * quarters // SUBLANES
    share = SUBLANES // quarters
    rows = tiles * lev_dev
    for field in range(fields):
        start = field * rows
        part = field % share
        for tile in range(panel_tiles):
            for level in range(lev_dev):
                chunk = (level * fields + field) // share
                row = (tile * chunks + chunk) * SUBLANES
                rim = jnp.sum(
                    jnp.where(sub // quarters == part, found[row : row + SUBLANES, :], 0.0),
                    axis=0,
                    keepdims=True,
                )
                row = start + tile * lev_dev + level
                staged[row : row + 1, :] = 0.5 * (state[row : row + 1, :] + rim)
        rest = start + panel_tiles * lev_dev
        staged[rest : start + rows, :] = state[rest : start + rows, :]
        send(field)


def finish_coarse(lev_dev, fields, tiles, coarse, pages, spread_high, spread_low, state, staged, send):
    quarters = pages[0].shape[0] // 2
    width = quarters * SUBLANES
    shift = (LANES // coarse).bit_length() - 1
    tile = iota((tiles, LANES), 0)
    lane = iota((1, LANES), 1)
    runs = jnp.full((1, LANES), -1, jnp.int32)
    for number, page in enumerate(pages):
        turned = page[quarters : quarters + 1, :]
        if number:
            turned = pltpu.roll(jnp.broadcast_to(turned, (SUBLANES, LANES)), number * width, 1)[0:1]
        runs = jnp.where(lane // width == number, turned, runs)
    lands = (tile == jnp.broadcast_to(runs >> shift, tile.shape)).astype(jnp.bfloat16)
    lands = lands[:, : ROUNDS * width]

    def landed(kind):
        here = (slice(None), slice(kind * LANES, (kind + 1) * LANES))
        high = jnp.dot(lands, spread_high[here], preferred_element_type=jnp.float32)
        return high + jnp.dot(lands, spread_low[here], preferred_element_type=jnp.float32)

    scale = 1.0 / (1.0 + landed(lev_dev * fields))
    for field in range(fields):
        for level in range(lev_dev):
            here = pl.ds(field * tiles * lev_dev + level, tiles, stride=lev_dev)
            staged[here, :] = (state[here, :] + landed(level * fields + field)) * scale
        send(field)


def finish_kernel(lev_dev, fields, coarse, groups, number, section, *refs):
    pages, slots, kept, state = refs[:3], refs[3], refs[4:7], refs[7]
    out, spread_high, spread_low, found, staged, sems = refs[8:]
    tiles = state.shape[0] // (fields * lev_dev)
    rows = tiles * lev_dev
    copies = [
        pltpu.make_async_copy(
            staged.at[field * rows : (field + 1) * rows],
            out.at[field * rows : (field + 1) * rows],
            sems.at[field],
        )
        for field in range(fields)
    ]
    side = lax.axis_index("side")

    def send(field):
        copies[field].start()

    @pl.when(side == 0)
    def _():
        spread_high[...] = kept[0][...]
        spread_low[...] = kept[1][...]
        place_blocks(coarse, number, section, pages[number], spread_high, spread_low)
        finish_coarse(
            lev_dev, fields, tiles, coarse, pages, spread_high, spread_low, state, staged, send
        )

    @pl.when(side == 1)
    def _():
        found[...] = kept[2][...]
        place_panel(lev_dev, fields, answer_round(number, groups), False, section, slots, found)
        finish_panel(lev_dev, fields, tiles, slots.shape[0], found, state, staged, send)

    for copy in copies:
        copy.wait()


def specs(*spaces):
    return [pl.BlockSpec(memory_space=space) for space in spaces]


def params():
    return pltpu.CompilerParams(vmem_limit_bytes=16 * 1024 * 1024)


def in_hbm(value):
    return pltpu.with_memory_space_constraint(value, pltpu.HBM)


def struct(shape, dtype=jnp.float32):
    return jax.ShapeDtypeStruct(shape, dtype)


def on_device(
    model_state, terrain_level, panel_owner, panel_cell, block_weight, block_owner, block_row
):
    groups, partners = lax.axis_size("grid"), lax.axis_size("lev")
    sides = lax.axis_size("side")
    _, lev_dev, fields, cell_dev = model_state.shape
    levels = terrain_level.shape[1]
    tiles = cell_dev // LANES
    blocks, coarse, _ = block_weight.shape
    panel_tiles = panel_cell.shape[0] // LANES
    quarters = panel_tiles // 2
    state = (
        model_state.reshape(lev_dev, fields, tiles, LANES)
        .transpose(1, 2, 0, 3)
        .reshape(fields * tiles * lev_dev, LANES)
    )
    terrain = (
        terrain_level.reshape(levels, tiles, LANES).transpose(1, 0, 2).reshape(tiles * levels, LANES)
    )
    message = struct((MESSAGE_ROWS, LANES), jnp.int32)
    page = struct((panel_tiles, LANES), jnp.int32)
    first, second, own, slots, state, terrain, weight = pl.pallas_call(
        functools.partial(list_kernel, groups),
        out_shape=[message] * 3
        + [page]
        + [struct(state.shape), struct(terrain.shape, jnp.int32), struct(block_weight.shape)],
        in_specs=specs(*[VMEM] * 3, *[pl.ANY] * 4),
        out_specs=specs(*[VMEM] * 7),
        scratch_shapes=[
            VMEM(page.shape, jnp.int32),
            VMEM((SUBLANES, LANES), jnp.int32),
            VMEM((SUBLANES, LANES), jnp.int32),
            pltpu.SemaphoreType.DMA((4,)),
        ],
        compiler_params=params(),
        name="lists",
    )(
        panel_owner.reshape(page.shape),
        block_owner.reshape(1, blocks),
        block_row.reshape(1, blocks),
        panel_cell.reshape(page.shape),
        in_hbm(state),
        in_hbm(terrain),
        in_hbm(block_weight),
    )

    def towards(number_of, cross):
        return [
            (tile * sides + side, partner_of(tile, number_of(side), groups) * sides + (side ^ cross))
            for tile in range(groups)
            for side in range(sides)
        ]

    first = lax.ppermute(first, ("grid", "side"), towards(lambda side: 2 * side, 0))
    second = lax.ppermute(second, ("grid", "side"), towards(lambda side: 1, 0))
    third = lax.ppermute(first, "side", [(0, 1), (1, 0)])
    lists = [first, second, third]
    scratch_rows = ROUNDS * fields * quarters
    part = struct((lev_dev * scratch_rows, LANES))
    *parts, mass = pl.pallas_call(
        functools.partial(produce_kernel, lev_dev, fields, partners, groups),
        out_shape=[part] * partners + [struct((2 * SUBLANES, LANES))],
        in_specs=specs(*[VMEM] * 7),
        out_specs=specs(*[VMEM] * (partners + 1)),
        scratch_shapes=[
            VMEM((scratch_rows * SUBLANES, LANES), jnp.float32),
            VMEM((tiles, LANES), jnp.int32),
            SMEM((MESSAGE_ROWS, LANES), jnp.int32),
            pltpu.SemaphoreType.DMA,
        ],
        compiler_params=params(),
        name="produce",
    )(own, *lists, state, terrain, weight)
    arrived = [parts[0]] + [
        lax.ppermute(parts[distance], "lev", [(rank, rank ^ distance) for rank in range(partners)])
        for distance in range(partners - 1, 0, -1)
    ]
    section_rows = HELD_ROWS * quarters
    sections = pl.pallas_call(
        functools.partial(sum_kernel, lev_dev, fields, partners),
        out_shape=[struct((section_rows, LANES))] * 3,
        in_specs=specs(*[VMEM] * (partners + 1)),
        out_specs=specs(*[VMEM] * 3),
        compiler_params=params(),
        name="sections",
    )(*arrived, mass)
    sections = [
        lax.ppermute(sections[number], ("grid", "side"), towards(lambda side: number, 1))
        for number in range(ROUNDS - 1, -1, -1)
    ][::-1]
    kinds = lev_dev * fields + 1
    spread = struct((ROUNDS * quarters * SUBLANES, kinds * LANES), jnp.bfloat16)
    kept = [spread, spread, struct((panel_tiles * lev_dev * fields * quarters, LANES))]
    sizes = (lev_dev, fields, coarse, groups)
    held = []
    for number in range(ROUNDS - 1, 0, -1):
        held = pl.pallas_call(
            functools.partial(place_kernel, *sizes, number, not held),
            out_shape=kept,
            in_specs=specs(*[VMEM] * (3 + len(held))),
            out_specs=specs(*[VMEM] * 3),
            input_output_aliases={3 + index: index for index in range(len(held))},
            compiler_params=params(),
            name="place",
        )(sections[number], lists[number], slots, *held)
    result = pl.pallas_call(
        functools.partial(finish_kernel, *sizes, 0),
        out_shape=pltpu.HBM(state.shape, jnp.float32),
        in_specs=specs(*[VMEM] * 9),
        out_specs=pl.BlockSpec(memory_space=pltpu.HBM),
        scratch_shapes=[VMEM(one.shape, one.dtype) for one in kept]
        + [VMEM(state.shape, jnp.float32), pltpu.SemaphoreType.DMA((fields,))],
        compiler_params=params(),
        name="finish",
    )(sections[0], *lists, slots, *held, state)
    return (
        result.reshape(fields, tiles, lev_dev, LANES)
        .transpose(2, 0, 1, 3)
        .reshape(1, lev_dev, fields, cell_dev)
    )


def solution(mesh):
    in_specs = (
        P("side", "lev", None, "grid"),
        P("side", None, "grid"),
        P("grid", None),
        P("grid"),
        P("grid", None, None),
        P("grid", None),
        P("grid"),
    )
    out_specs = P("side", "lev", None, "grid")
    return jax.shard_map(
        on_device, mesh=mesh, in_specs=in_specs, out_specs=out_specs, check_vma=False
    )
```

```python
import functools

import jax
import jax.numpy as jnp
from jax import lax
from jax.experimental import pallas as pl
from jax.experimental.pallas import tpu as pltpu
from jax.sharding import PartitionSpec as P

LANES = 128
LANE_BITS = 7
SUBLANES = 8
VALUE_BITS = 24
ROW_BITS = 16
SECTION_ORDER = (2, 0, 1)
HELD_ROWS = 16
ROUNDS = 3
TOGETHER = 2
VMEM = pltpu.VMEM
SMEM = pltpu.SMEM


def partner_of(tile, number, groups):
    if groups == ROUNDS + 1:
        return tile ^ (number + 1)
    return (tile + (groups - 1, 1, groups // 2)[number]) % groups


def answer_round(number, groups):
    return number if groups == ROUNDS + 1 else (1, 0, 2)[number]


def iota(shape, dimension):
    return lax.broadcasted_iota(jnp.int32, shape, dimension)


def gather_lanes(values, index):
    return jnp.take_along_axis(values, index, axis=1, mode="promise_in_bounds")


def compact(hits, values, pages):
    rows, lanes = hits[0].shape
    shape = (rows, lanes)
    lane, row = iota(shape, 1), iota(shape, 0)
    ones, above = [], []
    for hit in hits:
        one = hit.astype(jnp.int32)
        upper = one
        step = 1
        while step < rows:
            upper = upper + jnp.where(row >= step, pltpu.roll(upper, step, 0), 0)
            step *= 2
        ones.append(one.astype(jnp.float32))
        above.append((upper - one).astype(jnp.float32))
    blank = [jnp.zeros(shape, jnp.float32)] * (-len(hits) % 2)
    left = jnp.concatenate(ones + blank + above + blank, axis=0).astype(jnp.bfloat16)
    square = (lanes, lanes)
    earlier = (iota(square, 0) < iota(square, 1)).astype(jnp.bfloat16)
    right = jnp.concatenate([earlier, jnp.ones(square, jnp.bfloat16)], axis=1)
    sums = jnp.dot(left, right, preferred_element_type=jnp.float32).astype(jnp.int32)
    results, places = [], []
    for number, hit in enumerate(hits):
        start = number * rows
        rank, count = sums[start : start + rows, :lanes], sums[start : start + rows, lanes:]
        start += (len(hits) + len(blank)) * rows
        before = sums[start : start + rows, lanes:]
        held = jnp.where(hit, ((lane - rank) << VALUE_BITS) | values, -1)
        bit = 0
        while 1 << bit < lanes:
            coming = pltpu.roll(held, lanes - (1 << bit), 1)
            comes = (coming >= 0) & ((coming >> (VALUE_BITS + bit)) & 1 == 1)
            stays = (held >= 0) & ((held >> (VALUE_BITS + bit)) & 1 == 0)
            held = jnp.where(comes, coming, jnp.where(stays, held, -1))
            bit += 1
        held = held & ((1 << VALUE_BITS) - 1)
        lines = []
        for page in range(pages):
            offset = page * lanes + lane - before
            inside = (offset >= 0) & (offset < count)
            got = jnp.where(inside, gather_lanes(held, offset & (lanes - 1)), 0)
            lines.append(jnp.sum(got, axis=0, keepdims=True))
        results.append(lines)
        places.append(rank + before)
    return results, places


def list_kernel(groups, owner_any, cell_any, first, second, slot_ref, owner_ref, cell_ref, sems):
    copies = [
        pltpu.make_async_copy(source, target, sems.at[index])
        for index, (source, target) in enumerate(((owner_any, owner_ref), (cell_any, cell_ref)))
    ]
    for copy in copies:
        copy.start()
    tile, side = lax.axis_index("grid"), lax.axis_index("side")
    for copy in copies:
        copy.wait()
    owners = owner_ref[...]
    half = owners.shape[0] // 2
    hits = [owners == partner_of(tile, number, groups) for number in range(ROUNDS)]
    pages, ranks = compact(hits, cell_ref[...], half)
    slots = jnp.zeros_like(owners)
    for number, (hit, rank) in enumerate(zip(hits, ranks)):
        slots = jnp.where(hit, number * half * LANES + rank, slots)
    slot_ref[...] = slots
    for target, here, there in ((first, 0, 2), (second, 1, 1)):
        target[...] = jnp.zeros(target.shape, jnp.int32)
        for line in range(half):
            target[line : line + 1, :] = jnp.where(side == 0, pages[here][line], pages[there][line])


def fold(values, least):
    step = values.shape[0] // 2
    while step >= least:
        values = values + pltpu.roll(values, step, 0)
        step //= 2
    return values


def panel_rows(lev_dev, fields, tiles, groups, lists, group, state, packed, scratch):
    levels = SUBLANES
    bits = (levels - 1).bit_length()
    shape = (SUBLANES, LANES)
    sub = iota(shape, 0)
    per = SUBLANES // lev_dev
    quarters = lists[0].shape[0] // 2
    for number in range(ROUNDS):
        for quarter in range(quarters):
            cells = jnp.broadcast_to(lists[number][quarter : quarter + 1, :], shape)
            high, low = cells >> LANE_BITS, cells & (LANES - 1)
            sums = [jnp.zeros(shape, jnp.float32) for _ in range(fields)]
            code = jnp.zeros(shape, jnp.int32)
            for chunk in range(tiles // per):
                here = high == chunk * per + sub // lev_dev
                for field in range(fields):
                    start = field * tiles * lev_dev + chunk * SUBLANES
                    got = gather_lanes(state[start : start + SUBLANES, :], low)
                    sums[field] = jnp.where(here, got, sums[field])
            for chunk in range(tiles // SUBLANES):
                got = gather_lanes(packed[chunk * SUBLANES : (chunk + 1) * SUBLANES, :], low)
                code = jnp.where(high == chunk * SUBLANES + sub, got, code)
            source = (fold(code, 1) >> (bits * sub)) & (levels - 1)
            section = answer_round(number, groups)
            for field in range(fields):
                both = fold(sums[field], lev_dev)
                placed = jnp.zeros(shape, jnp.float32)
                for level in range(lev_dev):
                    one = both
                    for turn in range(1, lev_dev):
                        one = jnp.where((sub - level) % lev_dev == turn, pltpu.roll(both, turn, 0), one)
                    placed = jnp.where(source == group * lev_dev + level, one, placed)
                row = ((section * fields + field) * quarters + quarter) * levels
                scratch[row : row + levels, :] = placed


def block_rows(lev_dev, fields, tiles, own, group, state, terrain, weight, scratch, mass):
    levels = SUBLANES
    coarse = weight.shape[1]
    per = LANES // coarse
    quarters = tiles // 2 // per

    def some_tiles(index, carry):
        number, quarter = index // (quarters // TOGETHER), index % (quarters // TOGETHER) * TOGETHER

        @pl.when(own[number, quarter * per] >= 0)
        def _():
            for more in range(TOGETHER):
                fill_tile(number * quarters + quarter + more, number, quarter + more)

        return carry

    def fill_tile(index, number, quarter):
        lefts, rights = [], []
        for place in range(per):
            name = own[number, quarter * per + place]
            block = jnp.maximum(name, 0)
            source = terrain[pl.ds(pl.multiple_of(block * levels, levels), levels), :]
            parts = []
            for field in range(fields):
                placed = jnp.zeros((levels, LANES), jnp.float32)
                for level in range(lev_dev):
                    line = state[pl.ds((field * tiles + block) * lev_dev + level, 1), :]
                    placed = jnp.where(source == group * lev_dev + level, line, placed)
                parts.append(placed)
            moved = jnp.concatenate(parts, axis=0)
            moved_high = moved.astype(jnp.bfloat16)
            moved_low = (moved - moved_high.astype(jnp.float32)).astype(jnp.bfloat16)
            lefts.append(
                jnp.concatenate(
                    [moved_high, moved_low, jnp.ones((2 * SUBLANES, LANES), jnp.bfloat16)], axis=0
                )
            )
            dense = jnp.where(name >= 0, weight[block], 0.0)
            dense_high = dense.astype(jnp.bfloat16)
            dense_low = (dense - dense_high.astype(jnp.float32)).astype(jnp.bfloat16)
            blank = jnp.zeros((coarse, LANES), jnp.bfloat16)
            rights.append(
                jnp.concatenate(
                    [dense_high if other == place else blank for other in range(per)]
                    + [dense_low if other == place else blank for other in range(per)],
                    axis=0,
                )
            )
        product = lax.dot_general(
            jnp.concatenate(lefts, axis=1),
            jnp.concatenate(rights, axis=1),
            (((1,), (1,)), ((), ())),
            preferred_element_type=jnp.float32,
        )
        product = product[:, :LANES] + product[:, LANES:]
        rows = fields * levels
        result = product[:rows] + product[rows : 2 * rows]
        for field in range(fields):
            row = ((number * fields + field) * quarters + quarter) * levels
            scratch[pl.ds(pl.multiple_of(row, levels), levels), :] = result[
                field * levels : (field + 1) * levels
            ]
        mass[pl.ds(index, 1), :] = product[2 * rows : 2 * rows + 1]

    lax.fori_loop(0, ROUNDS * quarters // TOGETHER, some_tiles, 0)


def prepare_kernel(lev_dev, fields, groups, block_owner, block_row, *refs):
    sources, (state, packed, table, facts) = refs[:3], refs[3:7]
    terrain, weight, owner_pad, row_pad, own_page, own, sems = refs[7:]
    state_copy, terrain_copy, weight_copy = [
        pltpu.make_async_copy(source, target, sems.at[index])
        for index, (source, target) in enumerate(zip(sources, (state, terrain, weight)))
    ]
    own_copy = pltpu.make_async_copy(own_page, own, sems.at[3])
    tile, side, group = lax.axis_index("grid"), lax.axis_index("side"), lax.axis_index("lev")
    tiles = packed.shape[0]
    terrain_copy.start()
    state_copy.start()

    @pl.when(side == 0)
    def _():
        levels = SUBLANES
        bits = (levels - 1).bit_length()
        terrain_copy.wait()
        total = jnp.zeros((tiles, LANES), jnp.int32)
        for level in range(levels):
            total = total | (terrain[pl.ds(level, tiles, stride=levels), :] << (bits * level))
        packed[...] = total
        state_copy.wait()

    @pl.when(side == 1)
    def _():
        weight_copy.start()
        blocks = block_owner.shape[1]
        owner_pad[...] = jnp.full(owner_pad.shape, -1, jnp.int32)
        row_pad[...] = jnp.zeros(row_pad.shape, jnp.int32)
        owner_pad[0:1, 0:blocks] = block_owner[...]
        row_pad[0:1, 0:blocks] = block_row[...]
        owners = owner_pad[...]
        hits = [owners == partner_of(tile, number, groups) for number in range(ROUNDS)]
        marked = ((iota(owners.shape, 1) + 1) << ROW_BITS) | row_pad[...]
        pages, _ = compact(hits, marked, 1)
        own_page[...] = jnp.zeros(own_page.shape, jnp.int32)
        count = facts.shape[0] - SUBLANES
        facts[count:, :] = jnp.zeros((SUBLANES, LANES), jnp.float32)
        for number, (line,) in enumerate(pages):
            name = line >> ROW_BITS
            own_page[number : number + 1, :] = name - 1
            run = jnp.where(name > 0, line & ((1 << ROW_BITS) - 1), -1)
            facts[count + number : count + number + 1, :] = run.astype(jnp.float32)
        own_copy.start()
        own_copy.wait()
        terrain_copy.wait()
        state_copy.wait()
        weight_copy.wait()
        block_rows(lev_dev, fields, tiles, own, group, state, terrain, weight, table, facts)


def produce_kernel(lev_dev, fields, partners, groups, *refs):
    lists, state, packed, table = refs[:3], refs[3], refs[4], refs[5]
    parts, scratch = refs[6 : 6 + partners], refs[6 + partners]
    tiles = packed.shape[0]
    side, group = lax.axis_index("side"), lax.axis_index("lev")

    def emit(source):
        rows = source.shape[0] // SUBLANES
        for distance in range(partners):
            target = group ^ distance
            for level in range(lev_dev):
                parts[distance][level * rows : (level + 1) * rows, :] = source[
                    pl.ds(target * lev_dev + level, rows, stride=SUBLANES), :
                ]

    @pl.when(side == 0)
    def _():
        panel_rows(lev_dev, fields, tiles, groups, lists, group, state, packed, scratch)
        emit(scratch)

    @pl.when(side == 1)
    def _():
        emit(table)


def sum_kernel(lev_dev, fields, partners, *refs):
    parts, facts, sections = refs[:partners], refs[partners], refs[partners + 1 :]
    total = parts[0][...]
    for part in parts[1:]:
        total = total + part[...]
    rows = total.shape[0] // lev_dev
    span = rows // ROUNDS
    quarters = span // fields
    masses = facts.shape[0] - SUBLANES
    for number, section in enumerate(sections):
        for level in range(lev_dev):
            start = level * rows + number * span
            section[level * span : (level + 1) * span, :] = total[start : start + span]
        last = lev_dev * span + quarters
        section[last - quarters : last, :] = facts[number * quarters : (number + 1) * quarters, :]
        section[last:, :] = jnp.zeros((section.shape[0] - last, LANES), jnp.float32)
        section[last : last + 1, :] = facts[masses + number : masses + number + 1, :]


def place_panel(lev_dev, fields, number, fresh, section, slots, found):
    shape = (SUBLANES, LANES)
    sub = iota(shape, 0)
    panel_tiles = slots.shape[0]
    quarters = panel_tiles // 2
    chunks = lev_dev * fields * quarters // SUBLANES
    for tile in range(panel_tiles):
        place = jnp.broadcast_to(slots[tile : tile + 1, :], shape)
        here = place >> LANE_BITS == number * quarters + sub % quarters
        low = place & (LANES - 1)
        for chunk in range(chunks):
            got = gather_lanes(section[chunk * SUBLANES : (chunk + 1) * SUBLANES, :], low)
            row = (tile * chunks + chunk) * SUBLANES
            before = 0.0 if fresh else found[row : row + SUBLANES, :]
            found[row : row + SUBLANES, :] = jnp.where(here, got, before)


def runs_of(section, quarters, kinds):
    row = quarters * kinds
    return section[row : row + 1, :].astype(jnp.int32)


def place_blocks(coarse, quarters, number, section, spread_high, spread_low):
    shape = (SUBLANES, LANES)
    lane, sub = iota(shape, 1), iota(shape, 0)
    kinds = spread_high.shape[1] // LANES
    runs = jnp.broadcast_to(runs_of(section, quarters, kinds), shape)
    indices, heres = [], []
    for quarter in range(quarters):
        run = jnp.where(lane == quarter * SUBLANES + sub, runs, 0)
        run = jnp.broadcast_to(jnp.sum(run, axis=1, keepdims=True), shape)
        shift = lane - (run & (LANES // coarse - 1)) * coarse
        indices.append((shift + sub * coarse) & (LANES - 1))
        heres.append((shift >= 0) & (shift < coarse) & (run >= 0))
    for pair in range(0, quarters, 2):
        for kind in range(kinds):
            both = []
            for quarter in (pair, pair + 1):
                row = kind * quarters + quarter
                line = jnp.broadcast_to(section[row : row + 1, :], shape)
                both.append(jnp.where(heres[quarter], gather_lanes(line, indices[quarter]), 0.0))
            both = jnp.concatenate(both, axis=0)
            high = both.astype(jnp.bfloat16)
            start = (number * quarters + pair) * SUBLANES
            here = (slice(start, start + 2 * SUBLANES), slice(kind * LANES, (kind + 1) * LANES))
            spread_high[here] = high
            spread_low[here] = (both - high.astype(jnp.float32)).astype(jnp.bfloat16)


def place_kernel(lev_dev, fields, coarse, groups, number, fresh, section, slots, *refs):
    spread_high, spread_low, found = refs[-3:]
    side = lax.axis_index("side")

    @pl.when(side == 0)
    def _():
        place_blocks(coarse, slots.shape[0] // 2, number, section, spread_high, spread_low)

    @pl.when(side == 1)
    def _():
        place_panel(lev_dev, fields, answer_round(number, groups), fresh, section, slots, found)


def finish_panel(lev_dev, fields, tiles, panel_tiles, found, state, staged, send):
    shape = (SUBLANES, LANES)
    sub = iota(shape, 0)
    quarters = panel_tiles // 2
    chunks = lev_dev * fields * quarters // SUBLANES
    share = SUBLANES // quarters
    rows = tiles * lev_dev
    for field in range(fields):
        start = field * rows
        part = field % share
        for tile in range(panel_tiles):
            for level in range(lev_dev):
                chunk = (level * fields + field) // share
                row = (tile * chunks + chunk) * SUBLANES
                rim = jnp.sum(
                    jnp.where(sub // quarters == part, found[row : row + SUBLANES, :], 0.0),
                    axis=0,
                    keepdims=True,
                )
                row = start + tile * lev_dev + level
                staged[row : row + 1, :] = 0.5 * (state[row : row + 1, :] + rim)
        rest = start + panel_tiles * lev_dev
        staged[rest : start + rows, :] = state[rest : start + rows, :]
        send(field)


def finish_coarse(
    lev_dev, fields, tiles, coarse, quarters, sections, spread_high, spread_low, state, staged, send
):
    width = quarters * SUBLANES
    shift = (LANES // coarse).bit_length() - 1
    tile = iota((tiles, LANES), 0)
    lane = iota((1, LANES), 1)
    runs = jnp.full((1, LANES), -1, jnp.int32)
    for number, section in enumerate(sections):
        turned = runs_of(section, quarters, lev_dev * fields + 1)
        if number:
            turned = pltpu.roll(jnp.broadcast_to(turned, (SUBLANES, LANES)), number * width, 1)[0:1]
        runs = jnp.where(lane // width == number, turned, runs)
    lands = (tile == jnp.broadcast_to(runs >> shift, tile.shape)).astype(jnp.bfloat16)
    lands = lands[:, : ROUNDS * width]

    def landed(kind):
        here = (slice(None), slice(kind * LANES, (kind + 1) * LANES))
        high = jnp.dot(lands, spread_high[here], preferred_element_type=jnp.float32)
        return high + jnp.dot(lands, spread_low[here], preferred_element_type=jnp.float32)

    scale = 1.0 / (1.0 + landed(lev_dev * fields))
    for field in range(fields):
        for level in range(lev_dev):
            here = pl.ds(field * tiles * lev_dev + level, tiles, stride=lev_dev)
            staged[here, :] = (state[here, :] + landed(level * fields + field)) * scale
        send(field)


def finish_kernel(lev_dev, fields, coarse, groups, number, *refs):
    sections, slots, kept, state = refs[:3], refs[3], refs[4:7], refs[7]
    out, spread_high, spread_low, found, staged, sems = refs[8:]
    quarters = slots.shape[0] // 2
    tiles = state.shape[0] // (fields * lev_dev)
    rows = tiles * lev_dev
    copies = [
        pltpu.make_async_copy(
            staged.at[field * rows : (field + 1) * rows],
            out.at[field * rows : (field + 1) * rows],
            sems.at[field],
        )
        for field in range(fields)
    ]
    side = lax.axis_index("side")

    def send(field):
        copies[field].start()

    @pl.when(side == 0)
    def _():
        spread_high[...] = kept[0][...]
        spread_low[...] = kept[1][...]
        place_blocks(coarse, quarters, number, sections[number], spread_high, spread_low)
        finish_coarse(
            lev_dev, fields, tiles, coarse, quarters, sections, spread_high, spread_low, state, staged, send
        )

    @pl.when(side == 1)
    def _():
        found[...] = kept[2][...]
        place_panel(lev_dev, fields, answer_round(number, groups), False, sections[number], slots, found)
        finish_panel(lev_dev, fields, tiles, slots.shape[0], found, state, staged, send)

    for copy in copies:
        copy.wait()


def specs(*spaces):
    return [pl.BlockSpec(memory_space=space) for space in spaces]


def params():
    return pltpu.CompilerParams(vmem_limit_bytes=16 * 1024 * 1024)


def in_hbm(value):
    return pltpu.with_memory_space_constraint(value, pltpu.HBM)


def struct(shape, dtype=jnp.float32):
    return jax.ShapeDtypeStruct(shape, dtype)


def on_device(
    model_state, terrain_level, panel_owner, panel_cell, block_weight, block_owner, block_row
):
    groups, partners = lax.axis_size("grid"), lax.axis_size("lev")
    sides = lax.axis_size("side")
    _, lev_dev, fields, cell_dev = model_state.shape
    levels = terrain_level.shape[1]
    tiles = cell_dev // LANES
    blocks, coarse, _ = block_weight.shape
    panel_tiles = panel_cell.shape[0] // LANES
    quarters = panel_tiles // 2
    state = (
        model_state.reshape(lev_dev, fields, tiles, LANES)
        .transpose(1, 2, 0, 3)
        .reshape(fields * tiles * lev_dev, LANES)
    )
    terrain = (
        terrain_level.reshape(levels, tiles, LANES).transpose(1, 0, 2).reshape(tiles * levels, LANES)
    )
    page = struct((panel_tiles, LANES), jnp.int32)
    first, second, slots = pl.pallas_call(
        functools.partial(list_kernel, groups),
        out_shape=[page] * 3,
        in_specs=specs(*[pl.ANY] * 2),
        out_specs=specs(*[VMEM] * 3),
        scratch_shapes=[
            VMEM(page.shape, jnp.int32),
            VMEM(page.shape, jnp.int32),
            pltpu.SemaphoreType.DMA((2,)),
        ],
        compiler_params=params(),
        name="lists",
    )(in_hbm(panel_owner.reshape(page.shape)), in_hbm(panel_cell.reshape(page.shape)))

    def towards(number_of, cross):
        return [
            (tile * sides + side, partner_of(tile, number_of(side), groups) * sides + (side ^ cross))
            for tile in range(groups)
            for side in range(sides)
        ]

    first = lax.ppermute(first, ("grid", "side"), towards(lambda side: 2 * side, 0))
    second = lax.ppermute(second, ("grid", "side"), towards(lambda side: 1, 0))
    third = lax.ppermute(first, "side", [(0, 1), (1, 0)])
    lists = [first, second, third]
    scratch_rows = ROUNDS * fields * quarters
    table_shape = (scratch_rows * SUBLANES, LANES)
    state, packed, table, facts = pl.pallas_call(
        functools.partial(prepare_kernel, lev_dev, fields, groups),
        out_shape=[
            struct(state.shape),
            struct((tiles, LANES), jnp.int32),
            struct(table_shape),
            struct((ROUNDS * quarters + SUBLANES, LANES)),
        ],
        in_specs=specs(*[VMEM] * 2, *[pl.ANY] * 3),
        out_specs=specs(*[VMEM] * 4),
        scratch_shapes=[
            VMEM(terrain.shape, jnp.int32),
            VMEM(block_weight.shape, jnp.float32),
            *[VMEM((SUBLANES, LANES), jnp.int32)] * 3,
            SMEM((SUBLANES, LANES), jnp.int32),
            pltpu.SemaphoreType.DMA((4,)),
        ],
        cost_estimate=pl.CostEstimate(flops=0, bytes_accessed=8_000_000, transcendentals=0),
        compiler_params=params(),
        name="prepare",
    )(
        block_owner.reshape(1, blocks),
        block_row.reshape(1, blocks),
        in_hbm(state),
        in_hbm(terrain),
        in_hbm(block_weight),
    )
    part = struct((lev_dev * scratch_rows, LANES))
    parts = pl.pallas_call(
        functools.partial(produce_kernel, lev_dev, fields, partners, groups),
        out_shape=[part] * partners,
        in_specs=specs(*[VMEM] * 6),
        out_specs=specs(*[VMEM] * partners),
        scratch_shapes=[VMEM(table_shape, jnp.float32)],
        compiler_params=params(),
        name="produce",
    )(*lists, state, packed, table)
    arrived = [parts[0]] + [
        lax.ppermute(parts[distance], "lev", [(rank, rank ^ distance) for rank in range(partners)])
        for distance in range(partners - 1, 0, -1)
    ]
    section_rows = HELD_ROWS * quarters
    sections = pl.pallas_call(
        functools.partial(sum_kernel, lev_dev, fields, partners),
        out_shape=[struct((section_rows, LANES))] * 3,
        in_specs=specs(*[VMEM] * (partners + 1)),
        out_specs=specs(*[VMEM] * 3),
        compiler_params=params(),
        name="sections",
    )(*arrived, facts)
    sections = [
        lax.ppermute(sections[number], ("grid", "side"), towards(lambda side: number, 1))
        for number in SECTION_ORDER
    ]
    sections = [sections[SECTION_ORDER.index(number)] for number in range(ROUNDS)]
    kinds = lev_dev * fields + 1
    spread = struct((ROUNDS * quarters * SUBLANES, kinds * LANES), jnp.bfloat16)
    kept = [spread, spread, struct((panel_tiles * lev_dev * fields * quarters, LANES))]
    sizes = (lev_dev, fields, coarse, groups)
    held = []
    for number in SECTION_ORDER[:-1]:
        held = pl.pallas_call(
            functools.partial(place_kernel, *sizes, number, not held),
            out_shape=kept,
            in_specs=specs(*[VMEM] * (2 + len(held))),
            out_specs=specs(*[VMEM] * 3),
            input_output_aliases={2 + index: index for index in range(len(held))},
            compiler_params=params(),
            name="place",
        )(sections[number], slots, *held)
    result = pl.pallas_call(
        functools.partial(finish_kernel, *sizes, SECTION_ORDER[-1]),
        out_shape=pltpu.HBM(state.shape, jnp.float32),
        in_specs=specs(*[VMEM] * 8),
        out_specs=pl.BlockSpec(memory_space=pltpu.HBM),
        scratch_shapes=[VMEM(one.shape, one.dtype) for one in kept]
        + [VMEM(state.shape, jnp.float32), pltpu.SemaphoreType.DMA((fields,))],
        compiler_params=params(),
        name="finish",
    )(*sections, slots, *held, state)
    return (
        result.reshape(fields, tiles, lev_dev, LANES)
        .transpose(2, 0, 1, 3)
        .reshape(1, lev_dev, fields, cell_dev)
    )


def solution(mesh):
    in_specs = (
        P("side", "lev", None, "grid"),
        P("side", None, "grid"),
        P("grid", None),
        P("grid"),
        P("grid", None, None),
        P("grid", None),
        P("grid"),
    )
    out_specs = P("side", "lev", None, "grid")
    return jax.shard_map(
        on_device, mesh=mesh, in_specs=in_specs, out_specs=out_specs, check_vma=False
    )
```

```python
import functools

import jax
import jax.numpy as jnp
from jax import lax
from jax.experimental import pallas as pl
from jax.experimental.pallas import tpu as pltpu
from jax.sharding import PartitionSpec as P

LANES = 128
LANE_BITS = 7
SUBLANES = 8
VALUE_BITS = 24
ROW_BITS = 16
SECTION_ORDER = (2, 0, 1)
HELD_ROWS = 16
ROUNDS = 3
TOGETHER = 4
DIGIT_BITS = 3
VMEM = pltpu.VMEM
SMEM = pltpu.SMEM


def partner_of(tile, number, groups):
    if groups == ROUNDS + 1:
        return tile ^ (number + 1)
    return (tile + (groups - 1, 1, groups // 2)[number]) % groups


def answer_round(number, groups):
    return number if groups == ROUNDS + 1 else (1, 0, 2)[number]


def iota(shape, dimension):
    return lax.broadcasted_iota(jnp.int32, shape, dimension)


def gather_lanes(values, index):
    return jnp.take_along_axis(values, index, axis=1, mode="promise_in_bounds")


def compact(hits, values, pages):
    rows, lanes = hits[0].shape
    shape = (rows, lanes)
    lane, row = iota(shape, 1), iota(shape, 0)
    ones, above = [], []
    for hit in hits:
        one = hit.astype(jnp.int32)
        uppers = [jnp.where(row >= step, pltpu.roll(one, step, 0), 0) for step in range(1, rows)]
        ones.append(one.astype(jnp.float32))
        above.append(sum(uppers).astype(jnp.float32))
    blank = [jnp.zeros(shape, jnp.float32)] * (-len(hits) % 2)
    left = jnp.concatenate(ones + blank + above + blank, axis=0).astype(jnp.bfloat16)
    square = (lanes, lanes)
    earlier = (iota(square, 0) < iota(square, 1)).astype(jnp.bfloat16)
    right = jnp.concatenate([earlier, jnp.ones(square, jnp.bfloat16)], axis=1)
    sums = jnp.dot(left, right, preferred_element_type=jnp.float32).astype(jnp.int32)
    results, places = [], []
    for number, hit in enumerate(hits):
        start = number * rows
        rank, count = sums[start : start + rows, :lanes], sums[start : start + rows, lanes:]
        start += (len(hits) + len(blank)) * rows
        before = sums[start : start + rows, lanes:]
        held = jnp.where(hit, ((lane - rank) << VALUE_BITS) | values, -1)
        bit, bits = 0, (lanes - 1).bit_length()
        while bit < bits:
            wide = min(DIGIT_BITS, bits - bit)
            moved = jnp.full(shape, -1, jnp.int32)
            for digit in range(1 << wide):
                coming = pltpu.roll(held, lanes - (digit << bit), 1) if digit else held
                comes = (coming >> (VALUE_BITS + bit)) & ((1 << wide) - 1) == digit
                moved = jnp.where(comes & (coming >= 0), coming, moved)
            held = moved
            bit += wide
        held = held & ((1 << VALUE_BITS) - 1)
        lines = []
        for page in range(pages):
            offset = page * lanes + lane - before
            inside = (offset >= 0) & (offset < count)
            got = jnp.where(inside, gather_lanes(held, offset & (lanes - 1)), 0)
            lines.append(jnp.sum(got, axis=0, keepdims=True))
        results.append(lines)
        places.append(rank + before)
    return results, places


def list_kernel(groups, owner_any, cell_any, first, second, slot_ref, owner_ref, cell_ref, sems):
    copies = [
        pltpu.make_async_copy(source, target, sems.at[index])
        for index, (source, target) in enumerate(((owner_any, owner_ref), (cell_any, cell_ref)))
    ]
    for copy in copies:
        copy.start()
    tile, side = lax.axis_index("grid"), lax.axis_index("side")
    for copy in copies:
        copy.wait()
    owners = owner_ref[...]
    half = owners.shape[0] // 2
    hits = [owners == partner_of(tile, number, groups) for number in range(ROUNDS)]
    pages, ranks = compact(hits, cell_ref[...], half)
    slots = jnp.zeros_like(owners)
    for number, (hit, rank) in enumerate(zip(hits, ranks)):
        slots = jnp.where(hit, number * half * LANES + rank, slots)
    slot_ref[...] = slots
    for target, here, there in ((first, 0, 2), (second, 1, 1)):
        target[...] = jnp.zeros(target.shape, jnp.int32)
        for line in range(half):
            target[line : line + 1, :] = jnp.where(side == 0, pages[here][line], pages[there][line])


def fold(values, least):
    step = values.shape[0] // 2
    while step >= least:
        values = values + pltpu.roll(values, step, 0)
        step //= 2
    return values


def panel_rows(lev_dev, fields, tiles, groups, lists, group, state, packed, scratch):
    levels = SUBLANES
    bits = (levels - 1).bit_length()
    shape = (SUBLANES, LANES)
    sub = iota(shape, 0)
    per = SUBLANES // lev_dev
    quarters = lists[0].shape[0] // 2
    for number in range(ROUNDS):
        for quarter in range(quarters):
            cells = jnp.broadcast_to(lists[number][quarter : quarter + 1, :], shape)
            high, low = cells >> LANE_BITS, cells & (LANES - 1)
            sums = [jnp.zeros(shape, jnp.float32) for _ in range(fields)]
            code = jnp.zeros(shape, jnp.int32)
            for chunk in range(tiles // per):
                here = high == chunk * per + sub // lev_dev
                for field in range(fields):
                    start = field * tiles * lev_dev + chunk * SUBLANES
                    got = gather_lanes(state[start : start + SUBLANES, :], low)
                    sums[field] = jnp.where(here, got, sums[field])
            for chunk in range(tiles // SUBLANES):
                got = gather_lanes(packed[chunk * SUBLANES : (chunk + 1) * SUBLANES, :], low)
                code = jnp.where(high == chunk * SUBLANES + sub, got, code)
            source = (fold(code, 1) >> (bits * sub)) & (levels - 1)
            section = answer_round(number, groups)
            for field in range(fields):
                both = fold(sums[field], lev_dev)
                placed = jnp.zeros(shape, jnp.float32)
                for level in range(lev_dev):
                    one = both
                    for turn in range(1, lev_dev):
                        one = jnp.where((sub - level) % lev_dev == turn, pltpu.roll(both, turn, 0), one)
                    placed = jnp.where(source == group * lev_dev + level, one, placed)
                row = ((section * fields + field) * quarters + quarter) * levels
                scratch[row : row + levels, :] = placed


def block_rows(lev_dev, fields, tiles, own, group, state, terrain, weight, scratch, mass):
    levels = SUBLANES
    coarse = weight.shape[1]
    per = LANES // coarse
    quarters = tiles // 2 // per

    def some_tiles(index, carry):
        number, quarter = index // (quarters // TOGETHER), index % (quarters // TOGETHER) * TOGETHER

        @pl.when(own[number, quarter * per] >= 0)
        def _():
            for more in range(TOGETHER):
                fill_tile(number * quarters + quarter + more, number, quarter + more)

        return carry

    def fill_tile(index, number, quarter):
        lefts, rights = [], []
        for place in range(per):
            name = own[number, quarter * per + place]
            block = jnp.maximum(name, 0)
            source = terrain[pl.ds(pl.multiple_of(block * levels, levels), levels), :]
            parts = []
            for field in range(fields):
                placed = jnp.zeros((levels, LANES), jnp.float32)
                for level in range(lev_dev):
                    line = state[pl.ds((field * tiles + block) * lev_dev + level, 1), :]
                    placed = jnp.where(source == group * lev_dev + level, line, placed)
                parts.append(placed)
            moved = jnp.concatenate(parts, axis=0)
            moved_high = moved.astype(jnp.bfloat16)
            moved_low = (moved - moved_high.astype(jnp.float32)).astype(jnp.bfloat16)
            lefts.append(
                jnp.concatenate(
                    [moved_high, moved_low, jnp.ones((2 * SUBLANES, LANES), jnp.bfloat16)], axis=0
                )
            )
            dense = jnp.where(name >= 0, weight[block], 0.0)
            dense_high = dense.astype(jnp.bfloat16)
            dense_low = (dense - dense_high.astype(jnp.float32)).astype(jnp.bfloat16)
            blank = jnp.zeros((coarse, LANES), jnp.bfloat16)
            rights.append(
                jnp.concatenate(
                    [dense_high if other == place else blank for other in range(per)]
                    + [dense_low if other == place else blank for other in range(per)],
                    axis=0,
                )
            )
        product = lax.dot_general(
            jnp.concatenate(lefts, axis=1),
            jnp.concatenate(rights, axis=1),
            (((1,), (1,)), ((), ())),
            preferred_element_type=jnp.float32,
        )
        product = product[:, :LANES] + product[:, LANES:]
        rows = fields * levels
        result = product[:rows] + product[rows : 2 * rows]
        for field in range(fields):
            row = ((number * fields + field) * quarters + quarter) * levels
            scratch[pl.ds(pl.multiple_of(row, levels), levels), :] = result[
                field * levels : (field + 1) * levels
            ]
        mass[pl.ds(index, 1), :] = product[2 * rows : 2 * rows + 1]

    lax.fori_loop(0, ROUNDS * quarters // TOGETHER, some_tiles, 0)


def prepare_kernel(lev_dev, fields, groups, block_owner, block_row, *refs):
    sources, (state, packed, table, facts) = refs[:3], refs[3:7]
    terrain, weight, own, owners, rows, sems = refs[7:]
    state_copy, terrain_copy, weight_copy = [
        pltpu.make_async_copy(source, target, sems.at[index])
        for index, (source, target) in enumerate(zip(sources, (state, terrain, weight)))
    ]
    owner_copy = pltpu.make_async_copy(block_owner, owners, sems.at[3])
    row_copy = pltpu.make_async_copy(block_row, rows, sems.at[4])
    tile, side, group = lax.axis_index("grid"), lax.axis_index("side"), lax.axis_index("lev")
    tiles = packed.shape[0]
    terrain_copy.start()
    state_copy.start()

    @pl.when(side == 0)
    def _():
        levels = SUBLANES
        bits = (levels - 1).bit_length()
        terrain_copy.wait()
        total = jnp.zeros((tiles, LANES), jnp.int32)
        for level in range(levels):
            total = total | (terrain[pl.ds(level, tiles, stride=levels), :] << (bits * level))
        packed[...] = total
        state_copy.wait()

    @pl.when(side == 1)
    def _():
        weight_copy.start()
        owner_copy.start()
        row_copy.start()
        blocks = owners.shape[1]
        count = facts.shape[0] - SUBLANES
        lane = iota((1, LANES), 1)
        partners = [partner_of(tile, number, groups) for number in range(ROUNDS)]

        def clear(place, carry):
            for number in range(ROUNDS):
                own[number, place] = -1
            return carry

        def enter(block, carry):
            counts, runs = list(carry[:ROUNDS]), list(carry[ROUNDS:])
            owner, row = owners[0, block], rows[0, block]
            for number in range(ROUNDS):
                mine = owner == partners[number]
                own[number, counts[number]] = jnp.where(mine, block, -1)
                runs[number] = jnp.where(
                    (lane == counts[number]) & mine, row.astype(jnp.float32), runs[number]
                )
                counts[number] = counts[number] + mine.astype(jnp.int32)
            return (*counts, *runs)

        lax.fori_loop(0, blocks // 2 + 1, clear, 0, unroll=True)
        owner_copy.wait()
        row_copy.wait()
        empty = jnp.full((1, LANES), -1.0, jnp.float32)
        carry = lax.fori_loop(
            0, blocks, enter, (jnp.int32(0),) * ROUNDS + (empty,) * ROUNDS, unroll=True
        )
        facts[count:, :] = jnp.zeros((SUBLANES, LANES), jnp.float32)
        for number in range(ROUNDS):
            facts[count + number : count + number + 1, :] = carry[ROUNDS + number]
        terrain_copy.wait()
        state_copy.wait()
        weight_copy.wait()
        block_rows(lev_dev, fields, tiles, own, group, state, terrain, weight, table, facts)


def produce_kernel(lev_dev, fields, partners, groups, *refs):
    lists, state, packed, table = refs[:3], refs[3], refs[4], refs[5]
    parts, scratch = refs[6 : 6 + partners], refs[6 + partners]
    tiles = packed.shape[0]
    side, group = lax.axis_index("side"), lax.axis_index("lev")

    def emit(source):
        rows = source.shape[0] // SUBLANES
        for distance in range(partners):
            target = group ^ distance
            for level in range(lev_dev):
                parts[distance][level * rows : (level + 1) * rows, :] = source[
                    pl.ds(target * lev_dev + level, rows, stride=SUBLANES), :
                ]

    @pl.when(side == 0)
    def _():
        panel_rows(lev_dev, fields, tiles, groups, lists, group, state, packed, scratch)
        emit(scratch)

    @pl.when(side == 1)
    def _():
        emit(table)


def sum_kernel(lev_dev, fields, partners, *refs):
    parts, facts, sections = refs[:partners], refs[partners], refs[partners + 1 :]
    total = parts[0][...]
    for part in parts[1:]:
        total = total + part[...]
    rows = total.shape[0] // lev_dev
    span = rows // ROUNDS
    quarters = span // fields
    masses = facts.shape[0] - SUBLANES
    for number, section in enumerate(sections):
        for level in range(lev_dev):
            start = level * rows + number * span
            section[level * span : (level + 1) * span, :] = total[start : start + span]
        last = lev_dev * span + quarters
        section[last - quarters : last, :] = facts[number * quarters : (number + 1) * quarters, :]
        section[last:, :] = jnp.zeros((section.shape[0] - last, LANES), jnp.float32)
        section[last : last + 1, :] = facts[masses + number : masses + number + 1, :]


def place_panel(lev_dev, fields, number, fresh, section, slots, found):
    shape = (SUBLANES, LANES)
    sub = iota(shape, 0)
    panel_tiles = slots.shape[0]
    quarters = panel_tiles // 2
    chunks = lev_dev * fields * quarters // SUBLANES
    for tile in range(panel_tiles):
        place = jnp.broadcast_to(slots[tile : tile + 1, :], shape)
        here = place >> LANE_BITS == number * quarters + sub % quarters
        low = place & (LANES - 1)
        for chunk in range(chunks):
            got = gather_lanes(section[chunk * SUBLANES : (chunk + 1) * SUBLANES, :], low)
            row = (tile * chunks + chunk) * SUBLANES
            before = 0.0 if fresh else found[row : row + SUBLANES, :]
            found[row : row + SUBLANES, :] = jnp.where(here, got, before)


def runs_of(section, quarters, kinds):
    row = quarters * kinds
    return section[row : row + 1, :].astype(jnp.int32)


def place_blocks(coarse, quarters, number, section, spread_high, spread_low):
    shape = (SUBLANES, LANES)
    lane, sub = iota(shape, 1), iota(shape, 0)
    kinds = spread_high.shape[1] // LANES
    runs = jnp.broadcast_to(runs_of(section, quarters, kinds), shape)
    indices, heres = [], []
    for quarter in range(quarters):
        run = jnp.where(lane == quarter * SUBLANES + sub, runs, 0)
        run = jnp.broadcast_to(jnp.sum(run, axis=1, keepdims=True), shape)
        shift = lane - (run & (LANES // coarse - 1)) * coarse
        indices.append((shift + sub * coarse) & (LANES - 1))
        heres.append((shift >= 0) & (shift < coarse) & (run >= 0))
    for pair in range(0, quarters, 2):
        for kind in range(kinds):
            both = []
            for quarter in (pair, pair + 1):
                row = kind * quarters + quarter
                line = jnp.broadcast_to(section[row : row + 1, :], shape)
                both.append(jnp.where(heres[quarter], gather_lanes(line, indices[quarter]), 0.0))
            both = jnp.concatenate(both, axis=0)
            high = both.astype(jnp.bfloat16)
            start = (number * quarters + pair) * SUBLANES
            here = (slice(start, start + 2 * SUBLANES), slice(kind * LANES, (kind + 1) * LANES))
            spread_high[here] = high
            spread_low[here] = (both - high.astype(jnp.float32)).astype(jnp.bfloat16)


def place_kernel(lev_dev, fields, coarse, groups, number, fresh, section, slots, *refs):
    spread_high, spread_low, found = refs[-3:]
    side = lax.axis_index("side")

    @pl.when(side == 0)
    def _():
        place_blocks(coarse, slots.shape[0] // 2, number, section, spread_high, spread_low)

    @pl.when(side == 1)
    def _():
        place_panel(lev_dev, fields, answer_round(number, groups), fresh, section, slots, found)


def finish_panel(lev_dev, fields, tiles, panel_tiles, found, state, staged, send):
    shape = (SUBLANES, LANES)
    sub = iota(shape, 0)
    quarters = panel_tiles // 2
    chunks = lev_dev * fields * quarters // SUBLANES
    share = SUBLANES // quarters
    rows = tiles * lev_dev
    for field in range(fields):
        start = field * rows
        part = field % share
        for tile in range(panel_tiles):
            for level in range(lev_dev):
                chunk = (level * fields + field) // share
                row = (tile * chunks + chunk) * SUBLANES
                rim = jnp.sum(
                    jnp.where(sub // quarters == part, found[row : row + SUBLANES, :], 0.0),
                    axis=0,
                    keepdims=True,
                )
                row = start + tile * lev_dev + level
                staged[row : row + 1, :] = 0.5 * (state[row : row + 1, :] + rim)
        rest = start + panel_tiles * lev_dev
        staged[rest : start + rows, :] = state[rest : start + rows, :]
        send(field)


def finish_coarse(
    lev_dev, fields, tiles, coarse, quarters, sections, spread_high, spread_low, state, staged, send
):
    width = quarters * SUBLANES
    shift = (LANES // coarse).bit_length() - 1
    tile = iota((tiles, LANES), 0)
    lane = iota((1, LANES), 1)
    runs = jnp.full((1, LANES), -1, jnp.int32)
    for number, section in enumerate(sections):
        turned = runs_of(section, quarters, lev_dev * fields + 1)
        if number:
            turned = pltpu.roll(jnp.broadcast_to(turned, (SUBLANES, LANES)), number * width, 1)[0:1]
        runs = jnp.where(lane // width == number, turned, runs)
    lands = (tile == jnp.broadcast_to(runs >> shift, tile.shape)).astype(jnp.bfloat16)
    lands = lands[:, : ROUNDS * width]

    def landed(kind):
        here = (slice(None), slice(kind * LANES, (kind + 1) * LANES))
        high = jnp.dot(lands, spread_high[here], preferred_element_type=jnp.float32)
        return high + jnp.dot(lands, spread_low[here], preferred_element_type=jnp.float32)

    scale = 1.0 / (1.0 + landed(lev_dev * fields))
    for field in range(fields):
        for level in range(lev_dev):
            here = pl.ds(field * tiles * lev_dev + level, tiles, stride=lev_dev)
            staged[here, :] = (state[here, :] + landed(level * fields + field)) * scale
        send(field)


def finish_kernel(lev_dev, fields, coarse, groups, number, *refs):
    sections, slots, kept, state = refs[:3], refs[3], refs[4:7], refs[7]
    out, spread_high, spread_low, found, staged, sems = refs[8:]
    quarters = slots.shape[0] // 2
    tiles = state.shape[0] // (fields * lev_dev)
    rows = tiles * lev_dev
    copies = [
        pltpu.make_async_copy(
            staged.at[field * rows : (field + 1) * rows],
            out.at[field * rows : (field + 1) * rows],
            sems.at[field],
        )
        for field in range(fields)
    ]
    side = lax.axis_index("side")

    def send(field):
        copies[field].start()

    @pl.when(side == 0)
    def _():
        spread_high[...] = kept[0][...]
        spread_low[...] = kept[1][...]
        place_blocks(coarse, quarters, number, sections[number], spread_high, spread_low)
        finish_coarse(
            lev_dev, fields, tiles, coarse, quarters, sections, spread_high, spread_low, state, staged, send
        )

    @pl.when(side == 1)
    def _():
        found[...] = kept[2][...]
        place_panel(lev_dev, fields, answer_round(number, groups), False, sections[number], slots, found)
        finish_panel(lev_dev, fields, tiles, slots.shape[0], found, state, staged, send)

    for copy in copies:
        copy.wait()


def specs(*spaces):
    return [pl.BlockSpec(memory_space=space) for space in spaces]


def params():
    return pltpu.CompilerParams(vmem_limit_bytes=16 * 1024 * 1024)


def in_hbm(value):
    return pltpu.with_memory_space_constraint(value, pltpu.HBM)


def struct(shape, dtype=jnp.float32):
    return jax.ShapeDtypeStruct(shape, dtype)


def on_device(
    model_state, terrain_level, panel_owner, panel_cell, block_weight, block_owner, block_row
):
    groups, partners = lax.axis_size("grid"), lax.axis_size("lev")
    sides = lax.axis_size("side")
    _, lev_dev, fields, cell_dev = model_state.shape
    levels = terrain_level.shape[1]
    tiles = cell_dev // LANES
    blocks, coarse, _ = block_weight.shape
    panel_tiles = panel_cell.shape[0] // LANES
    quarters = panel_tiles // 2
    state = (
        model_state.reshape(lev_dev, fields, tiles, LANES)
        .transpose(1, 2, 0, 3)
        .reshape(fields * tiles * lev_dev, LANES)
    )
    terrain = (
        terrain_level.reshape(levels, tiles, LANES).transpose(1, 0, 2).reshape(tiles * levels, LANES)
    )
    page = struct((panel_tiles, LANES), jnp.int32)
    first, second, slots = pl.pallas_call(
        functools.partial(list_kernel, groups),
        out_shape=[page] * 3,
        in_specs=specs(*[pl.ANY] * 2),
        out_specs=specs(*[VMEM] * 3),
        scratch_shapes=[
            VMEM(page.shape, jnp.int32),
            VMEM(page.shape, jnp.int32),
            pltpu.SemaphoreType.DMA((2,)),
        ],
        compiler_params=params(),
        name="lists",
    )(in_hbm(panel_owner.reshape(page.shape)), in_hbm(panel_cell.reshape(page.shape)))

    def towards(number_of, cross):
        return [
            (tile * sides + side, partner_of(tile, number_of(side), groups) * sides + (side ^ cross))
            for tile in range(groups)
            for side in range(sides)
        ]

    first = lax.ppermute(first, ("grid", "side"), towards(lambda side: 2 * side, 0))
    second = lax.ppermute(second, ("grid", "side"), towards(lambda side: 1, 0))
    third = lax.ppermute(first, "side", [(0, 1), (1, 0)])
    lists = [first, second, third]
    scratch_rows = ROUNDS * fields * quarters
    table_shape = (scratch_rows * SUBLANES, LANES)
    state, packed, table, facts = pl.pallas_call(
        functools.partial(prepare_kernel, lev_dev, fields, groups),
        out_shape=[
            struct(state.shape),
            struct((tiles, LANES), jnp.int32),
            struct(table_shape),
            struct((ROUNDS * quarters + SUBLANES, LANES)),
        ],
        in_specs=specs(*[pl.ANY] * 5),
        out_specs=specs(*[VMEM] * 4),
        scratch_shapes=[
            VMEM(terrain.shape, jnp.int32),
            VMEM(block_weight.shape, jnp.float32),
            SMEM((ROUNDS, LANES), jnp.int32),
            SMEM((1, blocks), jnp.int32),
            SMEM((1, blocks), jnp.int32),
            pltpu.SemaphoreType.DMA((5,)),
        ],
        cost_estimate=pl.CostEstimate(flops=0, bytes_accessed=8_000_000, transcendentals=0),
        compiler_params=params(),
        name="prepare",
    )(
        in_hbm(block_owner.reshape(1, blocks)),
        in_hbm(block_row.reshape(1, blocks)),
        in_hbm(state),
        in_hbm(terrain),
        in_hbm(block_weight),
    )
    part = struct((lev_dev * scratch_rows, LANES))
    parts = pl.pallas_call(
        functools.partial(produce_kernel, lev_dev, fields, partners, groups),
        out_shape=[part] * partners,
        in_specs=specs(*[VMEM] * 6),
        out_specs=specs(*[VMEM] * partners),
        scratch_shapes=[VMEM(table_shape, jnp.float32)],
        compiler_params=params(),
        name="produce",
    )(*lists, state, packed, table)
    arrived = [parts[0]] + [
        lax.ppermute(parts[distance], "lev", [(rank, rank ^ distance) for rank in range(partners)])
        for distance in range(partners - 1, 0, -1)
    ]
    section_rows = HELD_ROWS * quarters
    sections = pl.pallas_call(
        functools.partial(sum_kernel, lev_dev, fields, partners),
        out_shape=[struct((section_rows, LANES))] * 3,
        in_specs=specs(*[VMEM] * (partners + 1)),
        out_specs=specs(*[VMEM] * 3),
        compiler_params=params(),
        name="sections",
    )(*arrived, facts)
    sections = [
        lax.ppermute(sections[number], ("grid", "side"), towards(lambda side: number, 1))
        for number in SECTION_ORDER
    ]
    sections = [sections[SECTION_ORDER.index(number)] for number in range(ROUNDS)]
    kinds = lev_dev * fields + 1
    spread = struct((ROUNDS * quarters * SUBLANES, kinds * LANES), jnp.bfloat16)
    kept = [spread, spread, struct((panel_tiles * lev_dev * fields * quarters, LANES))]
    sizes = (lev_dev, fields, coarse, groups)
    held = []
    for number in SECTION_ORDER[:-1]:
        held = pl.pallas_call(
            functools.partial(place_kernel, *sizes, number, not held),
            out_shape=kept,
            in_specs=specs(*[VMEM] * (2 + len(held))),
            out_specs=specs(*[VMEM] * 3),
            input_output_aliases={2 + index: index for index in range(len(held))},
            compiler_params=params(),
            name="place",
        )(sections[number], slots, *held)
    result = pl.pallas_call(
        functools.partial(finish_kernel, *sizes, SECTION_ORDER[-1]),
        out_shape=pltpu.HBM(state.shape, jnp.float32),
        in_specs=specs(*[VMEM] * 8),
        out_specs=pl.BlockSpec(memory_space=pltpu.HBM),
        scratch_shapes=[VMEM(one.shape, one.dtype) for one in kept]
        + [VMEM(state.shape, jnp.float32), pltpu.SemaphoreType.DMA((fields,))],
        compiler_params=params(),
        name="finish",
    )(*sections, slots, *held, state)
    return (
        result.reshape(fields, tiles, lev_dev, LANES)
        .transpose(2, 0, 1, 3)
        .reshape(1, lev_dev, fields, cell_dev)
    )


def solution(mesh):
    in_specs = (
        P("side", "lev", None, "grid"),
        P("side", None, "grid"),
        P("grid", None),
        P("grid"),
        P("grid", None, None),
        P("grid", None),
        P("grid"),
    )
    out_specs = P("side", "lev", None, "grid")
    return jax.shard_map(
        on_device, mesh=mesh, in_specs=in_specs, out_specs=out_specs, check_vma=False
    )
```

```python
import functools

import jax
import jax.numpy as jnp
from jax import lax
from jax.experimental import pallas as pl
from jax.experimental.pallas import tpu as pltpu
from jax.sharding import PartitionSpec as P

LANES = 128
LANE_BITS = 7
SUBLANES = 8
VALUE_BITS = 24
ROW_BITS = 16
SECTION_ORDER = (2, 0, 1)
HELD_ROWS = 16
ROUNDS = 3
DIGIT_BITS = 3
VMEM = pltpu.VMEM
SMEM = pltpu.SMEM


def partner_of(tile, number, groups):
    if groups == ROUNDS + 1:
        return tile ^ (number + 1)
    return (tile + (groups - 1, 1, groups // 2)[number]) % groups


def answer_round(number, groups):
    return number if groups == ROUNDS + 1 else (1, 0, 2)[number]


def iota(shape, dimension):
    return lax.broadcasted_iota(jnp.int32, shape, dimension)


def gather_lanes(values, index):
    return jnp.take_along_axis(values, index, axis=1, mode="promise_in_bounds")


def compact(hits, values, pages):
    rows, lanes = hits[0].shape
    shape = (rows, lanes)
    lane, row = iota(shape, 1), iota(shape, 0)
    ones, above = [], []
    for hit in hits:
        one = hit.astype(jnp.int32)
        uppers = [jnp.where(row >= step, pltpu.roll(one, step, 0), 0) for step in range(1, rows)]
        ones.append(one.astype(jnp.float32))
        above.append(sum(uppers).astype(jnp.float32))
    blank = [jnp.zeros(shape, jnp.float32)] * (-len(hits) % 2)
    left = jnp.concatenate(ones + blank + above + blank, axis=0).astype(jnp.bfloat16)
    square = (lanes, lanes)
    earlier = (iota(square, 0) < iota(square, 1)).astype(jnp.bfloat16)
    right = jnp.concatenate([earlier, jnp.ones(square, jnp.bfloat16)], axis=1)
    sums = jnp.dot(left, right, preferred_element_type=jnp.float32).astype(jnp.int32)
    results, places = [], []
    for number, hit in enumerate(hits):
        start = number * rows
        rank, count = sums[start : start + rows, :lanes], sums[start : start + rows, lanes:]
        start += (len(hits) + len(blank)) * rows
        before = sums[start : start + rows, lanes:]
        held = jnp.where(hit, ((lane - rank) << VALUE_BITS) | values, -1)
        bit, bits = 0, (lanes - 1).bit_length()
        while bit < bits:
            wide = min(DIGIT_BITS, bits - bit)
            moved = jnp.full(shape, -1, jnp.int32)
            for digit in range(1 << wide):
                coming = pltpu.roll(held, lanes - (digit << bit), 1) if digit else held
                comes = (coming >> (VALUE_BITS + bit)) & ((1 << wide) - 1) == digit
                moved = jnp.where(comes & (coming >= 0), coming, moved)
            held = moved
            bit += wide
        held = held & ((1 << VALUE_BITS) - 1)
        lines = []
        for page in range(pages):
            offset = page * lanes + lane - before
            inside = (offset >= 0) & (offset < count)
            got = jnp.where(inside, gather_lanes(held, offset & (lanes - 1)), 0)
            lines.append(jnp.sum(got, axis=0, keepdims=True))
        results.append(lines)
        places.append(rank + before)
    return results, places


def list_kernel(groups, *refs):
    owner_any, cell_any, state_any, terrain_any, first, second, slot_ref, state, terrain = refs[:9]
    owner_ref, cell_ref, sems = refs[9:]
    copies = [
        pltpu.make_async_copy(source, target, sems.at[index])
        for index, (source, target) in enumerate(((owner_any, owner_ref), (cell_any, cell_ref)))
    ]
    for copy in copies:
        copy.start()
    tile, side = lax.axis_index("grid"), lax.axis_index("side")
    state_copy = pltpu.make_async_copy(state_any, state, sems.at[2])
    terrain_copy = pltpu.make_async_copy(terrain_any, terrain, sems.at[3])

    @pl.when(side == 0)
    def _():
        terrain_copy.start()
        state_copy.start()

    for copy in copies:
        copy.wait()
    owners = owner_ref[...]
    half = owners.shape[0] // 2
    hits = [owners == partner_of(tile, number, groups) for number in range(ROUNDS)]
    pages, ranks = compact(hits, cell_ref[...], half)
    slots = jnp.zeros_like(owners)
    for number, (hit, rank) in enumerate(zip(hits, ranks)):
        slots = jnp.where(hit, number * half * LANES + rank, slots)
    slot_ref[...] = slots
    for target, here, there in ((first, 0, 1), (second, 2, 2)):
        target[...] = jnp.zeros(target.shape, jnp.int32)
        for line in range(half):
            target[line : line + 1, :] = jnp.where(side == 0, pages[here][line], pages[there][line])

    @pl.when(side == 0)
    def _():
        terrain_copy.wait()
        state_copy.wait()


def fold(values, least):
    step = values.shape[0] // 2
    while step >= least:
        values = values + pltpu.roll(values, step, 0)
        step //= 2
    return values


def panel_rows(lev_dev, fields, tiles, groups, lists, group, state, packed, scratch):
    levels = SUBLANES
    bits = (levels - 1).bit_length()
    shape = (SUBLANES, LANES)
    sub = iota(shape, 0)
    per = SUBLANES // lev_dev
    quarters = lists[0].shape[0] // 2
    for number in range(ROUNDS):
        for quarter in range(quarters):
            cells = jnp.broadcast_to(lists[number][quarter : quarter + 1, :], shape)
            high, low = cells >> LANE_BITS, cells & (LANES - 1)
            sums = [jnp.zeros(shape, jnp.float32) for _ in range(fields)]
            code = jnp.zeros(shape, jnp.int32)
            for chunk in range(tiles // per):
                here = high == chunk * per + sub // lev_dev
                for field in range(fields):
                    start = field * tiles * lev_dev + chunk * SUBLANES
                    got = gather_lanes(state[start : start + SUBLANES, :], low)
                    sums[field] = jnp.where(here, got, sums[field])
            for chunk in range(tiles // SUBLANES):
                got = gather_lanes(packed[chunk * SUBLANES : (chunk + 1) * SUBLANES, :], low)
                code = jnp.where(high == chunk * SUBLANES + sub, got, code)
            source = (fold(code, 1) >> (bits * sub)) & (levels - 1)
            section = answer_round(number, groups)
            for field in range(fields):
                both = fold(sums[field], lev_dev)
                placed = jnp.zeros(shape, jnp.float32)
                for level in range(lev_dev):
                    one = both
                    for turn in range(1, lev_dev):
                        one = jnp.where((sub - level) % lev_dev == turn, pltpu.roll(both, turn, 0), one)
                    placed = jnp.where(source == group * lev_dev + level, one, placed)
                row = ((section * fields + field) * quarters + quarter) * levels
                scratch[row : row + levels, :] = placed


def block_rows(lev_dev, fields, tiles, group, state, terrain, weight, table, mass):
    levels = SUBLANES
    blocks, coarse, _ = weight.shape
    per = LANES // coarse
    for index in range(blocks // per):
        lefts, rights = [], []
        for place in range(per):
            block = index * per + place
            source = terrain[block * levels : (block + 1) * levels, :]
            parts = []
            for field in range(fields):
                placed = jnp.zeros((levels, LANES), jnp.float32)
                for level in range(lev_dev):
                    row = (field * tiles + block) * lev_dev + level
                    line = state[row : row + 1, :]
                    placed = jnp.where(source == group * lev_dev + level, line, placed)
                parts.append(placed)
            moved = jnp.concatenate(parts, axis=0)
            moved_high = moved.astype(jnp.bfloat16)
            moved_low = (moved - moved_high.astype(jnp.float32)).astype(jnp.bfloat16)
            lefts.append(
                jnp.concatenate(
                    [moved_high, moved_low, jnp.ones((2 * SUBLANES, LANES), jnp.bfloat16)], axis=0
                )
            )
            dense = weight[block]
            dense_high = dense.astype(jnp.bfloat16)
            dense_low = (dense - dense_high.astype(jnp.float32)).astype(jnp.bfloat16)
            blank = jnp.zeros((coarse, LANES), jnp.bfloat16)
            rights.append(
                jnp.concatenate(
                    [dense_high if other == place else blank for other in range(per)]
                    + [dense_low if other == place else blank for other in range(per)],
                    axis=0,
                )
            )
        product = lax.dot_general(
            jnp.concatenate(lefts, axis=1),
            jnp.concatenate(rights, axis=1),
            (((1,), (1,)), ((), ())),
            preferred_element_type=jnp.float32,
        )
        product = product[:, :LANES] + product[:, LANES:]
        rows = fields * levels
        result = product[:rows] + product[rows : 2 * rows]
        for field in range(fields):
            row = (field * (blocks // per) + index) * levels
            table[row : row + levels, :] = result[field * levels : (field + 1) * levels]
        mass[index : index + 1, :] = product[2 * rows : 2 * rows + 1]


def prepare_kernel(lev_dev, fields, groups, terrain_0, block_owner, block_row, *refs):
    sources, (state, packed, table, facts) = refs[:3], refs[3:7]
    terrain, weight, owners, rows, sems = refs[7:]
    copies = [
        pltpu.make_async_copy(source, target, sems.at[2 + index])
        for index, (source, target) in enumerate(zip(sources, (state, terrain, weight)))
    ]
    owner_copy = pltpu.make_async_copy(block_owner, owners, sems.at[0])
    row_copy = pltpu.make_async_copy(block_row, rows, sems.at[1])
    tile, side, group = lax.axis_index("grid"), lax.axis_index("side"), lax.axis_index("lev")
    tiles = packed.shape[0]

    @pl.when(side == 0)
    def _():
        levels = SUBLANES
        bits = (levels - 1).bit_length()
        total = jnp.zeros((tiles, LANES), jnp.int32)
        for level in range(levels):
            total = total | (terrain_0[pl.ds(level, tiles, stride=levels), :] << (bits * level))
        packed[...] = total

    @pl.when(side == 1)
    def _():
        for copy in copies:
            copy.start()
        owner_copy.start()
        row_copy.start()
        blocks = owners.shape[1]
        lane = iota((1, LANES), 1)
        partners = [partner_of(tile, number, groups) for number in range(ROUNDS)]

        def enter(block, carry):
            counts, names, runs = [list(carry[at : at + ROUNDS]) for at in range(0, 3 * ROUNDS, ROUNDS)]
            owner, run = owners[0, block], rows[0, block].astype(jnp.float32)
            name = block.astype(jnp.float32)
            for number in range(ROUNDS):
                mine = owner == partners[number]
                here = (lane == counts[number]) & mine
                names[number] = jnp.where(here, name, names[number])
                runs[number] = jnp.where(here, run, runs[number])
                counts[number] = counts[number] + mine.astype(jnp.int32)
            return (*counts, *names, *runs)

        owner_copy.wait()
        row_copy.wait()
        empty = jnp.full((1, LANES), -1.0, jnp.float32)
        carry = lax.fori_loop(
            0, blocks, enter, (jnp.int32(0),) * ROUNDS + (empty,) * (2 * ROUNDS), unroll=True
        )
        facts[SUBLANES:, :] = jnp.zeros((SUBLANES, LANES), jnp.float32)
        for number in range(2 * ROUNDS):
            facts[SUBLANES + number : SUBLANES + number + 1, :] = carry[ROUNDS + number]
        for copy in copies:
            copy.wait()
        block_rows(lev_dev, fields, tiles, group, state, terrain, weight, table, facts)


def produce_kernel(lev_dev, fields, partners, groups, *refs):
    lists, state, packed, table = refs[:3], refs[3], refs[4], refs[5]
    parts, scratch = refs[6 : 6 + partners], refs[6 + partners]
    tiles = packed.shape[0]
    side, group = lax.axis_index("side"), lax.axis_index("lev")

    def emit(source):
        rows = source.shape[0] // SUBLANES
        span = parts[0].shape[0] // lev_dev
        for distance in range(partners):
            target = group ^ distance
            for level in range(lev_dev):
                parts[distance][level * span : level * span + rows, :] = source[
                    pl.ds(target * lev_dev + level, rows, stride=SUBLANES), :
                ]

    @pl.when(side == 0)
    def _():
        panel_rows(lev_dev, fields, tiles, groups, lists, group, state, packed, scratch)
        emit(scratch)

    @pl.when(side == 1)
    def _():
        emit(table)


def sum_kernel(lev_dev, fields, coarse, partners, *refs):
    parts, facts, sections = refs[:partners], refs[partners], refs[partners + 1 :]
    total = parts[0][...]
    for part in parts[1:]:
        total = total + part[...]
    rows = total.shape[0] // lev_dev
    span = rows // ROUNDS
    quarters = span // fields
    side = lax.axis_index("side")
    kinds = lev_dev * fields + 1

    @pl.when(side == 0)
    def _():
        for number, section in enumerate(sections):
            for level in range(lev_dev):
                start = level * rows + number * span
                section[level * span : (level + 1) * span, :] = total[start : start + span]
            rest = section.shape[0] - lev_dev * span
            section[lev_dev * span :, :] = jnp.zeros((rest, LANES), jnp.float32)

    @pl.when(side == 1)
    def _():
        shape = (SUBLANES, LANES)
        lane, sub = iota(shape, 1), iota(shape, 0)
        per = LANES // coarse
        sources = [
            total[level * rows + field * SUBLANES : level * rows + (field + 1) * SUBLANES]
            for level in range(lev_dev)
            for field in range(fields)
        ] + [facts[0:SUBLANES, :]]
        for number, section in enumerate(sections):
            names = facts[SUBLANES + number : SUBLANES + number + 1, :].astype(jnp.int32)
            names = jnp.broadcast_to(names, shape)
            for quarter in range(quarters):
                name = gather_lanes(names, quarter * per + lane // coarse)
                low = (name & (per - 1)) * coarse + lane % coarse
                here = (sub == name // per) & (name >= 0)
                for kind, source in enumerate(sources):
                    got = jnp.where(here, gather_lanes(source, low), 0.0)
                    row = kind * quarters + quarter
                    section[row : row + 1, :] = jnp.sum(got, axis=0, keepdims=True)
            last = kinds * quarters
            section[last:, :] = jnp.zeros((section.shape[0] - last, LANES), jnp.float32)
            run = SUBLANES + ROUNDS + number
            section[last : last + 1, :] = facts[run : run + 1, :]


def place_panel(lev_dev, fields, number, fresh, section, slots, found):
    shape = (SUBLANES, LANES)
    sub = iota(shape, 0)
    panel_tiles = slots.shape[0]
    quarters = panel_tiles // 2
    chunks = lev_dev * fields * quarters // SUBLANES
    for tile in range(panel_tiles):
        place = jnp.broadcast_to(slots[tile : tile + 1, :], shape)
        here = place >> LANE_BITS == number * quarters + sub % quarters
        low = place & (LANES - 1)
        for chunk in range(chunks):
            got = gather_lanes(section[chunk * SUBLANES : (chunk + 1) * SUBLANES, :], low)
            row = (tile * chunks + chunk) * SUBLANES
            before = 0.0 if fresh else found[row : row + SUBLANES, :]
            found[row : row + SUBLANES, :] = jnp.where(here, got, before)


def runs_of(section, quarters, kinds):
    row = quarters * kinds
    return section[row : row + 1, :].astype(jnp.int32)


def place_blocks(coarse, quarters, number, section, spread_high, spread_low):
    shape = (SUBLANES, LANES)
    lane, sub = iota(shape, 1), iota(shape, 0)
    kinds = spread_high.shape[1] // LANES
    runs = jnp.broadcast_to(runs_of(section, quarters, kinds), shape)
    indices, heres = [], []
    for quarter in range(quarters):
        run = jnp.where(lane == quarter * SUBLANES + sub, runs, 0)
        run = jnp.broadcast_to(jnp.sum(run, axis=1, keepdims=True), shape)
        shift = lane - (run & (LANES // coarse - 1)) * coarse
        indices.append((shift + sub * coarse) & (LANES - 1))
        heres.append((shift >= 0) & (shift < coarse) & (run >= 0))
    for pair in range(0, quarters, 2):
        for kind in range(kinds):
            both = []
            for quarter in (pair, pair + 1):
                row = kind * quarters + quarter
                line = jnp.broadcast_to(section[row : row + 1, :], shape)
                both.append(jnp.where(heres[quarter], gather_lanes(line, indices[quarter]), 0.0))
            both = jnp.concatenate(both, axis=0)
            high = both.astype(jnp.bfloat16)
            start = (number * quarters + pair) * SUBLANES
            here = (slice(start, start + 2 * SUBLANES), slice(kind * LANES, (kind + 1) * LANES))
            spread_high[here] = high
            spread_low[here] = (both - high.astype(jnp.float32)).astype(jnp.bfloat16)


def place_kernel(lev_dev, fields, coarse, groups, number, fresh, section, slots, *refs):
    spread_high, spread_low, found = refs[-3:]
    side = lax.axis_index("side")

    @pl.when(side == 0)
    def _():
        place_blocks(coarse, slots.shape[0] // 2, number, section, spread_high, spread_low)

    @pl.when(side == 1)
    def _():
        place_panel(lev_dev, fields, answer_round(number, groups), fresh, section, slots, found)


def finish_panel(lev_dev, fields, tiles, panel_tiles, found, state, staged, send):
    shape = (SUBLANES, LANES)
    sub = iota(shape, 0)
    quarters = panel_tiles // 2
    chunks = lev_dev * fields * quarters // SUBLANES
    share = SUBLANES // quarters
    rows = tiles * lev_dev
    for field in range(fields):
        start = field * rows
        part = field % share
        for tile in range(panel_tiles):
            for level in range(lev_dev):
                chunk = (level * fields + field) // share
                row = (tile * chunks + chunk) * SUBLANES
                rim = jnp.sum(
                    jnp.where(sub // quarters == part, found[row : row + SUBLANES, :], 0.0),
                    axis=0,
                    keepdims=True,
                )
                row = start + tile * lev_dev + level
                staged[row : row + 1, :] = 0.5 * (state[row : row + 1, :] + rim)
        rest = start + panel_tiles * lev_dev
        staged[rest : start + rows, :] = state[rest : start + rows, :]
        send(field)


def finish_coarse(
    lev_dev, fields, tiles, coarse, quarters, sections, spread_high, spread_low, state, staged, send
):
    width = quarters * SUBLANES
    shift = (LANES // coarse).bit_length() - 1
    tile = iota((tiles, LANES), 0)
    lane = iota((1, LANES), 1)
    runs = jnp.full((1, LANES), -1, jnp.int32)
    for number, section in enumerate(sections):
        turned = runs_of(section, quarters, lev_dev * fields + 1)
        if number:
            turned = pltpu.roll(jnp.broadcast_to(turned, (SUBLANES, LANES)), number * width, 1)[0:1]
        runs = jnp.where(lane // width == number, turned, runs)
    lands = (tile == jnp.broadcast_to(runs >> shift, tile.shape)).astype(jnp.bfloat16)
    lands = lands[:, : ROUNDS * width]

    def landed(kind):
        here = (slice(None), slice(kind * LANES, (kind + 1) * LANES))
        high = jnp.dot(lands, spread_high[here], preferred_element_type=jnp.float32)
        return high + jnp.dot(lands, spread_low[here], preferred_element_type=jnp.float32)

    scale = 1.0 / (1.0 + landed(lev_dev * fields))
    for field in range(fields):
        for level in range(lev_dev):
            here = pl.ds(field * tiles * lev_dev + level, tiles, stride=lev_dev)
            staged[here, :] = (state[here, :] + landed(level * fields + field)) * scale
        send(field)


def finish_kernel(lev_dev, fields, coarse, groups, number, *refs):
    sections, slots, kept, state, state_1 = refs[:3], refs[3], refs[4:7], refs[7], refs[8]
    out, spread_high, spread_low, found, staged, sems = refs[9:]
    quarters = slots.shape[0] // 2
    tiles = state.shape[0] // (fields * lev_dev)
    rows = tiles * lev_dev
    copies = [
        pltpu.make_async_copy(
            staged.at[field * rows : (field + 1) * rows],
            out.at[field * rows : (field + 1) * rows],
            sems.at[field],
        )
        for field in range(fields)
    ]
    side = lax.axis_index("side")

    def send(field):
        copies[field].start()

    @pl.when(side == 0)
    def _():
        spread_high[...] = kept[0][...]
        spread_low[...] = kept[1][...]
        place_blocks(coarse, quarters, number, sections[number], spread_high, spread_low)
        finish_coarse(
            lev_dev, fields, tiles, coarse, quarters, sections, spread_high, spread_low, state, staged, send
        )

    @pl.when(side == 1)
    def _():
        found[...] = kept[2][...]
        place_panel(lev_dev, fields, answer_round(number, groups), False, sections[number], slots, found)
        finish_panel(lev_dev, fields, tiles, slots.shape[0], found, state_1, staged, send)

    for copy in copies:
        copy.wait()


def specs(*spaces):
    return [pl.BlockSpec(memory_space=space) for space in spaces]


def params():
    return pltpu.CompilerParams(vmem_limit_bytes=16 * 1024 * 1024)


def in_hbm(value):
    return pltpu.with_memory_space_constraint(value, pltpu.HBM)


def struct(shape, dtype=jnp.float32):
    return jax.ShapeDtypeStruct(shape, dtype)


def on_device(
    model_state, terrain_level, panel_owner, panel_cell, block_weight, block_owner, block_row
):
    groups, partners = lax.axis_size("grid"), lax.axis_size("lev")
    sides = lax.axis_size("side")
    _, lev_dev, fields, cell_dev = model_state.shape
    levels = terrain_level.shape[1]
    tiles = cell_dev // LANES
    blocks, coarse, _ = block_weight.shape
    panel_tiles = panel_cell.shape[0] // LANES
    quarters = panel_tiles // 2
    state = (
        model_state.reshape(lev_dev, fields, tiles, LANES)
        .transpose(1, 2, 0, 3)
        .reshape(fields * tiles * lev_dev, LANES)
    )
    terrain = (
        terrain_level.reshape(levels, tiles, LANES).transpose(1, 0, 2).reshape(tiles * levels, LANES)
    )
    page = struct((panel_tiles, LANES), jnp.int32)
    sources = [in_hbm(state), in_hbm(terrain), in_hbm(block_weight)]
    first, second, slots, state_0, terrain_0 = pl.pallas_call(
        functools.partial(list_kernel, groups),
        out_shape=[page] * 3 + [struct(state.shape), struct(terrain.shape, jnp.int32)],
        in_specs=specs(*[pl.ANY] * 4),
        out_specs=specs(*[VMEM] * 5),
        scratch_shapes=[
            VMEM(page.shape, jnp.int32),
            VMEM(page.shape, jnp.int32),
            pltpu.SemaphoreType.DMA((4,)),
        ],
        compiler_params=params(),
        name="lists",
    )(
        in_hbm(panel_owner.reshape(page.shape)),
        in_hbm(panel_cell.reshape(page.shape)),
        *sources[:2],
    )

    def towards(number_of, cross):
        return [
            (tile * sides + side, partner_of(tile, number_of(side), groups) * sides + (side ^ cross))
            for tile in range(groups)
            for side in range(sides)
        ]

    first = lax.ppermute(first, ("grid", "side"), towards(lambda side: side, 0))
    second = lax.ppermute(second, ("grid", "side"), towards(lambda side: 2, 1))
    third = lax.ppermute(first, "side", [(0, 1), (1, 0)])
    lists = [first, third, second]
    scratch_rows = ROUNDS * fields * quarters
    table_shape = (scratch_rows * SUBLANES, LANES)
    state_1, packed, table, facts = pl.pallas_call(
        functools.partial(prepare_kernel, lev_dev, fields, groups),
        out_shape=[
            struct(state.shape),
            struct((tiles, LANES), jnp.int32),
            struct((fields * blocks * coarse // LANES * levels, LANES)),
            struct((2 * SUBLANES, LANES)),
        ],
        in_specs=specs(VMEM, *[pl.ANY] * 5),
        out_specs=specs(*[VMEM] * 4),
        scratch_shapes=[
            VMEM(terrain.shape, jnp.int32),
            VMEM(block_weight.shape, jnp.float32),
            SMEM((1, blocks), jnp.int32),
            SMEM((1, blocks), jnp.int32),
            pltpu.SemaphoreType.DMA((5,)),
        ],
        cost_estimate=pl.CostEstimate(flops=0, bytes_accessed=8_000_000, transcendentals=0),
        compiler_params=params(),
        name="prepare",
    )(
        terrain_0,
        in_hbm(block_owner.reshape(1, blocks)),
        in_hbm(block_row.reshape(1, blocks)),
        *sources,
    )
    part = struct((lev_dev * scratch_rows, LANES))
    parts = pl.pallas_call(
        functools.partial(produce_kernel, lev_dev, fields, partners, groups),
        out_shape=[part] * partners,
        in_specs=specs(*[VMEM] * 6),
        out_specs=specs(*[VMEM] * partners),
        scratch_shapes=[VMEM(table_shape, jnp.float32)],
        compiler_params=params(),
        name="produce",
    )(*lists, state_0, packed, table)
    arrived = [parts[0]] + [
        lax.ppermute(parts[distance], "lev", [(rank, rank ^ distance) for rank in range(partners)])
        for distance in range(partners - 1, 0, -1)
    ]
    section_rows = HELD_ROWS * quarters
    sections = pl.pallas_call(
        functools.partial(sum_kernel, lev_dev, fields, coarse, partners),
        out_shape=[struct((section_rows, LANES))] * 3,
        in_specs=specs(*[VMEM] * (partners + 1)),
        out_specs=specs(*[VMEM] * 3),
        compiler_params=params(),
        name="sections",
    )(*arrived, facts)
    sections = [
        lax.ppermute(sections[number], ("grid", "side"), towards(lambda side: number, 1))
        for number in SECTION_ORDER
    ]
    sections = [sections[SECTION_ORDER.index(number)] for number in range(ROUNDS)]
    kinds = lev_dev * fields + 1
    spread = struct((ROUNDS * quarters * SUBLANES, kinds * LANES), jnp.bfloat16)
    kept = [spread, spread, struct((panel_tiles * lev_dev * fields * quarters, LANES))]
    sizes = (lev_dev, fields, coarse, groups)
    held = []
    for number in SECTION_ORDER[:-1]:
        held = pl.pallas_call(
            functools.partial(place_kernel, *sizes, number, not held),
            out_shape=kept,
            in_specs=specs(*[VMEM] * (2 + len(held))),
            out_specs=specs(*[VMEM] * 3),
            input_output_aliases={2 + index: index for index in range(len(held))},
            compiler_params=params(),
            name="place",
        )(sections[number], slots, *held)
    result = pl.pallas_call(
        functools.partial(finish_kernel, *sizes, SECTION_ORDER[-1]),
        out_shape=pltpu.HBM(state.shape, jnp.float32),
        in_specs=specs(*[VMEM] * 9),
        out_specs=pl.BlockSpec(memory_space=pltpu.HBM),
        scratch_shapes=[VMEM(one.shape, one.dtype) for one in kept]
        + [VMEM(state.shape, jnp.float32), pltpu.SemaphoreType.DMA((fields,))],
        compiler_params=params(),
        name="finish",
    )(*sections, slots, *held, state_0, state_1)
    return (
        result.reshape(fields, tiles, lev_dev, LANES)
        .transpose(2, 0, 1, 3)
        .reshape(1, lev_dev, fields, cell_dev)
    )


def solution(mesh):
    in_specs = (
        P("side", "lev", None, "grid"),
        P("side", None, "grid"),
        P("grid", None),
        P("grid"),
        P("grid", None, None),
        P("grid", None),
        P("grid"),
    )
    out_specs = P("side", "lev", None, "grid")
    return jax.shard_map(
        on_device, mesh=mesh, in_specs=in_specs, out_specs=out_specs, check_vma=False
    )
```

```python
import functools

import jax
import jax.numpy as jnp
from jax import lax
from jax.experimental import pallas as pl
from jax.experimental.pallas import tpu as pltpu
from jax.sharding import PartitionSpec as P

LANES = 128
LANE_BITS = 7
SUBLANES = 8
VALUE_BITS = 24
ROW_BITS = 16
SECTION_ORDER = (2, 0, 1)
HELD_ROWS = 16
ROUNDS = 3
DIGIT_BITS = 3
VMEM = pltpu.VMEM
SMEM = pltpu.SMEM


def partner_of(tile, number, groups):
    if groups == ROUNDS + 1:
        return tile ^ (number + 1)
    return (tile + (groups - 1, 1, groups // 2)[number]) % groups


def answer_round(number, groups):
    return number if groups == ROUNDS + 1 else (1, 0, 2)[number]


def quotient(value, divisor):
    return value >> (divisor - 1).bit_length()


def remainder(value, divisor):
    return value & (divisor - 1)


def iota(shape, dimension):
    return lax.broadcasted_iota(jnp.int32, shape, dimension)


def gather_lanes(values, index):
    return jnp.take_along_axis(values, index, axis=1, mode="promise_in_bounds")


def compact(hits, values, pages):
    rows, lanes = hits[0].shape
    shape = (rows, lanes)
    lane, row = iota(shape, 1), iota(shape, 0)
    ones, above = [], []
    for hit in hits:
        one = hit.astype(jnp.int32)
        uppers = [jnp.where(row >= step, pltpu.roll(one, step, 0), 0) for step in range(1, rows)]
        ones.append(one.astype(jnp.float32))
        above.append(sum(uppers).astype(jnp.float32))
    blank = [jnp.zeros(shape, jnp.float32)] * (-len(hits) % 2)
    left = jnp.concatenate(ones + blank + above + blank, axis=0).astype(jnp.bfloat16)
    square = (lanes, lanes)
    earlier = (iota(square, 0) < iota(square, 1)).astype(jnp.bfloat16)
    right = jnp.concatenate([earlier, jnp.ones(square, jnp.bfloat16)], axis=1)
    sums = jnp.dot(left, right, preferred_element_type=jnp.float32).astype(jnp.int32)
    results, places = [], []
    for number, hit in enumerate(hits):
        start = number * rows
        rank, count = sums[start : start + rows, :lanes], sums[start : start + rows, lanes:]
        start += (len(hits) + len(blank)) * rows
        before = sums[start : start + rows, lanes:]
        held = jnp.where(hit, ((lane - rank) << VALUE_BITS) | values, -1)
        bit, bits = 0, (lanes - 1).bit_length()
        while bit < bits:
            wide = min(DIGIT_BITS, bits - bit)
            moved = jnp.full(shape, -1, jnp.int32)
            for digit in range(1 << wide):
                coming = pltpu.roll(held, lanes - (digit << bit), 1) if digit else held
                comes = (coming >> (VALUE_BITS + bit)) & ((1 << wide) - 1) == digit
                moved = jnp.where(comes & (coming >= 0), coming, moved)
            held = moved
            bit += wide
        held = held & ((1 << VALUE_BITS) - 1)
        lines = []
        for page in range(pages):
            offset = page * lanes + lane - before
            inside = (offset >= 0) & (offset < count)
            got = jnp.where(inside, gather_lanes(held, offset & (lanes - 1)), 0)
            lines.append(jnp.sum(got, axis=0, keepdims=True))
        results.append(lines)
        places.append(rank + before)
    return results, places


def list_kernel(groups, *refs):
    owner_any, cell_any, state_any, terrain_any, first, second, slot_ref, state, terrain = refs[:9]
    owner_ref, cell_ref, sems = refs[9:]
    copies = [
        pltpu.make_async_copy(source, target, sems.at[index])
        for index, (source, target) in enumerate(((owner_any, owner_ref), (cell_any, cell_ref)))
    ]
    for copy in copies:
        copy.start()
    tile, side = lax.axis_index("grid"), lax.axis_index("side")
    state_copy = pltpu.make_async_copy(state_any, state, sems.at[2])
    terrain_copy = pltpu.make_async_copy(terrain_any, terrain, sems.at[3])

    terrain_copy.start()
    state_copy.start()
    for copy in copies:
        copy.wait()
    owners = owner_ref[...]
    half = owners.shape[0] // 2
    hits = [owners == partner_of(tile, number, groups) for number in range(ROUNDS)]
    pages, ranks = compact(hits, cell_ref[...], half)
    slots = jnp.zeros_like(owners)
    for number, (hit, rank) in enumerate(zip(hits, ranks)):
        slots = jnp.where(hit, number * half * LANES + rank, slots)
    slot_ref[...] = slots
    for target, here, there in ((first, 0, 1), (second, 2, 2)):
        target[...] = jnp.zeros(target.shape, jnp.int32)
        for line in range(half):
            target[line : line + 1, :] = jnp.where(side == 0, pages[here][line], pages[there][line])
    terrain_copy.wait()
    state_copy.wait()


def fold(values, least):
    step = values.shape[0] // 2
    while step >= least:
        values = values + pltpu.roll(values, step, 0)
        step //= 2
    return values


def panel_rows(lev_dev, fields, tiles, groups, lists, group, state, packed, scratch):
    levels = SUBLANES
    bits = (levels - 1).bit_length()
    shape = (SUBLANES, LANES)
    sub = iota(shape, 0)
    per = SUBLANES // lev_dev
    quarters = lists[0].shape[0] // 2
    for number in range(ROUNDS):
        for quarter in range(quarters):
            cells = jnp.broadcast_to(lists[number][quarter : quarter + 1, :], shape)
            high, low = cells >> LANE_BITS, cells & (LANES - 1)
            sums = [jnp.zeros(shape, jnp.float32) for _ in range(fields)]
            code = jnp.zeros(shape, jnp.int32)
            for chunk in range(tiles // per):
                here = high == chunk * per + quotient(sub, lev_dev)
                for field in range(fields):
                    start = field * tiles * lev_dev + chunk * SUBLANES
                    got = gather_lanes(state[start : start + SUBLANES, :], low)
                    sums[field] = jnp.where(here, got, sums[field])
            for chunk in range(tiles // SUBLANES):
                got = gather_lanes(packed[chunk * SUBLANES : (chunk + 1) * SUBLANES, :], low)
                code = jnp.where(high == chunk * SUBLANES + sub, got, code)
            source = (fold(code, 1) >> (bits * sub)) & (levels - 1)
            section = answer_round(number, groups)
            for field in range(fields):
                both = fold(sums[field], lev_dev)
                placed = jnp.zeros(shape, jnp.float32)
                for level in range(lev_dev):
                    one = both
                    for turn in range(1, lev_dev):
                        one = jnp.where(remainder(sub - level, lev_dev) == turn, pltpu.roll(both, turn, 0), one)
                    placed = jnp.where(source == group * lev_dev + level, one, placed)
                row = ((section * fields + field) * quarters + quarter) * levels
                scratch[row : row + levels, :] = placed


def block_rows(lev_dev, fields, tiles, group, state, terrain, weight, table, mass):
    levels = SUBLANES
    blocks, coarse, _ = weight.shape
    per = LANES // coarse
    for index in range(blocks // per):
        lefts, rights = [], []
        for place in range(per):
            block = index * per + place
            source = terrain[block * levels : (block + 1) * levels, :]
            parts = []
            for field in range(fields):
                placed = jnp.zeros((levels, LANES), jnp.float32)
                for level in range(lev_dev):
                    row = (field * tiles + block) * lev_dev + level
                    line = state[row : row + 1, :]
                    placed = jnp.where(source == group * lev_dev + level, line, placed)
                parts.append(placed)
            moved = jnp.concatenate(parts, axis=0)
            moved_high = moved.astype(jnp.bfloat16)
            moved_low = (moved - moved_high.astype(jnp.float32)).astype(jnp.bfloat16)
            lefts.append(
                jnp.concatenate(
                    [moved_high, moved_low, jnp.ones((2 * SUBLANES, LANES), jnp.bfloat16)], axis=0
                )
            )
            dense = weight[block]
            dense_high = dense.astype(jnp.bfloat16)
            dense_low = (dense - dense_high.astype(jnp.float32)).astype(jnp.bfloat16)
            blank = jnp.zeros((coarse, LANES), jnp.bfloat16)
            rights.append(
                jnp.concatenate(
                    [dense_high if other == place else blank for other in range(per)]
                    + [dense_low if other == place else blank for other in range(per)],
                    axis=0,
                )
            )
        product = lax.dot_general(
            jnp.concatenate(lefts, axis=1),
            jnp.concatenate(rights, axis=1),
            (((1,), (1,)), ((), ())),
            preferred_element_type=jnp.float32,
        )
        product = product[:, :LANES] + product[:, LANES:]
        rows = fields * levels
        result = product[:rows] + product[rows : 2 * rows]
        for field in range(fields):
            row = (field * (blocks // per) + index) * levels
            table[row : row + levels, :] = result[field * levels : (field + 1) * levels]
        mass[index : index + 1, :] = product[2 * rows : 2 * rows + 1]


def prepare_kernel(lev_dev, fields, groups, state, terrain, *refs):
    block_owner, block_row, weight_any, packed, table, facts, weight, owners, rows, sems = refs
    weight_copy = pltpu.make_async_copy(weight_any, weight, sems.at[2])
    owner_copy = pltpu.make_async_copy(block_owner, owners, sems.at[0])
    row_copy = pltpu.make_async_copy(block_row, rows, sems.at[1])
    tile, side, group = lax.axis_index("grid"), lax.axis_index("side"), lax.axis_index("lev")
    tiles = packed.shape[0]

    @pl.when(side == 0)
    def _():
        levels = SUBLANES
        bits = (levels - 1).bit_length()
        total = jnp.zeros((tiles, LANES), jnp.int32)
        for level in range(levels):
            total = total | (terrain[pl.ds(level, tiles, stride=levels), :] << (bits * level))
        packed[...] = total

    @pl.when(side == 1)
    def _():
        owner_copy.start()
        row_copy.start()
        weight_copy.start()
        blocks = owners.shape[1]
        lane = iota((1, LANES), 1)
        partners = [partner_of(tile, number, groups) for number in range(ROUNDS)]

        def enter(block, carry):
            counts, names, runs = [list(carry[at : at + ROUNDS]) for at in range(0, 3 * ROUNDS, ROUNDS)]
            owner, run = owners[0, block], rows[0, block].astype(jnp.float32)
            name = block.astype(jnp.float32)
            for number in range(ROUNDS):
                mine = owner == partners[number]
                here = (lane == counts[number]) & mine
                names[number] = jnp.where(here, name, names[number])
                runs[number] = jnp.where(here, run, runs[number])
                counts[number] = counts[number] + mine.astype(jnp.int32)
            return (*counts, *names, *runs)

        owner_copy.wait()
        row_copy.wait()
        empty = jnp.full((1, LANES), -1.0, jnp.float32)
        carry = lax.fori_loop(
            0, blocks, enter, (jnp.int32(0),) * ROUNDS + (empty,) * (2 * ROUNDS), unroll=True
        )
        facts[SUBLANES:, :] = jnp.zeros((SUBLANES, LANES), jnp.float32)
        for number in range(2 * ROUNDS):
            facts[SUBLANES + number : SUBLANES + number + 1, :] = carry[ROUNDS + number]
        weight_copy.wait()
        block_rows(lev_dev, fields, tiles, group, state, terrain, weight, table, facts)


def produce_kernel(lev_dev, fields, partners, groups, *refs):
    lists, state, packed, table = refs[:3], refs[3], refs[4], refs[5]
    parts, scratch = refs[6 : 6 + partners], refs[6 + partners]
    tiles = packed.shape[0]
    side, group = lax.axis_index("side"), lax.axis_index("lev")

    def emit(source):
        rows = source.shape[0] // SUBLANES
        span = parts[0].shape[0] // lev_dev
        for distance in range(partners):
            target = group ^ distance
            for level in range(lev_dev):
                parts[distance][level * span : level * span + rows, :] = source[
                    pl.ds(target * lev_dev + level, rows, stride=SUBLANES), :
                ]

    @pl.when(side == 0)
    def _():
        panel_rows(lev_dev, fields, tiles, groups, lists, group, state, packed, scratch)
        emit(scratch)

    @pl.when(side == 1)
    def _():
        emit(table)


def sum_kernel(lev_dev, fields, coarse, partners, *refs):
    parts, facts, sections = refs[:partners], refs[partners], refs[partners + 1 :]
    total = parts[0][...]
    for part in parts[1:]:
        total = total + part[...]
    rows = total.shape[0] // lev_dev
    span = rows // ROUNDS
    quarters = span // fields
    side = lax.axis_index("side")
    kinds = lev_dev * fields + 1

    @pl.when(side == 0)
    def _():
        for number, section in enumerate(sections):
            for level in range(lev_dev):
                start = level * rows + number * span
                section[level * span : (level + 1) * span, :] = total[start : start + span]
            rest = section.shape[0] - lev_dev * span
            section[lev_dev * span :, :] = jnp.zeros((rest, LANES), jnp.float32)

    @pl.when(side == 1)
    def _():
        shape = (SUBLANES, LANES)
        lane, sub = iota(shape, 1), iota(shape, 0)
        per = LANES // coarse
        sources = [
            total[level * rows + field * SUBLANES : level * rows + (field + 1) * SUBLANES]
            for level in range(lev_dev)
            for field in range(fields)
        ] + [facts[0:SUBLANES, :]]
        for number, section in enumerate(sections):
            names = facts[SUBLANES + number : SUBLANES + number + 1, :].astype(jnp.int32)
            names = jnp.broadcast_to(names, shape)
            for quarter in range(quarters):
                name = gather_lanes(names, quarter * per + quotient(lane, coarse))
                low = remainder(name, per) * coarse + remainder(lane, coarse)
                here = sub == quotient(name, per)
                for kind, source in enumerate(sources):
                    got = jnp.where(here, gather_lanes(source, low), 0.0)
                    row = kind * quarters + quarter
                    section[row : row + 1, :] = jnp.sum(got, axis=0, keepdims=True)
            last = kinds * quarters
            section[last:, :] = jnp.zeros((section.shape[0] - last, LANES), jnp.float32)
            run = SUBLANES + ROUNDS + number
            section[last : last + 1, :] = facts[run : run + 1, :]


def place_panel(lev_dev, fields, number, fresh, section, slots, found):
    shape = (SUBLANES, LANES)
    sub = iota(shape, 0)
    panel_tiles = slots.shape[0]
    quarters = panel_tiles // 2
    chunks = lev_dev * fields * quarters // SUBLANES
    for tile in range(panel_tiles):
        place = jnp.broadcast_to(slots[tile : tile + 1, :], shape)
        here = place >> LANE_BITS == number * quarters + remainder(sub, quarters)
        low = place & (LANES - 1)
        for chunk in range(chunks):
            got = gather_lanes(section[chunk * SUBLANES : (chunk + 1) * SUBLANES, :], low)
            row = (tile * chunks + chunk) * SUBLANES
            before = 0.0 if fresh else found[row : row + SUBLANES, :]
            found[row : row + SUBLANES, :] = jnp.where(here, got, before)


def runs_of(section, quarters, kinds):
    row = quarters * kinds
    return section[row : row + 1, :].astype(jnp.int32)


def place_blocks(coarse, quarters, number, section, spread_high, spread_low):
    shape = (SUBLANES, LANES)
    lane, sub = iota(shape, 1), iota(shape, 0)
    kinds = spread_high.shape[1] // LANES
    runs = jnp.broadcast_to(runs_of(section, quarters, kinds), shape)
    indices, heres = [], []
    for quarter in range(quarters):
        run = jnp.where(lane == quarter * SUBLANES + sub, runs, 0)
        run = jnp.broadcast_to(jnp.sum(run, axis=1, keepdims=True), shape)
        shift = lane - (run & (LANES // coarse - 1)) * coarse
        indices.append((shift + sub * coarse) & (LANES - 1))
        heres.append((shift >= 0) & (shift < coarse) & (run >= 0))
    for pair in range(0, quarters, 2):
        for kind in range(kinds):
            both = []
            for quarter in (pair, pair + 1):
                row = kind * quarters + quarter
                line = jnp.broadcast_to(section[row : row + 1, :], shape)
                both.append(jnp.where(heres[quarter], gather_lanes(line, indices[quarter]), 0.0))
            both = jnp.concatenate(both, axis=0)
            high = both.astype(jnp.bfloat16)
            start = (number * quarters + pair) * SUBLANES
            here = (slice(start, start + 2 * SUBLANES), slice(kind * LANES, (kind + 1) * LANES))
            spread_high[here] = high
            spread_low[here] = (both - high.astype(jnp.float32)).astype(jnp.bfloat16)


def place_kernel(lev_dev, fields, coarse, groups, number, fresh, section, slots, *refs):
    spread_high, spread_low, found = refs[-3:]
    side = lax.axis_index("side")

    @pl.when(side == 0)
    def _():
        place_blocks(coarse, slots.shape[0] // 2, number, section, spread_high, spread_low)

    @pl.when(side == 1)
    def _():
        place_panel(lev_dev, fields, answer_round(number, groups), fresh, section, slots, found)


def finish_panel(lev_dev, fields, tiles, panel_tiles, found, state, staged, send):
    shape = (SUBLANES, LANES)
    sub = iota(shape, 0)
    quarters = panel_tiles // 2
    chunks = lev_dev * fields * quarters // SUBLANES
    share = SUBLANES // quarters
    rows = tiles * lev_dev
    for field in range(fields):
        start = field * rows
        part = field % share
        for tile in range(panel_tiles):
            for level in range(lev_dev):
                chunk = (level * fields + field) // share
                row = (tile * chunks + chunk) * SUBLANES
                rim = jnp.sum(
                    jnp.where(quotient(sub, quarters) == part, found[row : row + SUBLANES, :], 0.0),
                    axis=0,
                    keepdims=True,
                )
                row = start + tile * lev_dev + level
                staged[row : row + 1, :] = 0.5 * (state[row : row + 1, :] + rim)
        rest = start + panel_tiles * lev_dev
        staged[rest : start + rows, :] = state[rest : start + rows, :]
        send(field)


def finish_coarse(
    lev_dev, fields, tiles, coarse, quarters, sections, spread_high, spread_low, state, staged, send
):
    width = quarters * SUBLANES
    shift = (LANES // coarse).bit_length() - 1
    tile = iota((tiles, LANES), 0)
    lane = iota((1, LANES), 1)
    runs = jnp.full((1, LANES), -1, jnp.int32)
    for number, section in enumerate(sections):
        turned = runs_of(section, quarters, lev_dev * fields + 1)
        if number:
            turned = pltpu.roll(jnp.broadcast_to(turned, (SUBLANES, LANES)), number * width, 1)[0:1]
        runs = jnp.where(quotient(lane, width) == number, turned, runs)
    lands = (tile == jnp.broadcast_to(runs >> shift, tile.shape)).astype(jnp.bfloat16)
    lands = lands[:, : ROUNDS * width]

    def landed(kind):
        here = (slice(None), slice(kind * LANES, (kind + 1) * LANES))
        high = jnp.dot(lands, spread_high[here], preferred_element_type=jnp.float32)
        return high + jnp.dot(lands, spread_low[here], preferred_element_type=jnp.float32)

    scale = 1.0 / (1.0 + landed(lev_dev * fields))
    for field in range(fields):
        for level in range(lev_dev):
            here = pl.ds(field * tiles * lev_dev + level, tiles, stride=lev_dev)
            staged[here, :] = (state[here, :] + landed(level * fields + field)) * scale
        send(field)


def finish_kernel(lev_dev, fields, coarse, groups, number, *refs):
    sections, slots, kept, state = refs[:3], refs[3], refs[4:7], refs[7]
    out, spread_high, spread_low, found, staged, sems = refs[8:]
    quarters = slots.shape[0] // 2
    tiles = state.shape[0] // (fields * lev_dev)
    rows = tiles * lev_dev
    copies = [
        pltpu.make_async_copy(
            staged.at[field * rows : (field + 1) * rows],
            out.at[field * rows : (field + 1) * rows],
            sems.at[field],
        )
        for field in range(fields)
    ]
    side = lax.axis_index("side")

    def send(field):
        copies[field].start()

    @pl.when(side == 0)
    def _():
        spread_high[...] = kept[0][...]
        spread_low[...] = kept[1][...]
        place_blocks(coarse, quarters, number, sections[number], spread_high, spread_low)
        finish_coarse(
            lev_dev, fields, tiles, coarse, quarters, sections, spread_high, spread_low, state, staged, send
        )

    @pl.when(side == 1)
    def _():
        found[...] = kept[2][...]
        place_panel(lev_dev, fields, answer_round(number, groups), False, sections[number], slots, found)
        finish_panel(lev_dev, fields, tiles, slots.shape[0], found, state, staged, send)

    for copy in copies:
        copy.wait()


def specs(*spaces):
    return [pl.BlockSpec(memory_space=space) for space in spaces]


def params():
    return pltpu.CompilerParams(vmem_limit_bytes=16 * 1024 * 1024)


def in_hbm(value):
    return pltpu.with_memory_space_constraint(value, pltpu.HBM)


def struct(shape, dtype=jnp.float32):
    return jax.ShapeDtypeStruct(shape, dtype)


def on_device(
    model_state, terrain_level, panel_owner, panel_cell, block_weight, block_owner, block_row
):
    groups, partners = lax.axis_size("grid"), lax.axis_size("lev")
    sides = lax.axis_size("side")
    _, lev_dev, fields, cell_dev = model_state.shape
    levels = terrain_level.shape[1]
    tiles = cell_dev // LANES
    blocks, coarse, _ = block_weight.shape
    panel_tiles = panel_cell.shape[0] // LANES
    quarters = panel_tiles // 2
    state = (
        model_state.reshape(lev_dev, fields, tiles, LANES)
        .transpose(1, 2, 0, 3)
        .reshape(fields * tiles * lev_dev, LANES)
    )
    terrain = (
        terrain_level.reshape(levels, tiles, LANES).transpose(1, 0, 2).reshape(tiles * levels, LANES)
    )
    page = struct((panel_tiles, LANES), jnp.int32)
    first, second, slots, state, terrain = pl.pallas_call(
        functools.partial(list_kernel, groups),
        out_shape=[page] * 3 + [struct(state.shape), struct(terrain.shape, jnp.int32)],
        in_specs=specs(*[pl.ANY] * 4),
        out_specs=specs(*[VMEM] * 5),
        scratch_shapes=[
            VMEM(page.shape, jnp.int32),
            VMEM(page.shape, jnp.int32),
            pltpu.SemaphoreType.DMA((4,)),
        ],
        compiler_params=params(),
        name="lists",
    )(
        in_hbm(panel_owner.reshape(page.shape)),
        in_hbm(panel_cell.reshape(page.shape)),
        in_hbm(state),
        in_hbm(terrain),
    )

    def towards(number_of, cross):
        return [
            (tile * sides + side, partner_of(tile, number_of(side), groups) * sides + (side ^ cross))
            for tile in range(groups)
            for side in range(sides)
        ]

    first = lax.ppermute(first, ("grid", "side"), towards(lambda side: side, 0))
    second = lax.ppermute(second, ("grid", "side"), towards(lambda side: 2, 1))
    third = lax.ppermute(first, "side", [(0, 1), (1, 0)])
    lists = [first, third, second]
    scratch_rows = ROUNDS * fields * quarters
    table_shape = (scratch_rows * SUBLANES, LANES)
    packed, table, facts = pl.pallas_call(
        functools.partial(prepare_kernel, lev_dev, fields, groups),
        out_shape=[
            struct((tiles, LANES), jnp.int32),
            struct((fields * blocks * coarse // LANES * levels, LANES)),
            struct((2 * SUBLANES, LANES)),
        ],
        in_specs=specs(*[VMEM] * 2, *[pl.ANY] * 3),
        out_specs=specs(*[VMEM] * 3),
        scratch_shapes=[
            VMEM(block_weight.shape, jnp.float32),
            SMEM((1, blocks), jnp.int32),
            SMEM((1, blocks), jnp.int32),
            pltpu.SemaphoreType.DMA((3,)),
        ],
        cost_estimate=pl.CostEstimate(flops=0, bytes_accessed=8_000_000, transcendentals=0),
        compiler_params=params(),
        name="prepare",
    )(
        state,
        terrain,
        in_hbm(block_owner.reshape(1, blocks)),
        in_hbm(block_row.reshape(1, blocks)),
        in_hbm(block_weight),
    )
    part = struct((lev_dev * scratch_rows, LANES))
    parts = pl.pallas_call(
        functools.partial(produce_kernel, lev_dev, fields, partners, groups),
        out_shape=[part] * partners,
        in_specs=specs(*[VMEM] * 6),
        out_specs=specs(*[VMEM] * partners),
        scratch_shapes=[VMEM(table_shape, jnp.float32)],
        compiler_params=params(),
        name="produce",
    )(*lists, state, packed, table)
    arrived = [parts[0]] + [
        lax.ppermute(parts[distance], "lev", [(rank, rank ^ distance) for rank in range(partners)])
        for distance in range(partners - 1, 0, -1)
    ]
    section_rows = HELD_ROWS * quarters
    sections = pl.pallas_call(
        functools.partial(sum_kernel, lev_dev, fields, coarse, partners),
        out_shape=[struct((section_rows, LANES))] * 3,
        in_specs=specs(*[VMEM] * (partners + 1)),
        out_specs=specs(*[VMEM] * 3),
        compiler_params=params(),
        name="sections",
    )(*arrived, facts)
    sections = [
        lax.ppermute(sections[number], ("grid", "side"), towards(lambda side: number, 1))
        for number in SECTION_ORDER
    ]
    sections = [sections[SECTION_ORDER.index(number)] for number in range(ROUNDS)]
    kinds = lev_dev * fields + 1
    spread = struct((ROUNDS * quarters * SUBLANES, kinds * LANES), jnp.bfloat16)
    kept = [spread, spread, struct((panel_tiles * lev_dev * fields * quarters, LANES))]
    sizes = (lev_dev, fields, coarse, groups)
    held = []
    for number in SECTION_ORDER[:-1]:
        held = pl.pallas_call(
            functools.partial(place_kernel, *sizes, number, not held),
            out_shape=kept,
            in_specs=specs(*[VMEM] * (2 + len(held))),
            out_specs=specs(*[VMEM] * 3),
            input_output_aliases={2 + index: index for index in range(len(held))},
            compiler_params=params(),
            name="place",
        )(sections[number], slots, *held)
    result = pl.pallas_call(
        functools.partial(finish_kernel, *sizes, SECTION_ORDER[-1]),
        out_shape=pltpu.HBM(state.shape, jnp.float32),
        in_specs=specs(*[VMEM] * 8),
        out_specs=pl.BlockSpec(memory_space=pltpu.HBM),
        scratch_shapes=[VMEM(one.shape, one.dtype) for one in kept]
        + [VMEM(state.shape, jnp.float32), pltpu.SemaphoreType.DMA((fields,))],
        compiler_params=params(),
        name="finish",
    )(*sections, slots, *held, state)
    return (
        result.reshape(fields, tiles, lev_dev, LANES)
        .transpose(2, 0, 1, 3)
        .reshape(1, lev_dev, fields, cell_dev)
    )


def solution(mesh):
    in_specs = (
        P("side", "lev", None, "grid"),
        P("side", None, "grid"),
        P("grid", None),
        P("grid"),
        P("grid", None, None),
        P("grid", None),
        P("grid"),
    )
    out_specs = P("side", "lev", None, "grid")
    return jax.shard_map(
        on_device, mesh=mesh, in_specs=in_specs, out_specs=out_specs, check_vma=False
    )
```

```python
import functools

import jax
import jax.numpy as jnp
from jax import lax
from jax.experimental import pallas as pl
from jax.experimental.pallas import tpu as pltpu
from jax.sharding import PartitionSpec as P

LANES = 128
LANE_BITS = 7
SUBLANES = 8
VALUE_BITS = 24
ROW_BITS = 16
SECTION_ORDER = (1, 2, 0)
HELD_ROWS = 16
ROUNDS = 3
DIGIT_BITS = 3
VMEM = pltpu.VMEM
SMEM = pltpu.SMEM


def partner_of(tile, number, groups):
    if groups == ROUNDS + 1:
        return tile ^ (number + 1)
    return (tile + (groups - 1, 1, groups // 2)[number]) % groups


def answer_round(number, groups):
    return number if groups == ROUNDS + 1 else (1, 0, 2)[number]


def iota(shape, dimension):
    return lax.broadcasted_iota(jnp.int32, shape, dimension)


def gather_lanes(values, index):
    return jnp.take_along_axis(values, index, axis=1, mode="promise_in_bounds")


def compact(hits, values, pages):
    rows, lanes = hits[0].shape
    shape = (rows, lanes)
    lane, row = iota(shape, 1), iota(shape, 0)
    ones, above = [], []
    for hit in hits:
        one = hit.astype(jnp.int32)
        uppers = [jnp.where(row >= step, pltpu.roll(one, step, 0), 0) for step in range(1, rows)]
        ones.append(one.astype(jnp.float32))
        above.append(sum(uppers).astype(jnp.float32))
    blank = [jnp.zeros(shape, jnp.float32)] * (-len(hits) % 2)
    left = jnp.concatenate(ones + blank + above + blank, axis=0).astype(jnp.bfloat16)
    square = (lanes, lanes)
    earlier = (iota(square, 0) < iota(square, 1)).astype(jnp.bfloat16)
    right = jnp.concatenate([earlier, jnp.ones(square, jnp.bfloat16)], axis=1)
    sums = jnp.dot(left, right, preferred_element_type=jnp.float32).astype(jnp.int32)
    results, places = [], []
    for number, hit in enumerate(hits):
        start = number * rows
        rank, count = sums[start : start + rows, :lanes], sums[start : start + rows, lanes:]
        start += (len(hits) + len(blank)) * rows
        before = sums[start : start + rows, lanes:]
        held = jnp.where(hit, ((lane - rank) << VALUE_BITS) | values, -1)
        bit, bits = 0, (lanes - 1).bit_length()
        while bit < bits:
            wide = min(DIGIT_BITS, bits - bit)
            moved = jnp.full(shape, -1, jnp.int32)
            for digit in range(1 << wide):
                coming = pltpu.roll(held, lanes - (digit << bit), 1) if digit else held
                comes = (coming >> (VALUE_BITS + bit)) & ((1 << wide) - 1) == digit
                moved = jnp.where(comes & (coming >= 0), coming, moved)
            held = moved
            bit += wide
        held = held & ((1 << VALUE_BITS) - 1)
        lines = []
        for page in range(pages):
            offset = page * lanes + lane - before
            inside = (offset >= 0) & (offset < count)
            got = jnp.where(inside, gather_lanes(held, offset & (lanes - 1)), 0)
            lines.append(jnp.sum(got, axis=0, keepdims=True))
        results.append(lines)
        places.append(rank + before)
    return results, places


def list_kernel(groups, *refs):
    owner_any, cell_any, state_any, terrain_any, first, second, slot_ref, state, terrain = refs[:9]
    owner_ref, cell_ref, sems = refs[9:]
    copies = [
        pltpu.make_async_copy(source, target, sems.at[index])
        for index, (source, target) in enumerate(((owner_any, owner_ref), (cell_any, cell_ref)))
    ]
    for copy in copies:
        copy.start()
    tile, side = lax.axis_index("grid"), lax.axis_index("side")
    state_copy = pltpu.make_async_copy(state_any, state, sems.at[2])
    terrain_copy = pltpu.make_async_copy(terrain_any, terrain, sems.at[3])

    @pl.when(side == 0)
    def _():
        terrain_copy.start()
        state_copy.start()

    for copy in copies:
        copy.wait()
    owners = owner_ref[...]
    half = owners.shape[0] // 2
    hits = [owners == partner_of(tile, number, groups) for number in range(ROUNDS)]
    pages, ranks = compact(hits, cell_ref[...], half)
    slots = jnp.zeros_like(owners)
    for number, (hit, rank) in enumerate(zip(hits, ranks)):
        slots = jnp.where(hit, number * half * LANES + rank, slots)
    slot_ref[...] = slots
    for target, here, there in ((first, 0, 1), (second, 2, 2)):
        target[...] = jnp.zeros(target.shape, jnp.int32)
        for line in range(half):
            target[line : line + 1, :] = jnp.where(side == 0, pages[here][line], pages[there][line])

    @pl.when(side == 0)
    def _():
        terrain_copy.wait()
        state_copy.wait()


def fold(values, least):
    step = values.shape[0] // 2
    while step >= least:
        values = values + pltpu.roll(values, step, 0)
        step //= 2
    return values


def panel_rows(lev_dev, fields, tiles, groups, lists, group, state, packed, scratch):
    levels = SUBLANES
    bits = (levels - 1).bit_length()
    shape = (SUBLANES, LANES)
    sub = iota(shape, 0)
    per = SUBLANES // lev_dev
    quarters = lists[0].shape[0] // 2
    for number in range(ROUNDS):
        for quarter in range(quarters):
            cells = jnp.broadcast_to(lists[number][quarter : quarter + 1, :], shape)
            high, low = cells >> LANE_BITS, cells & (LANES - 1)
            sums = [jnp.zeros(shape, jnp.float32) for _ in range(fields)]
            code = jnp.zeros(shape, jnp.int32)
            for chunk in range(tiles // per):
                here = high == chunk * per + sub // lev_dev
                for field in range(fields):
                    start = field * tiles * lev_dev + chunk * SUBLANES
                    got = gather_lanes(state[start : start + SUBLANES, :], low)
                    sums[field] = jnp.where(here, got, sums[field])
            for chunk in range(tiles // SUBLANES):
                got = gather_lanes(packed[chunk * SUBLANES : (chunk + 1) * SUBLANES, :], low)
                code = jnp.where(high == chunk * SUBLANES + sub, got, code)
            source = (fold(code, 1) >> (bits * sub)) & (levels - 1)
            section = answer_round(number, groups)
            for field in range(fields):
                both = fold(sums[field], lev_dev)
                placed = jnp.zeros(shape, jnp.float32)
                for level in range(lev_dev):
                    one = both
                    for turn in range(1, lev_dev):
                        one = jnp.where((sub - level) % lev_dev == turn, pltpu.roll(both, turn, 0), one)
                    placed = jnp.where(source == group * lev_dev + level, one, placed)
                row = ((section * fields + field) * quarters + quarter) * levels
                scratch[row : row + levels, :] = placed


def block_rows(lev_dev, fields, tiles, group, state, terrain, weight, table, mass):
    levels = SUBLANES
    blocks, coarse, _ = weight.shape
    per = LANES // coarse
    for index in range(blocks // per):
        lefts, rights = [], []
        for place in range(per):
            block = index * per + place
            source = terrain[block * levels : (block + 1) * levels, :]
            parts = []
            for field in range(fields):
                placed = jnp.zeros((levels, LANES), jnp.float32)
                for level in range(lev_dev):
                    row = (field * tiles + block) * lev_dev + level
                    line = state[row : row + 1, :]
                    placed = jnp.where(source == group * lev_dev + level, line, placed)
                parts.append(placed)
            moved = jnp.concatenate(parts, axis=0)
            moved_high = moved.astype(jnp.bfloat16)
            moved_low = (moved - moved_high.astype(jnp.float32)).astype(jnp.bfloat16)
            lefts.append(
                jnp.concatenate(
                    [moved_high, moved_low, jnp.ones((2 * SUBLANES, LANES), jnp.bfloat16)], axis=0
                )
            )
            dense = weight[block]
            dense_high = dense.astype(jnp.bfloat16)
            dense_low = (dense - dense_high.astype(jnp.float32)).astype(jnp.bfloat16)
            blank = jnp.zeros((coarse, LANES), jnp.bfloat16)
            rights.append(
                jnp.concatenate(
                    [dense_high if other == place else blank for other in range(per)]
                    + [dense_low if other == place else blank for other in range(per)],
                    axis=0,
                )
            )
        product = lax.dot_general(
            jnp.concatenate(lefts, axis=1),
            jnp.concatenate(rights, axis=1),
            (((1,), (1,)), ((), ())),
            preferred_element_type=jnp.float32,
        )
        product = product[:, :LANES] + product[:, LANES:]
        rows = fields * levels
        result = product[:rows] + product[rows : 2 * rows]
        for field in range(fields):
            row = (field * (blocks // per) + index) * levels
            table[row : row + levels, :] = result[field * levels : (field + 1) * levels]
        mass[index : index + 1, :] = product[2 * rows : 2 * rows + 1]


def prepare_kernel(lev_dev, fields, groups, terrain_0, block_owner, block_row, *refs):
    sources, (state, packed, table, facts) = refs[:3], refs[3:7]
    terrain, weight, owners, rows, sems = refs[7:]
    copies = [
        pltpu.make_async_copy(source, target, sems.at[2 + index])
        for index, (source, target) in enumerate(zip(sources, (state, terrain, weight)))
    ]
    owner_copy = pltpu.make_async_copy(block_owner, owners, sems.at[0])
    row_copy = pltpu.make_async_copy(block_row, rows, sems.at[1])
    tile, side, group = lax.axis_index("grid"), lax.axis_index("side"), lax.axis_index("lev")
    tiles = packed.shape[0]

    @pl.when(side == 0)
    def _():
        levels = SUBLANES
        bits = (levels - 1).bit_length()
        total = jnp.zeros((tiles, LANES), jnp.int32)
        for level in range(levels):
            total = total | (terrain_0[pl.ds(level, tiles, stride=levels), :] << (bits * level))
        packed[...] = total

    @pl.when(side == 1)
    def _():
        for copy in copies:
            copy.start()
        owner_copy.start()
        row_copy.start()
        blocks = owners.shape[1]
        lane = iota((1, LANES), 1)
        partners = [partner_of(tile, number, groups) for number in range(ROUNDS)]

        def enter(block, carry):
            counts, names, runs = [list(carry[at : at + ROUNDS]) for at in range(0, 3 * ROUNDS, ROUNDS)]
            owner, run = owners[0, block], rows[0, block].astype(jnp.float32)
            name = block.astype(jnp.float32)
            for number in range(ROUNDS):
                mine = owner == partners[number]
                here = (lane == counts[number]) & mine
                names[number] = jnp.where(here, name, names[number])
                runs[number] = jnp.where(here, run, runs[number])
                counts[number] = counts[number] + mine.astype(jnp.int32)
            return (*counts, *names, *runs)

        owner_copy.wait()
        row_copy.wait()
        empty = jnp.full((1, LANES), -1.0, jnp.float32)
        carry = lax.fori_loop(
            0, blocks, enter, (jnp.int32(0),) * ROUNDS + (empty,) * (2 * ROUNDS), unroll=True
        )
        facts[SUBLANES:, :] = jnp.zeros((SUBLANES, LANES), jnp.float32)
        for number in range(2 * ROUNDS):
            facts[SUBLANES + number : SUBLANES + number + 1, :] = carry[ROUNDS + number]
        for copy in copies:
            copy.wait()
        block_rows(lev_dev, fields, tiles, group, state, terrain, weight, table, facts)


def produce_kernel(lev_dev, fields, partners, groups, *refs):
    lists, state, packed, table = refs[:3], refs[3], refs[4], refs[5]
    parts, scratch = refs[6 : 6 + partners], refs[6 + partners]
    tiles = packed.shape[0]
    side, group = lax.axis_index("side"), lax.axis_index("lev")

    def emit(source):
        rows = source.shape[0] // SUBLANES
        span = parts[0].shape[0] // lev_dev
        for distance in range(partners):
            target = group ^ distance
            for level in range(lev_dev):
                parts[distance][level * span : level * span + rows, :] = source[
                    pl.ds(target * lev_dev + level, rows, stride=SUBLANES), :
                ]

    @pl.when(side == 0)
    def _():
        panel_rows(lev_dev, fields, tiles, groups, lists, group, state, packed, scratch)
        emit(scratch)

    @pl.when(side == 1)
    def _():
        emit(table)


def sum_kernel(lev_dev, fields, coarse, partners, *refs):
    parts, facts, sections = refs[:partners], refs[partners], refs[partners + 1 :]
    total = parts[0][...]
    for part in parts[1:]:
        total = total + part[...]
    rows = total.shape[0] // lev_dev
    span = rows // ROUNDS
    quarters = span // fields
    side = lax.axis_index("side")
    kinds = lev_dev * fields + 1

    @pl.when(side == 0)
    def _():
        for number, section in enumerate(sections):
            for level in range(lev_dev):
                start = level * rows + number * span
                section[level * span : (level + 1) * span, :] = total[start : start + span]
            rest = section.shape[0] - lev_dev * span
            section[lev_dev * span :, :] = jnp.zeros((rest, LANES), jnp.float32)

    @pl.when(side == 1)
    def _():
        shape = (SUBLANES, LANES)
        lane, sub = iota(shape, 1), iota(shape, 0)
        per = LANES // coarse
        sources = [
            total[level * rows + field * SUBLANES : level * rows + (field + 1) * SUBLANES]
            for level in range(lev_dev)
            for field in range(fields)
        ] + [facts[0:SUBLANES, :]]
        for number, section in enumerate(sections):
            names = facts[SUBLANES + number : SUBLANES + number + 1, :].astype(jnp.int32)
            names = jnp.broadcast_to(names, shape)
            for quarter in range(quarters):
                name = gather_lanes(names, quarter * per + lane // coarse)
                low = (name & (per - 1)) * coarse + lane % coarse
                here = (sub == name // per) & (name >= 0)
                for kind, source in enumerate(sources):
                    got = jnp.where(here, gather_lanes(source, low), 0.0)
                    row = kind * quarters + quarter
                    section[row : row + 1, :] = jnp.sum(got, axis=0, keepdims=True)
            last = kinds * quarters
            section[last:, :] = jnp.zeros((section.shape[0] - last, LANES), jnp.float32)
            run = SUBLANES + ROUNDS + number
            section[last : last + 1, :] = facts[run : run + 1, :]


def place_panel(lev_dev, fields, number, fresh, section, slots, found):
    shape = (SUBLANES, LANES)
    sub = iota(shape, 0)
    panel_tiles = slots.shape[0]
    quarters = panel_tiles // 2
    chunks = lev_dev * fields * quarters // SUBLANES
    for tile in range(panel_tiles):
        place = jnp.broadcast_to(slots[tile : tile + 1, :], shape)
        here = place >> LANE_BITS == number * quarters + sub % quarters
        low = place & (LANES - 1)
        for chunk in range(chunks):
            got = gather_lanes(section[chunk * SUBLANES : (chunk + 1) * SUBLANES, :], low)
            row = (tile * chunks + chunk) * SUBLANES
            before = 0.0 if fresh else found[row : row + SUBLANES, :]
            found[row : row + SUBLANES, :] = jnp.where(here, got, before)


def runs_of(section, quarters, kinds):
    row = quarters * kinds
    return section[row : row + 1, :].astype(jnp.int32)


def place_blocks(coarse, quarters, number, section, spread_high, spread_low):
    shape = (SUBLANES, LANES)
    lane, sub = iota(shape, 1), iota(shape, 0)
    kinds = spread_high.shape[1] // LANES
    runs = jnp.broadcast_to(runs_of(section, quarters, kinds), shape)
    indices, heres = [], []
    for quarter in range(quarters):
        run = jnp.where(lane == quarter * SUBLANES + sub, runs, 0)
        run = jnp.broadcast_to(jnp.sum(run, axis=1, keepdims=True), shape)
        shift = lane - (run & (LANES // coarse - 1)) * coarse
        indices.append((shift + sub * coarse) & (LANES - 1))
        heres.append((shift >= 0) & (shift < coarse) & (run >= 0))
    for pair in range(0, quarters, 2):
        for kind in range(kinds):
            both = []
            for quarter in (pair, pair + 1):
                row = kind * quarters + quarter
                line = jnp.broadcast_to(section[row : row + 1, :], shape)
                both.append(jnp.where(heres[quarter], gather_lanes(line, indices[quarter]), 0.0))
            both = jnp.concatenate(both, axis=0)
            high = both.astype(jnp.bfloat16)
            start = (number * quarters + pair) * SUBLANES
            here = (slice(start, start + 2 * SUBLANES), slice(kind * LANES, (kind + 1) * LANES))
            spread_high[here] = high
            spread_low[here] = (both - high.astype(jnp.float32)).astype(jnp.bfloat16)


def place_kernel(lev_dev, fields, coarse, groups, number, fresh, section, slots, *refs):
    spread_high, spread_low, found = refs[-3:]
    side = lax.axis_index("side")

    @pl.when(side == 0)
    def _():
        place_blocks(coarse, slots.shape[0] // 2, number, section, spread_high, spread_low)

    @pl.when(side == 1)
    def _():
        place_panel(lev_dev, fields, answer_round(number, groups), fresh, section, slots, found)


def finish_panel(lev_dev, fields, tiles, panel_tiles, found, state, staged, send):
    shape = (SUBLANES, LANES)
    sub = iota(shape, 0)
    quarters = panel_tiles // 2
    chunks = lev_dev * fields * quarters // SUBLANES
    share = SUBLANES // quarters
    rows = tiles * lev_dev
    for field in range(fields):
        start = field * rows
        part = field % share
        for tile in range(panel_tiles):
            for level in range(lev_dev):
                chunk = (level * fields + field) // share
                row = (tile * chunks + chunk) * SUBLANES
                rim = jnp.sum(
                    jnp.where(sub // quarters == part, found[row : row + SUBLANES, :], 0.0),
                    axis=0,
                    keepdims=True,
                )
                row = start + tile * lev_dev + level
                staged[row : row + 1, :] = 0.5 * (state[row : row + 1, :] + rim)
        rest = start + panel_tiles * lev_dev
        staged[rest : start + rows, :] = state[rest : start + rows, :]
        send(field)


def finish_coarse(
    lev_dev, fields, tiles, coarse, quarters, sections, spread_high, spread_low, state, staged, send
):
    width = quarters * SUBLANES
    shift = (LANES // coarse).bit_length() - 1
    tile = iota((tiles, LANES), 0)
    lane = iota((1, LANES), 1)
    runs = jnp.full((1, LANES), -1, jnp.int32)
    for number, section in enumerate(sections):
        turned = runs_of(section, quarters, lev_dev * fields + 1)
        if number:
            turned = pltpu.roll(jnp.broadcast_to(turned, (SUBLANES, LANES)), number * width, 1)[0:1]
        runs = jnp.where(lane // width == number, turned, runs)
    lands = (tile == jnp.broadcast_to(runs >> shift, tile.shape)).astype(jnp.bfloat16)
    lands = lands[:, : ROUNDS * width]

    def landed(kind):
        here = (slice(None), slice(kind * LANES, (kind + 1) * LANES))
        high = jnp.dot(lands, spread_high[here], preferred_element_type=jnp.float32)
        return high + jnp.dot(lands, spread_low[here], preferred_element_type=jnp.float32)

    scale = 1.0 / (1.0 + landed(lev_dev * fields))
    for field in range(fields):
        for level in range(lev_dev):
            here = pl.ds(field * tiles * lev_dev + level, tiles, stride=lev_dev)
            staged[here, :] = (state[here, :] + landed(level * fields + field)) * scale
        send(field)


def finish_kernel(lev_dev, fields, coarse, groups, number, *refs):
    sections, slots, kept, state, state_1 = refs[:3], refs[3], refs[4:7], refs[7], refs[8]
    out, spread_high, spread_low, found, staged, sems = refs[9:]
    quarters = slots.shape[0] // 2
    tiles = state.shape[0] // (fields * lev_dev)
    rows = tiles * lev_dev
    copies = [
        pltpu.make_async_copy(
            staged.at[field * rows : (field + 1) * rows],
            out.at[field * rows : (field + 1) * rows],
            sems.at[field],
        )
        for field in range(fields)
    ]
    side = lax.axis_index("side")

    def send(field):
        copies[field].start()

    @pl.when(side == 0)
    def _():
        spread_high[...] = kept[0][...]
        spread_low[...] = kept[1][...]
        place_blocks(coarse, quarters, number, sections[number], spread_high, spread_low)
        finish_coarse(
            lev_dev, fields, tiles, coarse, quarters, sections, spread_high, spread_low, state, staged, send
        )

    @pl.when(side == 1)
    def _():
        found[...] = kept[2][...]
        place_panel(lev_dev, fields, answer_round(number, groups), False, sections[number], slots, found)
        finish_panel(lev_dev, fields, tiles, slots.shape[0], found, state_1, staged, send)

    for copy in copies:
        copy.wait()


def specs(*spaces):
    return [pl.BlockSpec(memory_space=space) for space in spaces]


def params():
    return pltpu.CompilerParams(vmem_limit_bytes=16 * 1024 * 1024)


def in_hbm(value):
    return pltpu.with_memory_space_constraint(value, pltpu.HBM)


def struct(shape, dtype=jnp.float32):
    return jax.ShapeDtypeStruct(shape, dtype)


def on_device(
    model_state, terrain_level, panel_owner, panel_cell, block_weight, block_owner, block_row
):
    groups, partners = lax.axis_size("grid"), lax.axis_size("lev")
    sides = lax.axis_size("side")
    _, lev_dev, fields, cell_dev = model_state.shape
    levels = terrain_level.shape[1]
    tiles = cell_dev // LANES
    blocks, coarse, _ = block_weight.shape
    panel_tiles = panel_cell.shape[0] // LANES
    quarters = panel_tiles // 2
    state = (
        model_state.reshape(lev_dev, fields, tiles, LANES)
        .transpose(1, 2, 0, 3)
        .reshape(fields * tiles * lev_dev, LANES)
    )
    terrain = (
        terrain_level.reshape(levels, tiles, LANES).transpose(1, 0, 2).reshape(tiles * levels, LANES)
    )
    page = struct((panel_tiles, LANES), jnp.int32)
    sources = [in_hbm(state), in_hbm(terrain), in_hbm(block_weight)]
    first, second, slots, state_0, terrain_0 = pl.pallas_call(
        functools.partial(list_kernel, groups),
        out_shape=[page] * 3 + [struct(state.shape), struct(terrain.shape, jnp.int32)],
        in_specs=specs(*[pl.ANY] * 4),
        out_specs=specs(*[VMEM] * 5),
        scratch_shapes=[
            VMEM(page.shape, jnp.int32),
            VMEM(page.shape, jnp.int32),
            pltpu.SemaphoreType.DMA((4,)),
        ],
        compiler_params=params(),
        name="lists",
    )(
        in_hbm(panel_owner.reshape(page.shape)),
        in_hbm(panel_cell.reshape(page.shape)),
        *sources[:2],
    )

    def towards(number_of, cross):
        return [
            (tile * sides + side, partner_of(tile, number_of(side), groups) * sides + (side ^ cross))
            for tile in range(groups)
            for side in range(sides)
        ]

    first = lax.ppermute(first, ("grid", "side"), towards(lambda side: side, 0))
    second = lax.ppermute(second, ("grid", "side"), towards(lambda side: 2, 1))
    third = lax.ppermute(first, "side", [(0, 1), (1, 0)])
    lists = [first, third, second]
    scratch_rows = ROUNDS * fields * quarters
    table_shape = (scratch_rows * SUBLANES, LANES)
    state_1, packed, table, facts = pl.pallas_call(
        functools.partial(prepare_kernel, lev_dev, fields, groups),
        out_shape=[
            struct(state.shape),
            struct((tiles, LANES), jnp.int32),
            struct((fields * blocks * coarse // LANES * levels, LANES)),
            struct((2 * SUBLANES, LANES)),
        ],
        in_specs=specs(VMEM, *[pl.ANY] * 5),
        out_specs=specs(*[VMEM] * 4),
        scratch_shapes=[
            VMEM(terrain.shape, jnp.int32),
            VMEM(block_weight.shape, jnp.float32),
            SMEM((1, blocks), jnp.int32),
            SMEM((1, blocks), jnp.int32),
            pltpu.SemaphoreType.DMA((5,)),
        ],
        cost_estimate=pl.CostEstimate(flops=0, bytes_accessed=8_000_000, transcendentals=0),
        compiler_params=params(),
        name="prepare",
    )(
        terrain_0,
        in_hbm(block_owner.reshape(1, blocks)),
        in_hbm(block_row.reshape(1, blocks)),
        *sources,
    )
    part = struct((lev_dev * scratch_rows, LANES))
    parts = pl.pallas_call(
        functools.partial(produce_kernel, lev_dev, fields, partners, groups),
        out_shape=[part] * partners,
        in_specs=specs(*[VMEM] * 6),
        out_specs=specs(*[VMEM] * partners),
        scratch_shapes=[VMEM(table_shape, jnp.float32)],
        compiler_params=params(),
        name="produce",
    )(*lists, state_0, packed, table)
    arrived = [parts[0]] + [
        lax.ppermute(parts[distance], "lev", [(rank, rank ^ distance) for rank in range(partners)])
        for distance in range(partners - 1, 0, -1)
    ]
    section_rows = HELD_ROWS * quarters
    sections = pl.pallas_call(
        functools.partial(sum_kernel, lev_dev, fields, coarse, partners),
        out_shape=[struct((section_rows, LANES))] * 3,
        in_specs=specs(*[VMEM] * (partners + 1)),
        out_specs=specs(*[VMEM] * 3),
        compiler_params=params(),
        name="sections",
    )(*arrived, facts)
    sections = [
        lax.ppermute(sections[number], ("grid", "side"), towards(lambda side: number, 1))
        for number in SECTION_ORDER
    ]
    sections = [sections[SECTION_ORDER.index(number)] for number in range(ROUNDS)]
    kinds = lev_dev * fields + 1
    spread = struct((ROUNDS * quarters * SUBLANES, kinds * LANES), jnp.bfloat16)
    kept = [spread, spread, struct((panel_tiles * lev_dev * fields * quarters, LANES))]
    sizes = (lev_dev, fields, coarse, groups)
    held = []
    for number in SECTION_ORDER[:-1]:
        held = pl.pallas_call(
            functools.partial(place_kernel, *sizes, number, not held),
            out_shape=kept,
            in_specs=specs(*[VMEM] * (2 + len(held))),
            out_specs=specs(*[VMEM] * 3),
            input_output_aliases={2 + index: index for index in range(len(held))},
            compiler_params=params(),
            name="place",
        )(sections[number], slots, *held)
    result = pl.pallas_call(
        functools.partial(finish_kernel, *sizes, SECTION_ORDER[-1]),
        out_shape=pltpu.HBM(state.shape, jnp.float32),
        in_specs=specs(*[VMEM] * 9),
        out_specs=pl.BlockSpec(memory_space=pltpu.HBM),
        scratch_shapes=[VMEM(one.shape, one.dtype) for one in kept]
        + [VMEM(state.shape, jnp.float32), pltpu.SemaphoreType.DMA((fields,))],
        compiler_params=params(),
        name="finish",
    )(*sections, slots, *held, state_0, state_1)
    return (
        result.reshape(fields, tiles, lev_dev, LANES)
        .transpose(2, 0, 1, 3)
        .reshape(1, lev_dev, fields, cell_dev)
    )


def solution(mesh):
    in_specs = (
        P("side", "lev", None, "grid"),
        P("side", None, "grid"),
        P("grid", None),
        P("grid"),
        P("grid", None, None),
        P("grid", None),
        P("grid"),
    )
    out_specs = P("side", "lev", None, "grid")
    return jax.shard_map(
        on_device, mesh=mesh, in_specs=in_specs, out_specs=out_specs, check_vma=False
    )
```
